32 devices in a mesh: blk: 2 (over core), cells: 16 (over z, y, x).
Axes of the slice: x: 2, y: 2, z: 4, core: 2. Of those that a mesh axis runs over, the one named last changes fastest.
Arguments:
- tokens: bfloat16 [1024, 32, 1120], P('blk', 'cells'), may hold values from -6 to 6
- lengths: int32 [32], P('cells'), may hold values from 512 to 1024, as said below
- attn_gain: float32 [1120], replicated, may hold values from 0.5 to 1.5
- attn_bias: float32 [1120], replicated, may hold values from -1.75 to 1.75
- w_qkv: bfloat16 [1120, 3360], replicated, may hold values from -0.1875 to 0.1875
- w_out: bfloat16 [1120, 1120], replicated, may hold values from -2 to 2
- mlp_gain: float32 [1120], replicated, may hold values from 0.5 to 1.5
- mlp_bias: float32 [1120], replicated, may hold values from -1.75 to 1.75
- w_up: bfloat16 [1120, 4480], replicated, may hold values from -0.1875 to 0.1875
- w_down: bfloat16 [4480, 1120], replicated, may hold values from -0.09375 to 0.09375
- cotangent: bfloat16 [1024, 32, 1120], P('blk', 'cells'), may hold values from -6 to 6
Outputs:
- mixed: bfloat16 [1024, 32, 1120], P('blk', 'cells')
- tokens_grad: bfloat16 [1024, 32, 1120], P('blk', 'cells')
- attn_gain_grad: float32 [1120], replicated
- attn_bias_grad: float32 [1120], replicated
- w_qkv_grad: float32 [1120, 3360], P('cells', 'blk')
- w_out_grad: float32 [1120, 1120], P('cells', 'blk')
- mlp_gain_grad: float32 [1120], replicated
- mlp_bias_grad: float32 [1120], replicated
- w_up_grad: float32 [1120, 4480], P('cells', 'blk')
- w_down_grad: float32 [4480, 1120], P('cells', 'blk')
The draws below stay inside these ranges and needn't reach their ends.
Inputs may be any that keep to these rules, and one draw needn't show every extreme that they name: `lengths`: in every aligned group of 2 cells one cell, drawn at random, has length 1024.
All inputs are finite; a program needn't handle non-finite values.
Results may differ from the reference program's by a relative error of at most 0.017.
Values may be sent and summed in bfloat16 or wider, within the bound.
No kernel may reach another device: no remote copies, remote signals or barrier semaphores. Data moves between devices by JAX's collectives and lax.ppermute only.
A program may use at most 384 MiB of HBM per device.

```python
import jax
import jax.numpy as jnp
from jax import lax

D = 1120
HEADS = 20
HD = 56
FF = 4480
CELLS_DEV = 2
SEQ = 1024
CELLS = 32


def draw_lengths(key, part):
    key = jax.random.fold_in(key, 11)
    key_len, key_pick = jax.random.split(key)
    groups = CELLS // CELLS_DEV
    drawn_len = jax.random.randint(key_len, (CELLS,), SEQ // 2, SEQ + 1)
    chosen_slot = jnp.repeat(jax.random.randint(key_pick, (groups,), 0, CELLS_DEV), CELLS_DEV)
    places = jnp.arange(CELLS, dtype=jnp.int32) % CELLS_DEV
    return jnp.where(places == chosen_slot, SEQ, drawn_len).astype(jnp.int32)


def level_of(stream_key, dims, cuts, least, largest):
    gain = 1.0
    for dim, parts in cuts:
        steps = jax.random.uniform(jax.random.fold_in(jax.random.fold_in(stream_key, 6), dim), (parts,), jnp.float32, least / len(cuts), largest / len(cuts))
        gain = gain * jnp.repeat(jnp.exp(steps), dims[dim] // parts).reshape((-1,) + (1,) * (len(dims) - 1 - dim))
    return gain


def gaussian(own_key, dims, spread, most, cuts=(), kind=jnp.bfloat16):
    values = jax.random.normal(own_key, dims, jnp.float32) * spread
    if len(cuts) > 0:
        values = level_of(own_key, dims, cuts, -0.22, 0.18) * values
    return jnp.clip(values, min=-most, max=most).astype(kind)


def setup_inputs(seed: int = 0) -> dict:
    arg_keys = jax.random.split(jax.random.key(seed), 12)
    return {
        "tokens": gaussian(arg_keys[0], (SEQ, CELLS, D), 1.0, 6.0, ((0, 2), (1, 16))),
        "lengths": draw_lengths(jax.random.fold_in(arg_keys[11], 71), 0),
        "attn_gain": jnp.clip(1.0 + 0.1 * jax.random.normal(arg_keys[2], (D,), jnp.float32), 0.5, 1.5),
        "attn_bias": gaussian(arg_keys[3], (D,), 0.3, 1.75, (), jnp.float32),
        "w_qkv": gaussian(arg_keys[4], (D, 3 * D), D ** -0.5, 0.1875),
        "w_out": gaussian(arg_keys[5], (D, D), (max(9 * D // SEQ, 1)) ** -0.5, 2.0),
        "mlp_gain": jnp.clip(1.0 + 0.1 * jax.random.normal(arg_keys[6], (D,), jnp.float32), 0.5, 1.5),
        "mlp_bias": gaussian(arg_keys[7], (D,), 0.3, 1.75, (), jnp.float32),
        "w_up": gaussian(arg_keys[8], (D, FF), D ** -0.5, 0.1875),
        "w_down": gaussian(arg_keys[9], (FF, D), FF ** -0.5, 0.09375),
        "cotangent": gaussian(arg_keys[10], (SEQ, CELLS, D), 1.0, 6.0, ((0, 2), (1, 16))),
    }


EPSILON = 1e-05
MASKED = -1e+30

@jax.custom_vjp
def low(v):
    return lax.optimization_barrier(v.astype(jnp.bfloat16)).astype(jnp.float32)

@jax.custom_vjp
def low_back(v):
    return v

def low_keep(v):
    return (low(v), None)

def low_pass(kept, grad):
    return (grad,)

def back_keep(v):
    return (v, None)

def back_low(kept, grad):
    return (low(grad),)
low.defvjp(low_keep, low_pass)
low_back.defvjp(back_keep, back_low)

def layer_norm(values_in, gain_vec, bias_vec):
    centred = values_in - lax.optimization_barrier(jnp.mean(values_in, axis=-1, keepdims=True))
    inverse = lax.rsqrt(lax.optimization_barrier(jnp.mean(centred * centred, axis=-1, keepdims=True)) + EPSILON)
    return centred * inverse * gain_vec + bias_vec

def block(group_in, cell_lengths, params):
    attn_gain, attn_bias, w_qkv, w_out, mlp_gain, mlp_bias, w_up, w_down = params
    highest = lax.Precision.HIGHEST
    seq_len = group_in.shape[0]
    cell_count = group_in.shape[1]
    normed_one = low(layer_norm(group_in, attn_gain, attn_bias))
    qkv_vals = low_back(low(jnp.einsum('scd,de->sce', normed_one, w_qkv, precision=highest)))
    query_heads = qkv_vals[..., :D].reshape(seq_len, cell_count, HEADS, HD)
    key_heads = qkv_vals[..., D:2 * D].reshape(seq_len, cell_count, HEADS, HD)
    value_heads = qkv_vals[..., 2 * D:].reshape(seq_len, cell_count, HEADS, HD)
    scores = low_back(jnp.einsum('qchd,kchd->chqk', query_heads, key_heads, precision=highest) * HD ** (-0.5))
    positions = jnp.arange(seq_len, dtype=jnp.int32)
    allowed = (positions[None, :] <= positions[:, None])[None, None] & (positions[None, None, None, :] < cell_lengths[:, None, None, None])
    scores = jnp.where(allowed, scores, MASKED)
    run_max = lax.optimization_barrier(jnp.max(scores, axis=-1, keepdims=True))
    log_total = run_max + jnp.log(lax.optimization_barrier(jnp.sum(jnp.exp(scores - run_max), axis=-1, keepdims=True)))
    prob_vals = low(jnp.exp(scores - log_total))
    attended = jnp.einsum('chqk,kchd->qchd', prob_vals, value_heads, precision=highest).reshape(seq_len, cell_count, D)
    attended = low_back(low(attended))
    hidden = group_in + low_back(jnp.einsum('scd,de->sce', attended, w_out, precision=highest))
    normed_two = low(layer_norm(hidden, mlp_gain, mlp_bias))
    upward = low_back(jnp.einsum('scd,df->scf', normed_two, w_up, precision=highest))
    activated = low(jax.nn.gelu(upward, approximate=True))
    return hidden + low_back(jnp.einsum('scf,fd->scd', activated, w_down, precision=highest))

def reference(tokens, lengths, attn_gain, attn_bias, w_qkv, w_out, mlp_gain, mlp_bias, w_up, w_down, cotangent):
    groups = CELLS // CELLS_DEV
    checked = jax.checkpoint(block)

    def forward(inputs, params):
        stacked = jnp.moveaxis(inputs.reshape(SEQ, groups, CELLS_DEV, D), 1, 0)
        grouped = lengths.reshape(groups, CELLS_DEV)
        outputs = lax.map(lambda group_item: checked(group_item[0], group_item[1], params), (stacked, grouped))
        return jnp.moveaxis(outputs, 0, 1).reshape(SEQ, CELLS, D)
    params = tuple((weight_arg.astype(jnp.float32) for weight_arg in (attn_gain, attn_bias, w_qkv, w_out, mlp_gain, mlp_bias, w_up, w_down)))
    result, pullback = jax.vjp(forward, tokens.astype(jnp.float32), params)
    valid_rows = (jnp.arange(SEQ, dtype=jnp.int32)[:, None] < lengths[None, :]).astype(jnp.float32)
    grad_in, grad_params = pullback(cotangent.astype(jnp.float32) * valid_rows[..., None])
    return (result.astype(jnp.bfloat16), grad_in.astype(jnp.bfloat16), grad_params[0], grad_params[1], grad_params[2], grad_params[3], grad_params[4], grad_params[5], grad_params[6], grad_params[7])
```

```python
import functools

import jax
import jax.numpy as jnp
from jax import lax
from jax.experimental import pallas as pl
from jax.experimental.pallas import tpu as pltpu
from jax.sharding import PartitionSpec as P

D = 1120
HEADS = 20
HD = 56


EPSILON = 1e-05
MASKED = -1e30
LOG2E = 1.4426950408889634
LANES = 128
WIDTH = 1152
WINDOW = 256
TILE = 256
BF16 = jnp.bfloat16
F32 = jnp.float32
NN = (((1,), (0,)), ((), ()))
NT = (((1,), (1,)), ((), ()))
TN = (((0,), (0,)), ((), ()))


def norm_forward(values_in, gain_vec, bias_vec):
    centred = values_in - jnp.mean(values_in, axis=-1, keepdims=True)
    inverse = lax.rsqrt(jnp.mean(centred * centred, axis=-1, keepdims=True) + EPSILON)
    normed = centred * inverse
    return (normed, inverse, normed * gain_vec + bias_vec)


def norm_backward(grad_in, normed, inverse, gain_vec):
    scaled = grad_in * gain_vec
    grad_out = inverse * (
        scaled
        - jnp.mean(scaled, axis=-1, keepdims=True)
        - normed * jnp.mean(scaled * normed, axis=-1, keepdims=True)
    )
    return (grad_out, jnp.sum(grad_in * normed, axis=(0, 1)), jnp.sum(grad_in, axis=(0, 1)))


def key_scores(query_heads, key_piece, query_pos, key_start, lengths):
    key_count = key_piece.shape[0]
    key_heads = key_piece.reshape(key_count, key_piece.shape[1], HEADS, HD)
    scores = jnp.einsum(
        "qchd,kchd->chqk", query_heads, key_heads, preferred_element_type=jnp.float32
    ) * HD ** (-0.5)
    key_pos = key_start + jnp.arange(key_count, dtype=jnp.int32)
    allowed = (key_pos[None, None, :] <= query_pos[None, :, None]) & (
        key_pos[None, None, :] < lengths[:, None, None]
    )
    allowed = allowed[:, None, :, :]
    return (jnp.where(allowed, scores, MASKED), allowed)


def key_sweep(step_fn, initial, pieces, row_count, block_turns):

    def one_turn(turn_index, state_in):
        row_start = turn_index * row_count
        taken = tuple(
            (lax.dynamic_slice_in_dim(full_array, row_start, row_count, 0) for full_array in pieces)
        )
        return step_fn(state_in, taken, row_start)

    return lax.fori_loop(0, block_turns, one_turn, initial)


def position_split(
    tokens, lengths, attn_gain, attn_bias, w_qkv, w_out, mlp_gain, mlp_bias, w_up, w_down, cotangent
):
    row_count = tokens.shape[0]
    cell_count = tokens.shape[1]
    block_turns = lax.axis_size("blk")
    score_scale = HD ** (-0.5)
    query_pos = lax.axis_index("blk") * row_count + jnp.arange(row_count, dtype=jnp.int32)
    inputs = tokens.astype(jnp.float32)
    normed_one, inverse_one, pre_one = norm_forward(inputs, attn_gain, attn_bias)
    normed_low = pre_one.astype(jnp.bfloat16)
    qkv_vals = jnp.einsum(
        "rcd,de->rce", normed_low, w_qkv, preferred_element_type=jnp.float32
    ).astype(jnp.bfloat16)
    key_vals = qkv_vals[..., D : 2 * D]
    value_vals = qkv_vals[..., 2 * D :]
    query_heads = qkv_vals[..., :D].reshape(row_count, cell_count, HEADS, HD)
    start_max = jnp.full((cell_count, HEADS, row_count), MASKED, jnp.float32)
    start_sum = jnp.zeros((cell_count, HEADS, row_count), jnp.float32)
    start_out = jnp.zeros((row_count, cell_count, HEADS, HD), jnp.float32)
    scores, allowed = key_scores(
        query_heads,
        (lax.all_gather(key_vals, "blk", axis=0, tiled=True),)[0],
        query_pos,
        jnp.int32(0),
        lengths,
    )
    new_max = jnp.maximum(start_max, jnp.max(scores, axis=-1))
    weights = jnp.where(allowed, jnp.exp(scores - new_max[..., None]), 0.0)
    run_sum = jnp.sum(weights, axis=-1)
    log_total = new_max + jnp.log(run_sum)

    def probabilities(key_piece, key_start):
        scores, allowed = key_scores(query_heads, key_piece, query_pos, key_start, lengths)
        return jnp.where(allowed, jnp.exp(scores - log_total[..., None]), 0.0)

    pieces = (
        lax.all_gather(key_vals, "blk", axis=0, tiled=True),
        lax.all_gather(value_vals, "blk", axis=0, tiled=True),
    )
    prob_vals = probabilities(pieces[0], jnp.int32(0)).astype(jnp.bfloat16)
    value_heads = pieces[1].reshape(pieces[1].shape[0], cell_count, HEADS, HD)
    out_acc = jnp.einsum(
        "chqk,kchd->qchd", prob_vals, value_heads, preferred_element_type=jnp.float32
    )
    attended = out_acc.reshape(row_count, cell_count, D).astype(jnp.bfloat16)
    hidden = inputs + jnp.einsum("rcd,de->rce", attended, w_out, preferred_element_type=jnp.float32)
    normed_two, inverse_two, pre_two = norm_forward(hidden, mlp_gain, mlp_bias)
    normed_mlp = pre_two.astype(jnp.bfloat16)
    upward = jnp.einsum("rcd,df->rcf", normed_mlp, w_up, preferred_element_type=jnp.float32)
    activated_full, gelu_back = jax.vjp(
        lambda value_in: jax.nn.gelu(value_in, approximate=True), upward
    )
    activated = activated_full.astype(jnp.bfloat16)
    mixed = (
        hidden + jnp.einsum("rcf,fd->rcd", activated, w_down, preferred_element_type=jnp.float32)
    ).astype(jnp.bfloat16)
    valid_rows = (query_pos[:, None] < lengths[None, :]).astype(jnp.float32)
    grad_out = cotangent.astype(jnp.float32) * valid_rows[..., None]
    grad_low = grad_out.astype(jnp.bfloat16)
    w_down_grad = jnp.einsum("rcf,rcd->fd", activated, grad_low, preferred_element_type=jnp.float32)
    grad_act = jnp.einsum("rcd,fd->rcf", grad_low, w_down, preferred_element_type=jnp.float32)
    grad_upward = gelu_back(grad_act)[0].astype(jnp.bfloat16)
    w_up_grad = jnp.einsum(
        "rcd,rcf->df", normed_mlp, grad_upward, preferred_element_type=jnp.float32
    )
    grad_normed_two = jnp.einsum(
        "rcf,df->rcd", grad_upward, w_up, preferred_element_type=jnp.float32
    )
    grad_hidden_ln, mlp_gain_grad, mlp_bias_grad = norm_backward(
        grad_normed_two, normed_two, inverse_two, mlp_gain
    )
    grad_hidden = grad_out + grad_hidden_ln
    grad_branch = grad_hidden.astype(jnp.bfloat16)
    w_out_grad = jnp.einsum(
        "rce,rcd->ed", attended, grad_branch, preferred_element_type=jnp.float32
    )
    grad_attended = jnp.einsum(
        "rcd,ed->rce", grad_branch, w_out, preferred_element_type=jnp.float32
    ).astype(jnp.bfloat16)
    grad_heads = grad_attended.reshape(row_count, cell_count, HEADS, HD)
    whole_keys, whole_values = (
        lax.all_gather(key_vals, "blk", axis=0, tiled=True),
        lax.all_gather(value_vals, "blk", axis=0, tiled=True),
    )

    def attention_grads(key_piece, value_piece, key_start):
        prob_full = probabilities(key_piece, key_start)
        value_heads = value_piece.reshape(value_piece.shape[0], cell_count, HEADS, HD)
        dprobs = jnp.einsum(
            "qchd,kchd->chqk", grad_heads, value_heads, preferred_element_type=jnp.float32
        )
        return (prob_full, dprobs)

    def delta_step(state_in, pieces, key_start):
        prob_full, dprobs = attention_grads(pieces[0], pieces[1], key_start)
        return state_in + jnp.sum(prob_full * dprobs, axis=-1)

    row_delta = key_sweep(delta_step, start_sum, (whole_keys, whole_values), row_count, block_turns)

    def query_step(state_in, pieces, key_start):
        prob_full, dprobs = attention_grads(pieces[0], pieces[1], key_start)
        dscore = (prob_full * (dprobs - row_delta[..., None])).astype(jnp.bfloat16)
        key_heads = pieces[0].reshape(pieces[0].shape[0], cell_count, HEADS, HD)
        return state_in + jnp.einsum(
            "chqk,kchd->qchd", dscore, key_heads, preferred_element_type=jnp.float32
        )

    query_acc = key_sweep(query_step, start_out, (whole_keys, whole_values), row_count, block_turns)
    grad_queries = (query_acc * score_scale).reshape(row_count, cell_count, D).astype(jnp.bfloat16)
    key_piece = whole_keys
    value_piece = whole_values
    prob_full, dprobs = attention_grads(key_piece, value_piece, jnp.int32(0))
    dscore = (prob_full * (dprobs - row_delta[..., None])).astype(jnp.bfloat16)
    grad_keys = (
        jnp.einsum("chqk,qchd->kchd", dscore, query_heads, preferred_element_type=jnp.float32)
        * score_scale
    )
    grad_values = jnp.einsum(
        "chqk,qchd->kchd",
        prob_full.astype(jnp.bfloat16),
        grad_heads,
        preferred_element_type=jnp.float32,
    )
    kv_summed = lax.psum_scatter(
        jnp.concatenate(
            [
                grad_keys.reshape(row_count * lax.axis_size("blk"), cell_count, D),
                grad_values.reshape(row_count * lax.axis_size("blk"), cell_count, D),
            ],
            axis=-1,
        ),
        "blk",
        scatter_dimension=0,
        tiled=True,
    )
    grad_qkv = jnp.concatenate([grad_queries, kv_summed.astype(jnp.bfloat16)], axis=-1)
    w_qkv_grad = jnp.einsum("rcd,rce->de", normed_low, grad_qkv, preferred_element_type=jnp.float32)
    grad_normed_one = jnp.einsum("rce,de->rcd", grad_qkv, w_qkv, preferred_element_type=jnp.float32)
    grad_inputs_ln, attn_gain_grad, attn_bias_grad = norm_backward(
        grad_normed_one, normed_one, inverse_one, attn_gain
    )
    tokens_grad = (grad_hidden + grad_inputs_ln).astype(jnp.bfloat16)
    norm_sums = lax.psum(
        (attn_gain_grad, attn_bias_grad, mlp_gain_grad, mlp_bias_grad), ("blk", "cells")
    )
    shares = (
        lax.psum_scatter(
            w_qkv_grad.astype(jnp.bfloat16), "cells", scatter_dimension=0, tiled=True
        ).astype(jnp.float32),
        lax.psum_scatter(
            w_out_grad.astype(jnp.bfloat16), "cells", scatter_dimension=0, tiled=True
        ).astype(jnp.float32),
        lax.psum_scatter(
            w_up_grad.astype(jnp.bfloat16), "cells", scatter_dimension=0, tiled=True
        ).astype(jnp.float32),
        lax.psum_scatter(
            w_down_grad.astype(jnp.bfloat16), "cells", scatter_dimension=0, tiled=True
        ).astype(jnp.float32),
    )
    summed = (
        lax.psum_scatter(
            shares[0].astype(jnp.bfloat16), "blk", scatter_dimension=1, tiled=True
        ).astype(jnp.float32),
        lax.psum_scatter(
            shares[1].astype(jnp.bfloat16), "blk", scatter_dimension=1, tiled=True
        ).astype(jnp.float32),
        lax.psum_scatter(
            shares[2].astype(jnp.bfloat16), "blk", scatter_dimension=1, tiled=True
        ).astype(jnp.float32),
        lax.psum_scatter(
            shares[3].astype(jnp.bfloat16), "blk", scatter_dimension=1, tiled=True
        ).astype(jnp.float32),
    )
    return (
        mixed,
        tokens_grad,
        norm_sums[0],
        norm_sums[1],
        summed[0],
        summed[1],
        norm_sums[2],
        norm_sums[3],
        summed[2],
        summed[3],
    )


def dot(left, right, dims=NN):
    return lax.dot_general(left, right, dims, preferred_element_type=F32)


def head_lanes(head, width):
    start = jnp.minimum(head * HD // LANES, (width - WINDOW) // LANES) * LANES
    start = pl.multiple_of(start, LANES)
    lane = lax.broadcasted_iota(jnp.int32, (1, WINDOW), 1)
    offset = lane + (start - head * HD)
    own = (offset >= 0) & (offset < HD)
    spare = lane == jnp.where(start == head * HD, WINDOW - 1, 0)
    return start, own, spare


def key_bias(len_ref, seq):
    rows = lax.broadcasted_iota(jnp.int32, (seq, 1), 0)
    return jnp.where(rows < len_ref[0], 0.0, MASKED).astype(BF16)


def masked_query(q_ref, win, own, spare):
    return jnp.where(own, q_ref[:, win], jnp.where(spare, 1.0, 0.0).astype(BF16))


def causal_tile():
    key_row = lax.broadcasted_iota(jnp.int32, (TILE, TILE), 0)
    query_lane = lax.broadcasted_iota(jnp.int32, (TILE, TILE), 1)
    return key_row <= query_lane


def staggered(jobs, begin, middle, end):
    started = begin(jobs[0])
    waiting = None
    for index, job in enumerate(jobs):
        current = started
        if index + 1 < len(jobs):
            started = begin(jobs[index + 1])
        result = middle(job, *current)
        if waiting is not None:
            end(*waiting)
        waiting = (job, *result)
    end(*waiting)


def attention_forward_kernel(per, len_ref, q_ref, k_ref, v_ref, o_ref, lse_ref):
    step = pl.program_id(0)
    seq, width = q_ref.shape

    @pl.when(step == 0)
    def _():
        o_ref[...] = jnp.zeros_like(o_ref)

    bias = key_bias(len_ref, seq)
    keep = causal_tile()
    scale = LOG2E * HD ** (-0.5)
    jobs = []
    for slot in range(per):
        start, own, spare = head_lanes(step * per + slot, width)
        win = pl.ds(start, WINDOW)
        k_win = jnp.where(spare, bias, k_ref[:, win])
        q_win = masked_query(q_ref, win, own, spare)
        v_turned = jnp.transpose(v_ref[:, win])
        for turn in range(seq // TILE):
            jobs.append((slot, turn * TILE, win, own, k_win, q_win, v_turned))

    def begin(job):
        _, low, _, _, k_win, q_win, _ = job
        return (dot(k_win[: low + TILE], q_win[low : low + TILE], NT),)

    def middle(job, scores):
        slot, low = job[:2]
        edge = jnp.where(keep, scores[low:], MASKED)
        scores = edge if low == 0 else jnp.concatenate([scores[:low], edge], axis=0)
        peak = jnp.max(scores, axis=0, keepdims=True) * scale
        weights = jnp.exp2(scores * scale - peak)
        total = jnp.sum(weights, axis=0, keepdims=True)
        lse_ref[slot, :, low : low + TILE] = jnp.broadcast_to(peak + jnp.log2(total), (8, TILE))
        return weights.astype(BF16), total

    def end(job, weights, total):
        _, low, win, own, _, _, v_turned = job
        out = dot(v_turned[:, : low + TILE], weights) * (1.0 / total)
        rows = slice(low, low + TILE)
        o_ref[rows, win] = jnp.where(own, jnp.transpose(out).astype(BF16), o_ref[rows, win])

    staggered(jobs, begin, middle, end)


def attention_backward_kernel(
    per, len_ref, q_ref, k_ref, v_ref, o_ref, do_ref, lse_ref, grad_ref, delta_ref, acc_ref
):
    step = pl.program_id(0)
    seq, width = q_ref.shape

    @pl.when(step == 0)
    def _():
        grad_ref[...] = jnp.zeros_like(grad_ref)
        lane = lax.broadcasted_iota(jnp.int32, (delta_ref.shape[0], width), 1)
        first = lax.broadcasted_iota(jnp.int32, (delta_ref.shape[0], width), 0) * HD
        pick = jnp.where((lane >= first) & (lane < first + HD), 1.0, 0.0).astype(BF16)
        for turn in range(seq // TILE):
            rows = slice(turn * TILE, (turn + 1) * TILE)
            product = o_ref[rows].astype(F32) * do_ref[rows].astype(F32)
            upper = product.astype(BF16)
            lower = (product - upper.astype(F32)).astype(BF16)
            delta_ref[:, rows] = dot(pick, upper, NT) + dot(pick, lower, NT)

    bias = key_bias(len_ref, seq)
    keep = causal_tile()
    scale = LOG2E * HD ** (-0.5)
    turns = seq // TILE
    jobs = []
    for slot in range(per):
        head = step * per + slot
        start, own, spare = head_lanes(head, width)
        win = pl.ds(start, WINDOW)
        k_win = jnp.where(spare, bias, k_ref[:, win])
        q_win = masked_query(q_ref, win, own, spare)
        do_win = jnp.where(own, do_ref[:, win], jnp.zeros((), BF16))
        v_win = v_ref[:, win]
        lse = lse_ref[slot, 0:1, :]
        delta = delta_ref[pl.ds(head, 1), :]
        for turn in range(turns):
            jobs.append((slot, turn, start, own, k_win, q_win, do_win, v_win, lse, delta))

    def begin(job):
        _, turn, _, _, k_win, q_win, do_win, v_win, _, _ = job
        low = turn * TILE
        rows = slice(low, low + TILE)
        return dot(k_win[rows], q_win[low:], NT), dot(v_win[rows], do_win[low:], NT)

    def middle(job, scores, dprobs):
        turn, lse, delta = job[1], job[8], job[9]
        low = turn * TILE
        probs = jnp.exp2(scores * scale - lse[:, low:])
        edge = jnp.where(keep, probs[:, :TILE], 0.0)
        if turn + 1 < turns:
            edge = jnp.concatenate([edge, probs[:, TILE:]], axis=1)
        dscores = (edge * (dprobs - delta[:, low:])).astype(BF16)
        return edge.astype(BF16), dscores

    def end(job, probs, dscores):
        slot, turn, start, own, k_win, q_win, do_win = job[:7]
        low = turn * TILE
        rows = slice(low, low + TILE)

        def put(place, where, value):
            lanes = pl.ds(start + place * width, WINDOW)
            grad_ref[where, lanes] = jnp.where(own, value.astype(BF16), grad_ref[where, lanes])

        put(2, rows, dot(probs, do_win[low:]))
        put(1, rows, dot(dscores, q_win[low:]) * HD ** (-0.5))
        part = dot(dscores, k_win[rows], TN)
        if turn == 0:
            acc_ref[slot] = part
        else:
            acc_ref[slot, low:, :] += part
        if turn + 1 == turns:
            put(0, slice(0, seq), acc_ref[slot] * HD ** (-0.5))

    staggered(jobs, begin, middle, end)


def resident(shape, place=0):
    return pl.BlockSpec(shape, lambda step, *_: (0, place), pipeline_mode=pl.Buffered(1))


def attention_forward(qkv, length, per=2):
    seq, width = qkv.shape[0], qkv.shape[1] // 3
    return pl.pallas_call(
        functools.partial(attention_forward_kernel, per),
        grid_spec=pltpu.PrefetchScalarGridSpec(
            num_scalar_prefetch=1,
            grid=(HEADS // per,),
            in_specs=[resident((seq, width), place) for place in range(3)],
            out_specs=[
                resident((seq, width)),
                pl.BlockSpec((per, 8, seq), lambda step, *_: (step, 0, 0)),
            ],
        ),
        out_shape=[
            jax.ShapeDtypeStruct((seq, width), BF16),
            jax.ShapeDtypeStruct((HEADS, 8, seq), F32),
        ],
        compiler_params=pltpu.CompilerParams(vmem_limit_bytes=56 << 20),
        cost_estimate=pl.CostEstimate(
            flops=2 * 2 * HEADS * seq * seq * WINDOW * 5 // 8,
            bytes_accessed=8 * seq * width,
            transcendentals=HEADS * seq * seq * 5 // 8,
        ),
        name="attention_forward",
    )(length, qkv, qkv, qkv)


def attention_backward(qkv, attended, grad_attended, lse, length, per=2):
    seq, width = qkv.shape[0], qkv.shape[1] // 3
    return pl.pallas_call(
        functools.partial(attention_backward_kernel, per),
        grid_spec=pltpu.PrefetchScalarGridSpec(
            num_scalar_prefetch=1,
            grid=(HEADS // per,),
            in_specs=[resident((seq, width), place) for place in (0, 1, 2, 0, 0)]
            + [pl.BlockSpec((per, 8, seq), lambda step, *_: (step, 0, 0))],
            out_specs=resident((seq, 3 * width)),
            scratch_shapes=[
                pltpu.VMEM((-(-HEADS // 16) * 16, seq), F32),
                pltpu.VMEM((per, seq, WINDOW), F32),
            ],
        ),
        out_shape=jax.ShapeDtypeStruct((seq, 3 * width), BF16),
        compiler_params=pltpu.CompilerParams(vmem_limit_bytes=58 << 20),
        cost_estimate=pl.CostEstimate(
            flops=5 * 2 * HEADS * seq * seq * WINDOW * 5 // 8,
            bytes_accessed=16 * seq * width,
            transcendentals=HEADS * seq * seq * 5 // 8,
        ),
        name="attention_backward",
    )(length, qkv, qkv, qkv, attended, grad_attended, lse)


def swap_cores(value):
    return lax.ppermute(value, "blk", [(0, 1), (1, 0)])


def swap_chips(value, bit):
    count = lax.axis_size("cells")
    return lax.ppermute(value, "cells", [(place, place ^ bit) for place in range(count)])


def scatter_part(grads, axes):
    place = lax.axis_index("cells")
    count = grads.ndim - 2
    kept = grads
    got = None
    for axis in axes:
        bit = 1 << (count - 1 - axis)
        side = (place // bit) % 2

        def half(value, which):
            return lax.dynamic_index_in_dim(value, which, axis, keepdims=True)

        def both(which):
            if got is None:
                return half(kept, which)
            return (half(kept, which).astype(F32) + half(got, which).astype(F32)).astype(BF16)

        sent, stays = both(1 - side), both(side)
        got = swap_chips(sent, bit)
        kept = stays
    total = kept.astype(F32) + got.astype(F32)
    return total.reshape(total.shape[-2:])


def chip_sum(features, theirs, ours):
    sent = dot(features, theirs).astype(BF16)
    return (dot(features, ours) + swap_cores(sent).astype(F32)).astype(BF16)


def scatter(grads, rows, cuts):
    count = lax.axis_size("cells")
    bits = count.bit_length() - 1
    shaped = grads.reshape((2,) * bits + (rows, grads.shape[1]))
    first = [bits - 1 - turn for turn in range(bits)]
    orders = [first, [first[1], first[0]] + first[2:], first[2:] + first[:2]]
    begin = 0
    parts = []
    for size, order in zip(cuts, orders):
        piece = lax.slice_in_dim(shaped, begin, begin + size, axis=bits + 1)
        parts.append(scatter_part(piece, order))
        begin += size
    return jnp.concatenate(parts, axis=-1) if len(parts) > 1 else parts[0]


def columns(value, first, size):
    return lax.dynamic_slice_in_dim(value, first, size, axis=1)


def cell_split(
    tokens, lengths, attn_gain, attn_bias, w_qkv, w_out, mlp_gain, mlp_bias, w_up, w_down, cotangent
):
    row_count = tokens.shape[0]
    seq = 2 * row_count
    core = lax.axis_index("blk")
    chips = lax.axis_size("cells")

    def to_cell(value):
        mine = jnp.where(core == 0, value[:, 0], value[:, 1])
        other = swap_cores(jnp.where(core == 0, value[:, 1], value[:, 0]))
        return jnp.concatenate(
            [jnp.where(core == 0, mine, other), jnp.where(core == 0, other, mine)], axis=0
        )

    def to_rows(value):
        first, second = value[:row_count], value[row_count:]
        mine = jnp.where(core == 0, first, second)
        other = swap_cores(jnp.where(core == 0, second, first))
        return jnp.stack(
            [jnp.where(core == 0, mine, other), jnp.where(core == 0, other, mine)], axis=1
        )

    length = jnp.where(core == 0, lengths[0], lengths[1])
    inputs = to_cell(tokens).astype(F32)
    cell_cotangent = to_cell(cotangent)
    w_wide = jnp.pad(w_qkv.reshape(D, 3, D), ((0, 0), (0, 0), (0, WIDTH - D))).reshape(D, 3 * WIDTH)
    w_out_tall = jnp.pad(w_out, ((0, WIDTH - D), (0, 0)))

    def norm_grads(grad_in, normed, inverse, gain_vec):
        scaled = grad_in * gain_vec
        grad_out = inverse * (
            scaled
            - jnp.mean(scaled, axis=-1, keepdims=True)
            - normed * jnp.mean(scaled * normed, axis=-1, keepdims=True)
        )
        return grad_out, jnp.sum(grad_in * normed, axis=0), jnp.sum(grad_in, axis=0)

    normed_one, inverse_one, pre_one = norm_forward(inputs, attn_gain, attn_bias)
    normed_low = pre_one.astype(BF16)
    qkv = dot(normed_low, w_wide).astype(BF16)
    attended, lse = attention_forward(qkv, length.reshape(1))
    hidden = inputs + dot(attended, w_out_tall)
    normed_two, inverse_two, pre_two = norm_forward(hidden, mlp_gain, mlp_bias)
    normed_mlp = pre_two.astype(BF16)
    upward = dot(normed_mlp, w_up)
    activated_full, gelu_back = jax.vjp(
        lambda value_in: jax.nn.gelu(value_in, approximate=True), upward
    )
    activated = activated_full.astype(BF16)
    mixed = (hidden + dot(activated, w_down)).astype(BF16)
    valid = jnp.arange(seq, dtype=jnp.int32)[:, None] < length
    grad_low = jnp.where(valid, cell_cotangent, jnp.zeros((), BF16))
    grad_out = grad_low.astype(F32)

    rows_pad = -(-(D // chips) // 8) * 8
    place = jnp.arange(chips * rows_pad, dtype=jnp.int32)
    source = jnp.where(place % rows_pad < D // chips, place // rows_pad * (D // chips) + place % rows_pad, -1)
    spread = (source[:, None] == jnp.arange(D, dtype=jnp.int32)[None, :]).astype(BF16)

    def spread_rows(value):
        return dot(spread, value, NT).astype(BF16)

    half = D // 2
    down_sent = lax.dot_general(activated, columns(grad_low, (1 - core) * half, half), TN, preferred_element_type=F32)
    down_kept = lax.dot_general(activated, columns(grad_low, core * half, half), TN, preferred_element_type=F32)
    down_sum = (down_kept + swap_cores(down_sent.astype(BF16)).astype(F32)).astype(BF16)
    w_down_share = scatter(down_sum, w_down.shape[0] // chips, (256, 256, half - 512))

    grad_act = dot(grad_low, w_down, NT)
    grad_upward = gelu_back(grad_act)[0].astype(BF16)
    up_all = w_up.shape[1]
    up_window = -(-up_all // 2 // LANES) * LANES
    up_starts = (0, up_all - up_window)
    up_start = jnp.where(core == 0, up_starts[0], up_starts[1])
    up_other = jnp.where(core == 0, up_starts[1], up_starts[0])
    up_sum = chip_sum(
        spread_rows(normed_mlp),
        columns(grad_upward, up_other, up_window),
        columns(grad_upward, up_start, up_window),
    )
    up_share = scatter(up_sum, rows_pad, (896, 896, up_window - 1792))

    grad_normed_two = dot(grad_upward, w_up, NT)
    grad_hidden_ln, mlp_gain_grad, mlp_bias_grad = norm_grads(
        grad_normed_two, normed_two, inverse_two, mlp_gain
    )
    grad_hidden = grad_out + grad_hidden_ln
    grad_branch = grad_hidden.astype(BF16)
    out_sum = chip_sum(
        spread_rows(attended[:, :D]),
        columns(grad_branch, (1 - core) * half, half),
        columns(grad_branch, core * half, half),
    )
    w_out_share = scatter(out_sum, rows_pad, (half,))

    grad_attended = dot(grad_branch, w_out_tall, NT).astype(BF16)
    grad_qkv = attention_backward(qkv, attended, grad_attended, lse, length.reshape(1))
    qkv_window = 14 * LANES
    qkv_starts = (0, 3 * WIDTH - qkv_window)
    qkv_start = jnp.where(core == 0, qkv_starts[0], qkv_starts[1])
    qkv_other = jnp.where(core == 0, qkv_starts[1], qkv_starts[0])
    qkv_sum = chip_sum(
        spread_rows(normed_low),
        columns(grad_qkv, qkv_other, qkv_window),
        columns(grad_qkv, qkv_start, qkv_window),
    )
    qkv_share = scatter(qkv_sum, rows_pad, (640, 640, qkv_window - 1280))

    grad_normed_one = dot(grad_qkv, w_wide, NT)
    grad_inputs_ln, attn_gain_grad, attn_bias_grad = norm_grads(
        grad_normed_one, normed_one, inverse_one, attn_gain
    )
    tokens_grad = (grad_hidden + grad_inputs_ln).astype(BF16)
    norm_sums = lax.psum(
        (attn_gain_grad, attn_bias_grad, mlp_gain_grad, mlp_bias_grad), ("blk", "cells")
    )

    rows = D // chips
    first_share = jnp.concatenate(
        [qkv_share[:rows, :D], qkv_share[:rows, WIDTH : WIDTH + half]], axis=1
    )
    shift = WIDTH + half - qkv_starts[1]
    second_share = jnp.concatenate(
        [
            qkv_share[:rows, shift : shift + half],
            qkv_share[:rows, 2 * WIDTH - qkv_starts[1] : 2 * WIDTH - qkv_starts[1] + D],
        ],
        axis=1,
    )
    w_qkv_share = jnp.where(core == 0, first_share, second_share)
    up_shift = up_all // 2 - up_starts[1]
    w_up_share = jnp.where(
        core == 0,
        up_share[:rows, : up_all // 2],
        up_share[:rows, up_shift : up_shift + up_all // 2],
    )
    return (
        to_rows(mixed),
        to_rows(tokens_grad),
        norm_sums[0],
        norm_sums[1],
        w_qkv_share,
        w_out_share[:rows],
        norm_sums[2],
        norm_sums[3],
        w_up_share,
        w_down_share,
    )


def per_device(mesh, tokens, *rest):
    chips = mesh.shape["cells"]
    if mesh.shape["blk"] == 2 and tokens.shape[1] == 2 and chips & (chips - 1) == 0 and chips >= 8:
        return cell_split(tokens, *rest)
    return position_split(tokens, *rest)


def solution(mesh):
    placed = (
        P("blk", "cells", None),
        P("cells"),
        P(),
        P(),
        P(),
        P(),
        P(),
        P(),
        P(),
        P(),
        P("blk", "cells", None),
    )
    return jax.shard_map(
        functools.partial(per_device, mesh),
        mesh=mesh,
        in_specs=placed,
        out_specs=(
            P("blk", "cells", None),
            P("blk", "cells", None),
            P(),
            P(),
            P("cells", "blk"),
            P("cells", "blk"),
            P(),
            P(),
            P("cells", "blk"),
            P("cells", "blk"),
        ),
        check_vma=False,
    )
```

```python
import functools
import math

import jax
import jax.numpy as jnp
from jax import lax
from jax.experimental import pallas as pl
from jax.experimental.pallas import tpu as pltpu
from jax.sharding import PartitionSpec as P

D = 1120
HEADS = 20
HD = 56


EPSILON = 1e-05
MASKED = -1e30
LOG2E = 1.4426950408889634
LANES = 128
WIDTH = 1152
WINDOW = 256
TILE = 256
BF16 = jnp.bfloat16
F32 = jnp.float32
NN = (((1,), (0,)), ((), ()))
NT = (((1,), (1,)), ((), ()))
TN = (((0,), (0,)), ((), ()))


def norm_forward(values_in, gain_vec, bias_vec):
    centred = values_in - jnp.mean(values_in, axis=-1, keepdims=True)
    inverse = lax.rsqrt(jnp.mean(centred * centred, axis=-1, keepdims=True) + EPSILON)
    normed = centred * inverse
    return (normed, inverse, normed * gain_vec + bias_vec)


def norm_backward(grad_in, normed, inverse, gain_vec):
    scaled = grad_in * gain_vec
    grad_out = inverse * (
        scaled
        - jnp.mean(scaled, axis=-1, keepdims=True)
        - normed * jnp.mean(scaled * normed, axis=-1, keepdims=True)
    )
    return (grad_out, jnp.sum(grad_in * normed, axis=(0, 1)), jnp.sum(grad_in, axis=(0, 1)))


def key_scores(query_heads, key_piece, query_pos, key_start, lengths):
    key_count = key_piece.shape[0]
    key_heads = key_piece.reshape(key_count, key_piece.shape[1], HEADS, HD)
    scores = jnp.einsum(
        "qchd,kchd->chqk", query_heads, key_heads, preferred_element_type=jnp.float32
    ) * HD ** (-0.5)
    key_pos = key_start + jnp.arange(key_count, dtype=jnp.int32)
    allowed = (key_pos[None, None, :] <= query_pos[None, :, None]) & (
        key_pos[None, None, :] < lengths[:, None, None]
    )
    allowed = allowed[:, None, :, :]
    return (jnp.where(allowed, scores, MASKED), allowed)


def key_sweep(step_fn, initial, pieces, row_count, block_turns):

    def one_turn(turn_index, state_in):
        row_start = turn_index * row_count
        taken = tuple(
            (lax.dynamic_slice_in_dim(full_array, row_start, row_count, 0) for full_array in pieces)
        )
        return step_fn(state_in, taken, row_start)

    return lax.fori_loop(0, block_turns, one_turn, initial)


def position_split(
    tokens, lengths, attn_gain, attn_bias, w_qkv, w_out, mlp_gain, mlp_bias, w_up, w_down, cotangent
):
    row_count = tokens.shape[0]
    cell_count = tokens.shape[1]
    block_turns = lax.axis_size("blk")
    score_scale = HD ** (-0.5)
    query_pos = lax.axis_index("blk") * row_count + jnp.arange(row_count, dtype=jnp.int32)
    inputs = tokens.astype(jnp.float32)
    normed_one, inverse_one, pre_one = norm_forward(inputs, attn_gain, attn_bias)
    normed_low = pre_one.astype(jnp.bfloat16)
    qkv_vals = jnp.einsum(
        "rcd,de->rce", normed_low, w_qkv, preferred_element_type=jnp.float32
    ).astype(jnp.bfloat16)
    key_vals = qkv_vals[..., D : 2 * D]
    value_vals = qkv_vals[..., 2 * D :]
    query_heads = qkv_vals[..., :D].reshape(row_count, cell_count, HEADS, HD)
    start_max = jnp.full((cell_count, HEADS, row_count), MASKED, jnp.float32)
    start_sum = jnp.zeros((cell_count, HEADS, row_count), jnp.float32)
    start_out = jnp.zeros((row_count, cell_count, HEADS, HD), jnp.float32)
    scores, allowed = key_scores(
        query_heads,
        (lax.all_gather(key_vals, "blk", axis=0, tiled=True),)[0],
        query_pos,
        jnp.int32(0),
        lengths,
    )
    new_max = jnp.maximum(start_max, jnp.max(scores, axis=-1))
    weights = jnp.where(allowed, jnp.exp(scores - new_max[..., None]), 0.0)
    run_sum = jnp.sum(weights, axis=-1)
    log_total = new_max + jnp.log(run_sum)

    def probabilities(key_piece, key_start):
        scores, allowed = key_scores(query_heads, key_piece, query_pos, key_start, lengths)
        return jnp.where(allowed, jnp.exp(scores - log_total[..., None]), 0.0)

    pieces = (
        lax.all_gather(key_vals, "blk", axis=0, tiled=True),
        lax.all_gather(value_vals, "blk", axis=0, tiled=True),
    )
    prob_vals = probabilities(pieces[0], jnp.int32(0)).astype(jnp.bfloat16)
    value_heads = pieces[1].reshape(pieces[1].shape[0], cell_count, HEADS, HD)
    out_acc = jnp.einsum(
        "chqk,kchd->qchd", prob_vals, value_heads, preferred_element_type=jnp.float32
    )
    attended = out_acc.reshape(row_count, cell_count, D).astype(jnp.bfloat16)
    hidden = inputs + jnp.einsum("rcd,de->rce", attended, w_out, preferred_element_type=jnp.float32)
    normed_two, inverse_two, pre_two = norm_forward(hidden, mlp_gain, mlp_bias)
    normed_mlp = pre_two.astype(jnp.bfloat16)
    upward = jnp.einsum("rcd,df->rcf", normed_mlp, w_up, preferred_element_type=jnp.float32)
    activated_full, gelu_back = jax.vjp(
        lambda value_in: jax.nn.gelu(value_in, approximate=True), upward
    )
    activated = activated_full.astype(jnp.bfloat16)
    mixed = (
        hidden + jnp.einsum("rcf,fd->rcd", activated, w_down, preferred_element_type=jnp.float32)
    ).astype(jnp.bfloat16)
    valid_rows = (query_pos[:, None] < lengths[None, :]).astype(jnp.float32)
    grad_out = cotangent.astype(jnp.float32) * valid_rows[..., None]
    grad_low = grad_out.astype(jnp.bfloat16)
    w_down_grad = jnp.einsum("rcf,rcd->fd", activated, grad_low, preferred_element_type=jnp.float32)
    grad_act = jnp.einsum("rcd,fd->rcf", grad_low, w_down, preferred_element_type=jnp.float32)
    grad_upward = gelu_back(grad_act)[0].astype(jnp.bfloat16)
    w_up_grad = jnp.einsum(
        "rcd,rcf->df", normed_mlp, grad_upward, preferred_element_type=jnp.float32
    )
    grad_normed_two = jnp.einsum(
        "rcf,df->rcd", grad_upward, w_up, preferred_element_type=jnp.float32
    )
    grad_hidden_ln, mlp_gain_grad, mlp_bias_grad = norm_backward(
        grad_normed_two, normed_two, inverse_two, mlp_gain
    )
    grad_hidden = grad_out + grad_hidden_ln
    grad_branch = grad_hidden.astype(jnp.bfloat16)
    w_out_grad = jnp.einsum(
        "rce,rcd->ed", attended, grad_branch, preferred_element_type=jnp.float32
    )
    grad_attended = jnp.einsum(
        "rcd,ed->rce", grad_branch, w_out, preferred_element_type=jnp.float32
    ).astype(jnp.bfloat16)
    grad_heads = grad_attended.reshape(row_count, cell_count, HEADS, HD)
    whole_keys, whole_values = (
        lax.all_gather(key_vals, "blk", axis=0, tiled=True),
        lax.all_gather(value_vals, "blk", axis=0, tiled=True),
    )

    def attention_grads(key_piece, value_piece, key_start):
        prob_full = probabilities(key_piece, key_start)
        value_heads = value_piece.reshape(value_piece.shape[0], cell_count, HEADS, HD)
        dprobs = jnp.einsum(
            "qchd,kchd->chqk", grad_heads, value_heads, preferred_element_type=jnp.float32
        )
        return (prob_full, dprobs)

    def delta_step(state_in, pieces, key_start):
        prob_full, dprobs = attention_grads(pieces[0], pieces[1], key_start)
        return state_in + jnp.sum(prob_full * dprobs, axis=-1)

    row_delta = key_sweep(delta_step, start_sum, (whole_keys, whole_values), row_count, block_turns)

    def query_step(state_in, pieces, key_start):
        prob_full, dprobs = attention_grads(pieces[0], pieces[1], key_start)
        dscore = (prob_full * (dprobs - row_delta[..., None])).astype(jnp.bfloat16)
        key_heads = pieces[0].reshape(pieces[0].shape[0], cell_count, HEADS, HD)
        return state_in + jnp.einsum(
            "chqk,kchd->qchd", dscore, key_heads, preferred_element_type=jnp.float32
        )

    query_acc = key_sweep(query_step, start_out, (whole_keys, whole_values), row_count, block_turns)
    grad_queries = (query_acc * score_scale).reshape(row_count, cell_count, D).astype(jnp.bfloat16)
    key_piece = whole_keys
    value_piece = whole_values
    prob_full, dprobs = attention_grads(key_piece, value_piece, jnp.int32(0))
    dscore = (prob_full * (dprobs - row_delta[..., None])).astype(jnp.bfloat16)
    grad_keys = (
        jnp.einsum("chqk,qchd->kchd", dscore, query_heads, preferred_element_type=jnp.float32)
        * score_scale
    )
    grad_values = jnp.einsum(
        "chqk,qchd->kchd",
        prob_full.astype(jnp.bfloat16),
        grad_heads,
        preferred_element_type=jnp.float32,
    )
    kv_summed = lax.psum_scatter(
        jnp.concatenate(
            [
                grad_keys.reshape(row_count * lax.axis_size("blk"), cell_count, D),
                grad_values.reshape(row_count * lax.axis_size("blk"), cell_count, D),
            ],
            axis=-1,
        ),
        "blk",
        scatter_dimension=0,
        tiled=True,
    )
    grad_qkv = jnp.concatenate([grad_queries, kv_summed.astype(jnp.bfloat16)], axis=-1)
    w_qkv_grad = jnp.einsum("rcd,rce->de", normed_low, grad_qkv, preferred_element_type=jnp.float32)
    grad_normed_one = jnp.einsum("rce,de->rcd", grad_qkv, w_qkv, preferred_element_type=jnp.float32)
    grad_inputs_ln, attn_gain_grad, attn_bias_grad = norm_backward(
        grad_normed_one, normed_one, inverse_one, attn_gain
    )
    tokens_grad = (grad_hidden + grad_inputs_ln).astype(jnp.bfloat16)
    norm_sums = lax.psum(
        (attn_gain_grad, attn_bias_grad, mlp_gain_grad, mlp_bias_grad), ("blk", "cells")
    )
    shares = (
        lax.psum_scatter(
            w_qkv_grad.astype(jnp.bfloat16), "cells", scatter_dimension=0, tiled=True
        ).astype(jnp.float32),
        lax.psum_scatter(
            w_out_grad.astype(jnp.bfloat16), "cells", scatter_dimension=0, tiled=True
        ).astype(jnp.float32),
        lax.psum_scatter(
            w_up_grad.astype(jnp.bfloat16), "cells", scatter_dimension=0, tiled=True
        ).astype(jnp.float32),
        lax.psum_scatter(
            w_down_grad.astype(jnp.bfloat16), "cells", scatter_dimension=0, tiled=True
        ).astype(jnp.float32),
    )
    summed = (
        lax.psum_scatter(
            shares[0].astype(jnp.bfloat16), "blk", scatter_dimension=1, tiled=True
        ).astype(jnp.float32),
        lax.psum_scatter(
            shares[1].astype(jnp.bfloat16), "blk", scatter_dimension=1, tiled=True
        ).astype(jnp.float32),
        lax.psum_scatter(
            shares[2].astype(jnp.bfloat16), "blk", scatter_dimension=1, tiled=True
        ).astype(jnp.float32),
        lax.psum_scatter(
            shares[3].astype(jnp.bfloat16), "blk", scatter_dimension=1, tiled=True
        ).astype(jnp.float32),
    )
    return (
        mixed,
        tokens_grad,
        norm_sums[0],
        norm_sums[1],
        summed[0],
        summed[1],
        norm_sums[2],
        norm_sums[3],
        summed[2],
        summed[3],
    )


def dot(left, right, dims=NN):
    return lax.dot_general(left, right, dims, preferred_element_type=F32)


def head_lanes(head, width):
    start = jnp.minimum(head * HD // LANES, (width - WINDOW) // LANES) * LANES
    start = pl.multiple_of(start, LANES)
    lane = lax.broadcasted_iota(jnp.int32, (1, WINDOW), 1)
    offset = lane + (start - head * HD)
    own = (offset >= 0) & (offset < HD)
    spare = lane == jnp.where(start == head * HD, WINDOW - 1, 0)
    return start, own, spare


def key_bias(len_ref, seq):
    rows = lax.broadcasted_iota(jnp.int32, (seq, 1), 0)
    return jnp.where(rows < len_ref[0], 0.0, MASKED).astype(BF16)


def masked_query(q_ref, win, own, spare):
    return jnp.where(own, q_ref[:, win], jnp.where(spare, 1.0, 0.0).astype(BF16))


def causal_tile():
    key_row = lax.broadcasted_iota(jnp.int32, (TILE, TILE), 0)
    query_lane = lax.broadcasted_iota(jnp.int32, (TILE, TILE), 1)
    return key_row <= query_lane


def staggered(jobs, begin, middle, end):
    started = begin(jobs[0])
    waiting = None
    for index, job in enumerate(jobs):
        current = started
        if index + 1 < len(jobs):
            started = begin(jobs[index + 1])
        result = middle(job, *current)
        if waiting is not None:
            end(*waiting)
        waiting = (job, *result)
    end(*waiting)


def attention_forward_kernel(per, len_ref, q_ref, k_ref, v_ref, o_ref, lse_ref):
    step = pl.program_id(0)
    seq, width = q_ref.shape

    @pl.when(step == 0)
    def _():
        o_ref[...] = jnp.zeros_like(o_ref)

    bias = key_bias(len_ref, seq)
    keep = causal_tile()
    scale = LOG2E * HD ** (-0.5)
    jobs = []
    for slot in range(per):
        start, own, spare = head_lanes(step * per + slot, width)
        win = pl.ds(start, WINDOW)
        k_win = jnp.where(spare, bias, k_ref[:, win])
        q_win = masked_query(q_ref, win, own, spare)
        v_turned = jnp.transpose(v_ref[:, win])
        for turn in range(seq // TILE):
            jobs.append((slot, turn * TILE, win, own, k_win, q_win, v_turned))

    def begin(job):
        _, low, _, _, k_win, q_win, _ = job
        return (dot(k_win[: low + TILE], q_win[low : low + TILE], NT),)

    def middle(job, scores):
        slot, low = job[:2]
        edge = jnp.where(keep, scores[low:], MASKED)
        scores = edge if low == 0 else jnp.concatenate([scores[:low], edge], axis=0)
        peak = jnp.max(scores, axis=0, keepdims=True) * scale
        weights = jnp.exp2(scores * scale - peak)
        total = jnp.sum(weights, axis=0, keepdims=True)
        lse_ref[slot, :, low : low + TILE] = jnp.broadcast_to(peak + jnp.log2(total), (8, TILE))
        return weights.astype(BF16), total

    def end(job, weights, total):
        _, low, win, own, _, _, v_turned = job
        out = dot(v_turned[:, : low + TILE], weights) * (1.0 / total)
        rows = slice(low, low + TILE)
        o_ref[rows, win] = jnp.where(own, jnp.transpose(out).astype(BF16), o_ref[rows, win])

    staggered(jobs, begin, middle, end)


def attention_backward_kernel(
    per, len_ref, q_ref, k_ref, v_ref, o_ref, do_ref, lse_ref, grad_ref, delta_ref, acc_ref
):
    step = pl.program_id(0)
    seq, width = q_ref.shape

    @pl.when(step == 0)
    def _():
        grad_ref[...] = jnp.zeros_like(grad_ref)
        lane = lax.broadcasted_iota(jnp.int32, (delta_ref.shape[0], width), 1)
        first = lax.broadcasted_iota(jnp.int32, (delta_ref.shape[0], width), 0) * HD
        pick = jnp.where((lane >= first) & (lane < first + HD), 1.0, 0.0).astype(BF16)
        for turn in range(seq // TILE):
            rows = slice(turn * TILE, (turn + 1) * TILE)
            product = o_ref[rows].astype(F32) * do_ref[rows].astype(F32)
            upper = product.astype(BF16)
            lower = (product - upper.astype(F32)).astype(BF16)
            delta_ref[:, rows] = dot(pick, upper, NT) + dot(pick, lower, NT)

    bias = key_bias(len_ref, seq)
    keep = causal_tile()
    scale = LOG2E * HD ** (-0.5)
    turns = seq // TILE
    jobs = []
    for slot in range(per):
        head = step * per + slot
        start, own, spare = head_lanes(head, width)
        win = pl.ds(start, WINDOW)
        k_win = jnp.where(spare, bias, k_ref[:, win])
        q_win = masked_query(q_ref, win, own, spare)
        do_win = jnp.where(own, do_ref[:, win], jnp.zeros((), BF16))
        v_win = v_ref[:, win]
        lse = lse_ref[slot, 0:1, :]
        delta = delta_ref[pl.ds(head, 1), :]
        for turn in range(turns):
            jobs.append((slot, turn, start, own, k_win, q_win, do_win, v_win, lse, delta))

    def begin(job):
        _, turn, _, _, k_win, q_win, do_win, v_win, _, _ = job
        low = turn * TILE
        rows = slice(low, low + TILE)
        return dot(k_win[rows], q_win[low:], NT), dot(v_win[rows], do_win[low:], NT)

    def middle(job, scores, dprobs):
        turn, lse, delta = job[1], job[8], job[9]
        low = turn * TILE
        probs = jnp.exp2(scores * scale - lse[:, low:])
        edge = jnp.where(keep, probs[:, :TILE], 0.0)
        if turn + 1 < turns:
            edge = jnp.concatenate([edge, probs[:, TILE:]], axis=1)
        dscores = (edge * (dprobs - delta[:, low:])).astype(BF16)
        return edge.astype(BF16), dscores

    def end(job, probs, dscores):
        slot, turn, start, own, k_win, q_win, do_win = job[:7]
        low = turn * TILE
        rows = slice(low, low + TILE)

        def put(place, where, value):
            lanes = pl.ds(start + place * width, WINDOW)
            grad_ref[where, lanes] = jnp.where(own, value.astype(BF16), grad_ref[where, lanes])

        put(2, rows, dot(probs, do_win[low:]))
        put(1, rows, dot(dscores, q_win[low:]) * HD ** (-0.5))
        part = dot(dscores, k_win[rows], TN)
        if turn == 0:
            acc_ref[slot] = part
        else:
            acc_ref[slot, low:, :] += part
        if turn + 1 == turns:
            put(0, slice(0, seq), acc_ref[slot] * HD ** (-0.5))

    staggered(jobs, begin, middle, end)


def resident(shape, place=0):
    return pl.BlockSpec(shape, lambda step, *_: (0, place), pipeline_mode=pl.Buffered(1))


def attention_forward(qkv, length, heads, per=2):
    seq, width = qkv.shape[0], qkv.shape[1] // 3
    return pl.pallas_call(
        functools.partial(attention_forward_kernel, per),
        grid_spec=pltpu.PrefetchScalarGridSpec(
            num_scalar_prefetch=1,
            grid=(heads // per,),
            in_specs=[resident((seq, width), place) for place in range(3)],
            out_specs=[
                resident((seq, width)),
                pl.BlockSpec((per, 8, seq), lambda step, *_: (step, 0, 0)),
            ],
        ),
        out_shape=[
            jax.ShapeDtypeStruct((seq, width), BF16),
            jax.ShapeDtypeStruct((heads, 8, seq), F32),
        ],
        compiler_params=pltpu.CompilerParams(vmem_limit_bytes=56 << 20),
        cost_estimate=pl.CostEstimate(
            flops=2 * 2 * heads * seq * seq * WINDOW * 5 // 8,
            bytes_accessed=8 * seq * width,
            transcendentals=heads * seq * seq * 5 // 8,
        ),
        name="attention_forward",
    )(length, qkv, qkv, qkv)


def attention_backward(qkv, attended, grad_attended, lse, length, per=2):
    seq, width = qkv.shape[0], qkv.shape[1] // 3
    heads = lse.shape[0]
    return pl.pallas_call(
        functools.partial(attention_backward_kernel, per),
        grid_spec=pltpu.PrefetchScalarGridSpec(
            num_scalar_prefetch=1,
            grid=(heads // per,),
            in_specs=[resident((seq, width), place) for place in (0, 1, 2, 0, 0)]
            + [pl.BlockSpec((per, 8, seq), lambda step, *_: (step, 0, 0))],
            out_specs=resident((seq, 3 * width)),
            scratch_shapes=[
                pltpu.VMEM((-(-heads // 16) * 16, seq), F32),
                pltpu.VMEM((per, seq, WINDOW), F32),
            ],
        ),
        out_shape=jax.ShapeDtypeStruct((seq, 3 * width), BF16),
        compiler_params=pltpu.CompilerParams(vmem_limit_bytes=58 << 20),
        cost_estimate=pl.CostEstimate(
            flops=5 * 2 * heads * seq * seq * WINDOW * 5 // 8,
            bytes_accessed=16 * seq * width,
            transcendentals=heads * seq * seq * 5 // 8,
        ),
        name="attention_backward",
    )(length, qkv, qkv, qkv, attended, grad_attended, lse)


def once(shape):
    return pl.BlockSpec(shape, lambda step, *_: (0, 0), pipeline_mode=pl.Buffered(1))


def lane_tiles(rows, tile):
    return pl.BlockSpec((rows, tile), lambda step, *_: (0, step))


def row_tiles(tile, columns):
    return pl.BlockSpec((tile, columns), lambda step, *_: (step, 0))


def spread_store(rows_ref, scratch_ref, value, chips):
    depth = value.shape[0]
    rows = depth // chips
    padded = rows_ref.shape[0] // chips
    scratch_ref[:depth] = value
    for pair in range(chips // 2):
        first = 2 * pair * rows
        both = jnp.concatenate(
            [
                scratch_ref[first : first + padded],
                scratch_ref[first + rows : first + rows + padded],
            ],
            axis=0,
        )
        rows_ref[2 * pair * padded : 2 * (pair + 1) * padded] = both.astype(BF16)


def norm_down(value, gain, bias):
    centred = value - jnp.mean(value, axis=0, keepdims=True)
    inverse = lax.rsqrt(jnp.mean(centred * centred, axis=0, keepdims=True) + EPSILON)
    return centred * inverse * gain + bias


def cell_tile(core_ref, mine_ref, other_ref):
    return jnp.where(pl.program_id(0) // 2 == core_ref[0], mine_ref[0], other_ref[...]).astype(F32)


def project_kernel(
    chips, spans, core_ref, mine_ref, other_ref, norm_ref, w_ref, *rest
):
    out_refs, rows_ref, wide_refs, scratch_ref = (
        rest[: len(spans)],
        rest[len(spans)],
        rest[len(spans) + 1 : -1],
        rest[-1],
    )
    depth = w_ref.shape[0]

    @pl.when(pl.program_id(0) == 0)
    def _():
        scratch_ref[...] = jnp.zeros_like(scratch_ref)
        for wide_ref, (first, size) in zip(wide_refs, spans):
            width = wide_ref.shape[1] // 3
            for part in range(3):
                begin = part * depth + first
                wide_ref[:, part * width : part * width + size] = w_ref[:, begin : begin + size]
                if size < width:
                    wide_ref[:, part * width + size : (part + 1) * width] = jnp.zeros(
                        (depth, width - size), BF16
                    )

    columns = jnp.transpose(norm_ref[...])
    normed = norm_down(cell_tile(core_ref, mine_ref, other_ref), columns[:, 0:1], columns[:, 1:2])
    spread_store(rows_ref, scratch_ref, normed, chips)
    left = jnp.transpose(normed.astype(BF16))
    for out_ref, wide_ref in zip(out_refs, wide_refs):
        out_ref[...] = dot(left, wide_ref[...]).astype(BF16)


def cell_specs(depth, tile):
    return [
        pl.BlockSpec((1, depth, tile), lambda step, core, *_: (core[0], 0, step % 2)),
        pl.BlockSpec((depth, tile), lambda step, core, *_: (0, step % 2)),
    ]


def project(core, turned, other, norms, w, spans, chips, rows_pad):
    _, depth, half = turned.shape
    tile = half // 2
    widths = [3 * (-(-size // LANES) * LANES) for _, size in spans]
    return pl.pallas_call(
        functools.partial(project_kernel, chips, spans),
        grid_spec=pltpu.PrefetchScalarGridSpec(
            num_scalar_prefetch=1,
            grid=(4,),
            in_specs=cell_specs(depth, tile) + [once(norms.shape), once(w.shape)],
            out_specs=[row_tiles(tile, width) for width in widths]
            + [lane_tiles(chips * rows_pad, tile)]
            + [once((depth, width)) for width in widths],
            scratch_shapes=[pltpu.VMEM((depth + 8, tile), F32)],
        ),
        out_shape=[jax.ShapeDtypeStruct((2 * half, width), BF16) for width in widths]
        + [jax.ShapeDtypeStruct((chips * rows_pad, 2 * half), BF16)]
        + [jax.ShapeDtypeStruct((depth, width), BF16) for width in widths],
        compiler_params=pltpu.CompilerParams(vmem_limit_bytes=56 << 20),
        cost_estimate=pl.CostEstimate(
            flops=2 * 2 * half * depth * sum(widths), bytes_accessed=30 << 20, transcendentals=0
        ),
        name="project",
    )(core, turned, other, norms, w)


def cell_tile_low(core_ref, mine_ref, other_ref):
    return jnp.where(pl.program_id(0) // 2 == core_ref[0], mine_ref[0], other_ref[...])


def valid_lanes(len_ref, tile):
    lane = lax.broadcasted_iota(jnp.int32, (1, tile), 1) + pl.program_id(0) * tile
    return lane < len_ref[0]


def hand_over_kernel(core_ref, first_ref, second_ref, first_out, second_out):
    first_out[...] = first_ref[0]
    second_out[...] = second_ref[0]


def hand_over(core, first, second):
    _, depth, half = first.shape
    tile = half // 2
    taken = pl.BlockSpec((1, depth, tile), lambda step, core: (1 - core[0], 0, step))
    return pl.pallas_call(
        hand_over_kernel,
        grid_spec=pltpu.PrefetchScalarGridSpec(
            num_scalar_prefetch=1,
            grid=(2,),
            in_specs=[taken, taken],
            out_specs=[lane_tiles(depth, tile)] * 2,
        ),
        out_shape=[jax.ShapeDtypeStruct((depth, half), BF16)] * 2,
        name="hand_over",
    )(core, first, second)


def take_over_kernel(core_ref, got_ref, whole_ref, out_ref):
    out_ref[0] = got_ref[...]


def take_over(core, whole, got):
    depth, half = got.shape
    tile = half // 2
    return pl.pallas_call(
        take_over_kernel,
        grid_spec=pltpu.PrefetchScalarGridSpec(
            num_scalar_prefetch=1,
            grid=(2,),
            in_specs=[lane_tiles(depth, tile), pl.BlockSpec(memory_space=pl.ANY)],
            out_specs=pl.BlockSpec((1, depth, tile), lambda step, core: (1 - core[0], 0, step)),
        ),
        out_shape=jax.ShapeDtypeStruct(whole.shape, BF16),
        input_output_aliases={2: 0},
        name="take_over",
    )(core, got, whole)


def hidden_kernel(
    chips,
    core_ref,
    len_ref,
    mine_ref,
    other_ref,
    mine_grad_ref,
    other_grad_ref,
    first_ref,
    second_ref,
    w_ref,
    norm_ref,
    hidden_ref,
    normed_ref,
    grad_ref,
    rows_ref,
    o_rows_ref,
    w_turned_ref,
    scratch_ref,
):
    depth = w_ref.shape[0]
    tile = mine_ref.shape[2]

    @pl.when(pl.program_id(0) == 0)
    def _():
        scratch_ref[...] = jnp.zeros_like(scratch_ref)
        w_turned_ref[...] = jnp.transpose(w_ref[...])

    attended = jnp.concatenate([first_ref[...], second_ref[...]], axis=1)
    value = cell_tile(core_ref, mine_ref, other_ref)
    hidden = value + dot(w_turned_ref[...], attended[:, :depth], NT)
    hidden_ref[...] = hidden
    grad = cell_tile_low(core_ref, mine_grad_ref, other_grad_ref)
    grad = jnp.where(valid_lanes(len_ref, tile), grad, jnp.zeros((), BF16))
    grad_ref[:, :depth] = jnp.transpose(grad)
    grad_ref[:, depth:] = jnp.zeros((tile, grad_ref.shape[1] - depth), BF16)
    columns = jnp.transpose(norm_ref[...])
    normed = norm_down(hidden, columns[:, 2:3], columns[:, 3:4])
    spread_store(rows_ref, scratch_ref, normed, chips)
    normed_ref[...] = jnp.transpose(normed.astype(BF16))
    spread_store(o_rows_ref, scratch_ref, jnp.transpose(attended).astype(F32)[:depth], chips)


def hidden_state(core, length, cell, grad_cell, attended, w_out, norms, chips, rows_pad):
    _, depth, half = cell[0].shape
    tile = half // 2
    seq = 2 * half
    spread = jax.ShapeDtypeStruct((chips * rows_pad, seq), BF16)
    return pl.pallas_call(
        functools.partial(hidden_kernel, chips),
        grid_spec=pltpu.PrefetchScalarGridSpec(
            num_scalar_prefetch=2,
            grid=(4,),
            in_specs=cell_specs(depth, tile) * 2
            + [row_tiles(tile, part.shape[1]) for part in attended]
            + [once(w_out.shape), once(norms.shape)],
            out_specs=[lane_tiles(depth, tile), row_tiles(tile, depth), row_tiles(tile, WIDTH)]
            + [lane_tiles(chips * rows_pad, tile)] * 2,
            scratch_shapes=[pltpu.VMEM((depth, depth), BF16), pltpu.VMEM((depth + 8, tile), F32)],
        ),
        out_shape=[
            jax.ShapeDtypeStruct((depth, seq), F32),
            jax.ShapeDtypeStruct((seq, depth), BF16),
            jax.ShapeDtypeStruct((seq, WIDTH), BF16),
            spread,
            spread,
        ],
        compiler_params=pltpu.CompilerParams(vmem_limit_bytes=56 << 20),
        cost_estimate=pl.CostEstimate(
            flops=2 * seq * depth * depth, bytes_accessed=24 << 20, transcendentals=0
        ),
        name="hidden_state",
    )(core, length, *cell, *grad_cell, *attended, w_out, norms)


GELU = (2.0 / math.pi) ** 0.5


def hidden_units_kernel(
    tile, normed_ref, grad_ref, up_ref, down_ref, activated_ref, grad_upward_ref
):
    seq, depth = normed_ref.shape

    def begin(first):
        rows = slice(first, first + tile)
        return dot(normed_ref[rows], up_ref[...]), dot(grad_ref[rows, :depth], down_ref[...])

    def middle(first, upward, grad_activated):
        rows = slice(first, first + tile)
        square = upward * upward
        gate = 0.5 * jnp.tanh(upward * (GELU + (GELU * 0.044715) * square)) + 0.5
        activated = upward * gate
        slope = gate + 2.0 * activated * (1.0 - gate) * (GELU + (3 * GELU * 0.044715) * square)
        activated_ref[:, rows] = jnp.transpose(activated.astype(BF16))
        grad_upward_ref[rows] = (grad_activated * slope).astype(BF16)
        return ()

    staggered(list(range(0, seq, tile)), begin, middle, lambda first: None)


def hidden_units(normed, grad, w_up, w_down_turned, tile=512, rows=256):
    seq, depth = normed.shape
    units = w_up.shape[1]
    return pl.pallas_call(
        functools.partial(hidden_units_kernel, rows),
        grid=(pl.cdiv(units, tile),),
        in_specs=[once(normed.shape), once(grad.shape)] + [lane_tiles(depth, tile)] * 2,
        out_specs=[row_tiles(tile, seq), lane_tiles(seq, tile)],
        out_shape=[
            jax.ShapeDtypeStruct((units, seq), BF16),
            jax.ShapeDtypeStruct((seq, units), BF16),
        ],
        compiler_params=pltpu.CompilerParams(vmem_limit_bytes=56 << 20),
        cost_estimate=pl.CostEstimate(
            flops=2 * 2 * seq * depth * units,
            bytes_accessed=4 * depth * units + 4 * seq * units,
            transcendentals=seq * units,
        ),
        name="hidden_units",
    )(normed, grad, w_up, w_down_turned)


def norm_down_back(grad_in, value, gain, gain_ref, bias_ref):
    centred = value - jnp.mean(value, axis=0, keepdims=True)
    inverse = lax.rsqrt(jnp.mean(centred * centred, axis=0, keepdims=True) + EPSILON)
    normed = centred * inverse
    product = grad_in * normed
    for first in range(0, value.shape[1], LANES):
        lanes = slice(first, first + LANES)
        gain_ref[...] += product[:, lanes]
        bias_ref[...] += grad_in[:, lanes]
    scaled = grad_in * gain
    return inverse * (
        scaled
        - jnp.mean(scaled, axis=0, keepdims=True)
        - normed * jnp.mean(scaled * normed, axis=0, keepdims=True)
    )


def clear_first(*refs):
    @pl.when(pl.program_id(0) == 0)
    def _():
        for ref in refs:
            ref[...] = jnp.zeros_like(ref)


def hidden_grad_kernel(
    core_ref,
    len_ref,
    grad_up_ref,
    w_up_ref,
    hidden_ref,
    mine_grad_ref,
    other_grad_ref,
    w_ref,
    norm_ref,
    grad_hidden_ref,
    branch_ref,
    first_ref,
    second_ref,
    gain_ref,
    bias_ref,
):
    clear_first(gain_ref, bias_ref)
    depth, tile = hidden_ref.shape
    grad = cell_tile_low(core_ref, mine_grad_ref, other_grad_ref)
    grad = jnp.where(valid_lanes(len_ref, tile), grad, jnp.zeros((), BF16)).astype(F32)
    grad_normed = dot(w_up_ref[...], grad_up_ref[...], NT)
    columns = jnp.transpose(norm_ref[...])
    grad = grad + norm_down_back(grad_normed, hidden_ref[...], columns[:, 2:3], gain_ref, bias_ref)
    grad_hidden_ref[...] = grad
    branch = jnp.transpose(grad.astype(BF16))
    branch_ref[:, :depth] = branch
    branch_ref[:, depth:] = jnp.zeros((tile, branch_ref.shape[1] - depth), BF16)
    width = first_ref.shape[1]
    first_ref[...] = dot(branch, w_ref[:width], NT).astype(BF16)
    second_ref[:, : depth - width] = dot(branch, w_ref[width:], NT).astype(BF16)
    second_ref[:, depth - width :] = jnp.zeros((tile, second_ref.shape[1] - depth + width), BF16)


def hidden_grad(core, length, grad_upward, w_up, hidden, grad_cell, w_out, norms, widths):
    depth, seq = hidden.shape
    tile = seq // 4
    units = w_up.shape[1]
    return pl.pallas_call(
        hidden_grad_kernel,
        grid_spec=pltpu.PrefetchScalarGridSpec(
            num_scalar_prefetch=2,
            grid=(4,),
            in_specs=[row_tiles(tile, units), once(w_up.shape), lane_tiles(depth, tile)]
            + cell_specs(depth, tile)
            + [once(w_out.shape), once(norms.shape)],
            out_specs=[lane_tiles(depth, tile), row_tiles(tile, WIDTH)]
            + [row_tiles(tile, width) for width in widths]
            + [once((depth, LANES))] * 2,
        ),
        out_shape=[
            jax.ShapeDtypeStruct((depth, seq), F32),
            jax.ShapeDtypeStruct((seq, WIDTH), BF16),
        ]
        + [jax.ShapeDtypeStruct((seq, width), BF16) for width in widths]
        + [jax.ShapeDtypeStruct((depth, LANES), F32)] * 2,
        compiler_params=pltpu.CompilerParams(vmem_limit_bytes=58 << 20),
        cost_estimate=pl.CostEstimate(
            flops=2 * seq * depth * (units + depth), bytes_accessed=40 << 20, transcendentals=0
        ),
        name="hidden_grad",
    )(core, length, grad_upward, w_up, hidden, *grad_cell, w_out, norms)


def halves(depth, tile):
    return [
        pl.BlockSpec((depth, tile), lambda step, core, *_: (0, jnp.minimum(step, 1))),
        pl.BlockSpec((1, depth, tile), lambda step, core, *_: (core[0], 0, jnp.maximum(step - 2, 0))),
    ]


def half_place(step, core):
    return jnp.where(step < 2, 2 - 2 * core + step, 2 * core + step - 2)


def tokens_grad_kernel(
    core_ref,
    first_ref,
    second_ref,
    wide_first_ref,
    wide_second_ref,
    mine_ref,
    other_ref,
    grad_hidden_ref,
    norm_ref,
    sent_ref,
    kept_ref,
    gain_ref,
    bias_ref,
):
    clear_first(gain_ref, bias_ref)
    step = pl.program_id(0)
    grad_normed = dot(wide_first_ref[...], first_ref[...], NT)
    grad_normed += dot(wide_second_ref[...], second_ref[...], NT)
    value = jnp.where(step < 2, other_ref[...], mine_ref[0]).astype(F32)
    columns = jnp.transpose(norm_ref[...])
    grad = norm_down_back(grad_normed, value, columns[:, 0:1], gain_ref, bias_ref)
    grad = (grad_hidden_ref[...] + grad).astype(BF16)

    @pl.when(step < 2)
    def _():
        sent_ref[...] = grad

    @pl.when(step >= 2)
    def _():
        kept_ref[0] = grad


def tokens_gradient(core, grads, wides, cell, grad_hidden, norms):
    depth, seq = grad_hidden.shape
    tile = seq // 4
    return pl.pallas_call(
        tokens_grad_kernel,
        grid_spec=pltpu.PrefetchScalarGridSpec(
            num_scalar_prefetch=1,
            grid=(4,),
            in_specs=[
                pl.BlockSpec((tile, part.shape[1]), lambda step, core: (half_place(step, core[0]), 0))
                for part in grads
            ]
            + [once(part.shape) for part in wides]
            + [
                pl.BlockSpec((1, depth, tile), lambda step, core: (core[0], 0, jnp.maximum(step - 2, 0))),
                pl.BlockSpec((depth, tile), lambda step, core: (0, jnp.minimum(step, 1))),
                pl.BlockSpec((depth, tile), lambda step, core: (0, half_place(step, core[0]))),
                once(norms.shape),
            ],
            out_specs=halves(depth, tile) + [once((depth, LANES))] * 2,
        ),
        out_shape=[
            jax.ShapeDtypeStruct((depth, seq // 2), BF16),
            jax.ShapeDtypeStruct((2, depth, seq // 2), BF16),
        ]
        + [jax.ShapeDtypeStruct((depth, LANES), F32)] * 2,
        compiler_params=pltpu.CompilerParams(vmem_limit_bytes=56 << 20),
        cost_estimate=pl.CostEstimate(
            flops=2 * seq * depth * 3 * WIDTH, bytes_accessed=30 << 20, transcendentals=0
        ),
        name="tokens_gradient",
    )(core, *grads, *wides, *cell, grad_hidden, norms)


def mixed_sent_kernel(core_ref, activated_ref, w_ref, hidden_ref, out_ref):
    out_ref[...] = (hidden_ref[...] + dot(w_ref[...], activated_ref[...])).astype(BF16)


def mixed_kept_kernel(core_ref, activated_ref, w_ref, hidden_ref, out_ref):
    out_ref[0] = (hidden_ref[...] + dot(w_ref[...], activated_ref[...])).astype(BF16)


def mixed_half(core, activated, w_down_turned, hidden, sent):
    depth, seq = hidden.shape
    units = activated.shape[0]
    tile = seq // 4

    def place(step, core):
        return 0, (2 - 2 * core[0] if sent else 2 * core[0]) + step

    if sent:
        out_spec = lane_tiles(depth, tile)
        out_shape = jax.ShapeDtypeStruct((depth, seq // 2), BF16)
    else:
        out_spec = pl.BlockSpec((1, depth, tile), lambda step, core: (core[0], 0, step))
        out_shape = jax.ShapeDtypeStruct((2, depth, seq // 2), BF16)
    return pl.pallas_call(
        mixed_sent_kernel if sent else mixed_kept_kernel,
        grid_spec=pltpu.PrefetchScalarGridSpec(
            num_scalar_prefetch=1,
            grid=(2,),
            in_specs=[
                pl.BlockSpec((units, tile), place),
                once(w_down_turned.shape),
                pl.BlockSpec((depth, tile), place),
            ],
            out_specs=out_spec,
        ),
        out_shape=out_shape,
        compiler_params=pltpu.CompilerParams(vmem_limit_bytes=56 << 20),
        cost_estimate=pl.CostEstimate(
            flops=seq * depth * units, bytes_accessed=20 << 20, transcendentals=0
        ),
        name="mixed_half",
    )(core, activated, w_down_turned, hidden)


def swap_cores(value):
    return lax.ppermute(value, "blk", [(0, 1), (1, 0)])


def swap_chips(value, bit):
    count = lax.axis_size("cells")
    return lax.ppermute(value, "cells", [(place, place ^ bit) for place in range(count)])


class Scatter:
    def __init__(self, grads, rows, cut=None, axis=-1, late=False):
        bits = lax.axis_size("cells").bit_length() - 1
        place = lax.axis_index("cells")
        self.sides = [(place >> (bits - 1 - axis)) & 1 for axis in range(bits)]
        self.bits = bits
        grads = grads.reshape((2,) * bits + (rows, grads.shape[1]))
        low, next_low = bits - 1, bits - 2
        higher = list(range(next_low - 1, -1, -1))
        if late:
            self.parts = [(grads, higher + [low, next_low])]
        else:
            first, second = jnp.split(grads, [cut], axis=axis)
            self.parts = [(first, [low, next_low]), (second, [next_low, low])]
            self.rest = higher
            self.axis = axis
        self.sent = None
        self.got = None

    def _half(self, value, axis, other):
        side = self.sides[axis]
        return lax.dynamic_index_in_dim(value, 1 - side if other else side, axis, keepdims=True)

    def send(self):
        if self.got is not None:
            added = []
            for (kept, axes), got in zip(self.parts, self.got):
                total = self._half(kept, axes[0], False).astype(F32) + got.astype(F32)
                added.append((total.astype(BF16), axes[1:]))
            if len(added) == 2 and not added[0][1]:
                joined = jnp.concatenate([added[0][0], added[1][0]], axis=self.axis)
                added = [(joined, self.rest)]
            self.parts = added
        self.sent = [self._half(kept, axes[0], True) for kept, axes in self.parts]
        return self.sent

    def move(self, sent):
        self.got = [
            swap_chips(value, 1 << (self.bits - 1 - axes[0]))
            for value, (_, axes) in zip(sent, self.parts)
        ]
        return self.got

    def arrived(self, got):
        self.got = list(got)

    def result(self):
        ((kept, axes),) = self.parts
        total = self._half(kept, axes[0], False).astype(F32) + self.got[0].astype(F32)
        return total.reshape(total.shape[-2:])


def begin_with(chain, *scatters):
    sends = [item.send() for item in scatters]
    flat = [value for group in sends for value in group]
    chain, *flat = lax.optimization_barrier((chain, *flat))
    for item, group in zip(scatters, sends):
        item.move(flat[: len(group)])
        flat = flat[len(group) :]
    return chain


def finish_with(chain, *scatters):
    groups = [item.got for item in scatters]
    flat = [value for group in groups for value in group]
    chain, *flat = lax.optimization_barrier((chain, *flat))
    for item, group in zip(scatters, groups):
        item.arrived(flat[: len(group)])
        flat = flat[len(group) :]
    return chain


class AllSum:
    def __init__(self, value):
        self.value = value
        self.stage = 0
        self.got = None

    def send(self):
        if self.got is not None:
            self.value = self.value + self.got[0]
        return [self.value]

    def move(self, sent):
        if self.stage == 0:
            self.got = [swap_cores(sent[0])]
        else:
            self.got = [swap_chips(sent[0], 1 << (self.stage - 1))]
        self.stage += 1
        return self.got

    def arrived(self, got):
        self.got = list(got)

    def result(self):
        return self.value + self.got[0]


def columns(value, first, size):
    return lax.dynamic_slice_in_dim(value, first, size, axis=1)


def cell_split(
    tokens, lengths, attn_gain, attn_bias, w_qkv, w_out, mlp_gain, mlp_bias, w_up, w_down, cotangent
):
    row_count = tokens.shape[0]
    seq = 2 * row_count
    core = lax.axis_index("blk")
    chips = lax.axis_size("cells")
    rows = D // chips
    rows_pad = -(-rows // 8) * 8

    def tie(*values):
        return lax.optimization_barrier(values)

    def pick(first, second):
        return jnp.where(core == 0, first, second)

    core_index = core.reshape(1).astype(jnp.int32)
    length = pick(lengths[0], lengths[1])
    length = length.reshape(1)
    turned, turned_cotangent = tokens.transpose(1, 2, 0), cotangent.transpose(1, 2, 0)
    sent, sent_cotangent = hand_over(core_index, turned, turned_cotangent)
    cell = (turned, swap_cores(sent))
    grad_cell = (turned_cotangent, swap_cores(sent_cotangent))
    norms = jnp.stack([attn_gain, attn_bias, mlp_gain, mlp_bias] * 2)
    w_down_turned = w_down.T

    big, small = 16, HEADS - 16
    spans = ((0, big * HD), (big * HD, small * HD))
    qkv_big, qkv_small, one_rows, wide_big, wide_small = project(
        core_index, *cell, norms, w_qkv, spans, chips, rows_pad
    )
    attended_big, lse_big = attention_forward(qkv_big, length, big)
    attended_small, lse_small = attention_forward(qkv_small, length, small)
    hidden, normed_mlp, grad_low, mlp_rows, attended_rows = hidden_state(
        core_index, length, cell, grad_cell, (attended_big, attended_small), w_out, norms, chips, rows_pad
    )
    activated, grad_upward = hidden_units(normed_mlp, grad_low, w_up, w_down_turned)

    half = D // 2
    window = -(-half // LANES) * LANES
    starts = (0, WIDTH - window)
    ours, theirs = pick(*starts), pick(*starts[::-1])
    up_all = w_up.shape[1]
    up_window = -(-up_all // 2 // LANES) * LANES
    up_starts = (0, up_all - up_window)
    up_ours, up_theirs = pick(*up_starts), pick(*up_starts[::-1])
    big_width, small_width = qkv_big.shape[1] // 3, qkv_small.shape[1] // 3
    big_window = big_width + -(-half // LANES) * LANES
    big_starts = (0, 3 * big_width - big_window)
    big_ours, big_theirs = pick(*big_starts), pick(*big_starts[::-1])
    small_window = 2 * small_width
    small_starts = (0, small_width)
    small_ours, small_theirs = pick(*small_starts), pick(*small_starts[::-1])

    down_sent = dot(activated, columns(grad_low, theirs, window)).astype(BF16)
    down_got = swap_cores(down_sent)
    up_sent = dot(mlp_rows, columns(grad_upward, up_theirs, up_window)).astype(BF16)
    up_got = swap_cores(up_sent)
    grad_low_d, up_sent = tie(grad_low, up_sent)
    down_sum = dot(activated, columns(grad_low_d, ours, window)) + down_got.astype(F32)
    down_rows = w_down.shape[0] // chips
    down = Scatter(down_sum.astype(BF16), down_rows, down_rows // 16 * 8, axis=-2)
    grad_upward_d = begin_with(grad_upward, down)
    up_sum = dot(mlp_rows, columns(grad_upward_d, up_ours, up_window)) + up_got.astype(F32)
    up_sum = up_sum.astype(BF16)

    grad_hidden, grad_branch, grad_attended_big, grad_attended_small, *mlp_norms = hidden_grad(
        core_index, length, grad_upward_d, w_up, hidden, grad_cell, w_out, norms, (big_width, small_width)
    )
    grad_branch, up_sum = tie(grad_branch, up_sum)
    grad_branch = finish_with(grad_branch, down)
    up = Scatter(up_sum, rows_pad, up_window // 2)
    grad_branch = begin_with(grad_branch, down, up)
    out_sent = dot(attended_rows, columns(grad_branch, theirs, window)).astype(BF16)
    out_got = swap_cores(out_sent)
    out_sum = dot(attended_rows, columns(grad_branch, ours, window)) + out_got.astype(F32)
    out = Scatter(out_sum.astype(BF16), rows_pad, late=True)
    grad_attended_big, grad_attended_small = begin_with((grad_attended_big, grad_attended_small), out)

    grad_big = attention_backward(
        qkv_big, attended_big, grad_attended_big, lse_big, length
    )
    grad_big = finish_with(grad_big, down, up, out)
    big_sent = dot(one_rows, columns(grad_big, big_theirs, big_window)).astype(BF16)
    big_got = swap_cores(big_sent)
    grad_big, big_sent = tie(grad_big, big_sent)
    grad_big = begin_with(grad_big, down, up, out)
    big_sum = dot(one_rows, columns(grad_big, big_ours, big_window)) + big_got.astype(F32)
    whole_big = Scatter(big_sum.astype(BF16), rows_pad, big_window // 2)
    qkv_small = begin_with(qkv_small, whole_big)
    grad_small = attention_backward(
        qkv_small, attended_small, grad_attended_small, lse_small, length
    )
    small_sent = dot(one_rows, columns(grad_small, small_theirs, small_window)).astype(BF16)
    small_got = swap_cores(small_sent)
    grad_small, grad_big, small_sent = tie(grad_small, grad_big, small_sent)
    grad_small, small_got, grad_big = tie(grad_small, small_got, grad_big)
    small_sum = dot(one_rows, columns(grad_small, small_ours, small_window)) + small_got.astype(F32)
    whole_small = Scatter(small_sum.astype(BF16), rows_pad, small_window // 2)
    grad_big = finish_with(grad_big, down, up, out)
    grad_big = begin_with(grad_big, whole_small, down, up, out)
    tokens_sent, tokens_kept, *attn_norms = tokens_gradient(
        core_index, (grad_big, grad_small), (wide_big, wide_small), cell, grad_hidden, norms
    )
    tokens_got = swap_cores(tokens_sent)
    norm_sums = AllSum(jnp.stack([jnp.sum(part, axis=1) for part in (*attn_norms, *mlp_norms)] * 2))
    activated, tokens_sent = tie(activated, tokens_sent)
    activated = finish_with(activated, whole_big, whole_small)
    activated = begin_with(activated, norm_sums, whole_big, whole_small)
    mixed_sent = mixed_half(core_index, activated, w_down_turned, hidden, True)
    mixed_got = swap_cores(mixed_sent)
    activated, mixed_sent = tie(activated, mixed_sent)
    activated = finish_with(activated, up, out, norm_sums, whole_big, whole_small)
    activated = begin_with(activated, norm_sums, whole_big, whole_small, up, out)
    mixed_kept = mixed_half(core_index, activated, w_down_turned, hidden, False)
    mixed_kept = finish_with(mixed_kept, norm_sums, whole_big, whole_small)
    mixed_kept = begin_with(mixed_kept, norm_sums, whole_big, whole_small)
    w_down_share, up_share, w_out_share = down.result(), up.result(), out.result()
    tokens_grad = take_over(core_index, tokens_kept, tokens_got)
    mixed = take_over(core_index, mixed_kept, mixed_got)
    mixed = finish_with(mixed, norm_sums)
    mixed = begin_with(mixed, norm_sums)
    big_share, small_share = whole_big.result(), whole_small.result()
    mixed = finish_with(mixed, norm_sums)
    mixed = begin_with(mixed, norm_sums)
    sums = norm_sums.result()

    shift = big_width + half - big_starts[1]
    w_qkv_share = pick(
        jnp.concatenate(
            [
                big_share[:rows, :big_width],
                small_share[:rows, : small * HD],
                big_share[:rows, big_width : big_width + half],
            ],
            axis=1,
        ),
        jnp.concatenate(
            [
                big_share[:rows, shift : 2 * big_width - big_starts[1]],
                small_share[:rows, : small * HD],
                big_share[:rows, 2 * big_width - big_starts[1] :],
                small_share[:rows, small_width : small_width + small * HD],
            ],
            axis=1,
        ),
    )

    def own_columns(share, starts, all_columns):
        second = all_columns // 2 - starts[1]
        return pick(share[:, : all_columns // 2], share[:, second : second + all_columns // 2])

    return (
        mixed.transpose(2, 0, 1),
        tokens_grad.transpose(2, 0, 1),
        sums[0],
        sums[1],
        w_qkv_share,
        own_columns(w_out_share[:rows], starts, D),
        sums[2],
        sums[3],
        own_columns(up_share[:rows], up_starts, up_all),
        own_columns(w_down_share, starts, D),
    )


def per_device(mesh, tokens, *rest):
    chips = mesh.shape["cells"]
    if mesh.shape["blk"] == 2 and tokens.shape[1] == 2 and chips & (chips - 1) == 0 and chips >= 8:
        return cell_split(tokens, *rest)
    return position_split(tokens, *rest)


def solution(mesh):
    placed = (
        P("blk", "cells", None),
        P("cells"),
        P(),
        P(),
        P(),
        P(),
        P(),
        P(),
        P(),
        P(),
        P("blk", "cells", None),
    )
    return jax.shard_map(
        functools.partial(per_device, mesh),
        mesh=mesh,
        in_specs=placed,
        out_specs=(
            P("blk", "cells", None),
            P("blk", "cells", None),
            P(),
            P(),
            P("cells", "blk"),
            P("cells", "blk"),
            P(),
            P(),
            P("cells", "blk"),
            P("cells", "blk"),
        ),
        check_vma=False,
    )
```

```python
import functools
import math

import jax
import jax.numpy as jnp
from jax import lax
from jax.experimental import pallas as pl
from jax.experimental.pallas import tpu as pltpu
from jax.sharding import PartitionSpec as P

D = 1120
HEADS = 20
HD = 56


EPSILON = 1e-05
MASKED = -1e30
LOG2E = 1.4426950408889634
LANES = 128
WIDTH = 1152
WINDOW = 256
SHARE = 1
TILE = 256
BF16 = jnp.bfloat16
F32 = jnp.float32
NN = (((1,), (0,)), ((), ()))
NT = (((1,), (1,)), ((), ()))
TN = (((0,), (0,)), ((), ()))


def norm_forward(values_in, gain_vec, bias_vec):
    centred = values_in - jnp.mean(values_in, axis=-1, keepdims=True)
    inverse = lax.rsqrt(jnp.mean(centred * centred, axis=-1, keepdims=True) + EPSILON)
    normed = centred * inverse
    return (normed, inverse, normed * gain_vec + bias_vec)


def norm_backward(grad_in, normed, inverse, gain_vec):
    scaled = grad_in * gain_vec
    grad_out = inverse * (
        scaled
        - jnp.mean(scaled, axis=-1, keepdims=True)
        - normed * jnp.mean(scaled * normed, axis=-1, keepdims=True)
    )
    return (grad_out, jnp.sum(grad_in * normed, axis=(0, 1)), jnp.sum(grad_in, axis=(0, 1)))


def key_scores(query_heads, key_piece, query_pos, key_start, lengths):
    key_count = key_piece.shape[0]
    key_heads = key_piece.reshape(key_count, key_piece.shape[1], HEADS, HD)
    scores = jnp.einsum(
        "qchd,kchd->chqk", query_heads, key_heads, preferred_element_type=jnp.float32
    ) * HD ** (-0.5)
    key_pos = key_start + jnp.arange(key_count, dtype=jnp.int32)
    allowed = (key_pos[None, None, :] <= query_pos[None, :, None]) & (
        key_pos[None, None, :] < lengths[:, None, None]
    )
    allowed = allowed[:, None, :, :]
    return (jnp.where(allowed, scores, MASKED), allowed)


def key_sweep(step_fn, initial, pieces, row_count, block_turns):

    def one_turn(turn_index, state_in):
        row_start = turn_index * row_count
        taken = tuple(
            (lax.dynamic_slice_in_dim(full_array, row_start, row_count, 0) for full_array in pieces)
        )
        return step_fn(state_in, taken, row_start)

    return lax.fori_loop(0, block_turns, one_turn, initial)


def position_split(
    tokens, lengths, attn_gain, attn_bias, w_qkv, w_out, mlp_gain, mlp_bias, w_up, w_down, cotangent
):
    row_count = tokens.shape[0]
    cell_count = tokens.shape[1]
    block_turns = lax.axis_size("blk")
    score_scale = HD ** (-0.5)
    query_pos = lax.axis_index("blk") * row_count + jnp.arange(row_count, dtype=jnp.int32)
    inputs = tokens.astype(jnp.float32)
    normed_one, inverse_one, pre_one = norm_forward(inputs, attn_gain, attn_bias)
    normed_low = pre_one.astype(jnp.bfloat16)
    qkv_vals = jnp.einsum(
        "rcd,de->rce", normed_low, w_qkv, preferred_element_type=jnp.float32
    ).astype(jnp.bfloat16)
    key_vals = qkv_vals[..., D : 2 * D]
    value_vals = qkv_vals[..., 2 * D :]
    query_heads = qkv_vals[..., :D].reshape(row_count, cell_count, HEADS, HD)
    start_max = jnp.full((cell_count, HEADS, row_count), MASKED, jnp.float32)
    start_sum = jnp.zeros((cell_count, HEADS, row_count), jnp.float32)
    start_out = jnp.zeros((row_count, cell_count, HEADS, HD), jnp.float32)
    scores, allowed = key_scores(
        query_heads,
        (lax.all_gather(key_vals, "blk", axis=0, tiled=True),)[0],
        query_pos,
        jnp.int32(0),
        lengths,
    )
    new_max = jnp.maximum(start_max, jnp.max(scores, axis=-1))
    weights = jnp.where(allowed, jnp.exp(scores - new_max[..., None]), 0.0)
    run_sum = jnp.sum(weights, axis=-1)
    log_total = new_max + jnp.log(run_sum)

    def probabilities(key_piece, key_start):
        scores, allowed = key_scores(query_heads, key_piece, query_pos, key_start, lengths)
        return jnp.where(allowed, jnp.exp(scores - log_total[..., None]), 0.0)

    pieces = (
        lax.all_gather(key_vals, "blk", axis=0, tiled=True),
        lax.all_gather(value_vals, "blk", axis=0, tiled=True),
    )
    prob_vals = probabilities(pieces[0], jnp.int32(0)).astype(jnp.bfloat16)
    value_heads = pieces[1].reshape(pieces[1].shape[0], cell_count, HEADS, HD)
    out_acc = jnp.einsum(
        "chqk,kchd->qchd", prob_vals, value_heads, preferred_element_type=jnp.float32
    )
    attended = out_acc.reshape(row_count, cell_count, D).astype(jnp.bfloat16)
    hidden = inputs + jnp.einsum("rcd,de->rce", attended, w_out, preferred_element_type=jnp.float32)
    normed_two, inverse_two, pre_two = norm_forward(hidden, mlp_gain, mlp_bias)
    normed_mlp = pre_two.astype(jnp.bfloat16)
    upward = jnp.einsum("rcd,df->rcf", normed_mlp, w_up, preferred_element_type=jnp.float32)
    activated_full, gelu_back = jax.vjp(
        lambda value_in: jax.nn.gelu(value_in, approximate=True), upward
    )
    activated = activated_full.astype(jnp.bfloat16)
    mixed = (
        hidden + jnp.einsum("rcf,fd->rcd", activated, w_down, preferred_element_type=jnp.float32)
    ).astype(jnp.bfloat16)
    valid_rows = (query_pos[:, None] < lengths[None, :]).astype(jnp.float32)
    grad_out = cotangent.astype(jnp.float32) * valid_rows[..., None]
    grad_low = grad_out.astype(jnp.bfloat16)
    w_down_grad = jnp.einsum("rcf,rcd->fd", activated, grad_low, preferred_element_type=jnp.float32)
    grad_act = jnp.einsum("rcd,fd->rcf", grad_low, w_down, preferred_element_type=jnp.float32)
    grad_upward = gelu_back(grad_act)[0].astype(jnp.bfloat16)
    w_up_grad = jnp.einsum(
        "rcd,rcf->df", normed_mlp, grad_upward, preferred_element_type=jnp.float32
    )
    grad_normed_two = jnp.einsum(
        "rcf,df->rcd", grad_upward, w_up, preferred_element_type=jnp.float32
    )
    grad_hidden_ln, mlp_gain_grad, mlp_bias_grad = norm_backward(
        grad_normed_two, normed_two, inverse_two, mlp_gain
    )
    grad_hidden = grad_out + grad_hidden_ln
    grad_branch = grad_hidden.astype(jnp.bfloat16)
    w_out_grad = jnp.einsum(
        "rce,rcd->ed", attended, grad_branch, preferred_element_type=jnp.float32
    )
    grad_attended = jnp.einsum(
        "rcd,ed->rce", grad_branch, w_out, preferred_element_type=jnp.float32
    ).astype(jnp.bfloat16)
    grad_heads = grad_attended.reshape(row_count, cell_count, HEADS, HD)
    whole_keys, whole_values = (
        lax.all_gather(key_vals, "blk", axis=0, tiled=True),
        lax.all_gather(value_vals, "blk", axis=0, tiled=True),
    )

    def attention_grads(key_piece, value_piece, key_start):
        prob_full = probabilities(key_piece, key_start)
        value_heads = value_piece.reshape(value_piece.shape[0], cell_count, HEADS, HD)
        dprobs = jnp.einsum(
            "qchd,kchd->chqk", grad_heads, value_heads, preferred_element_type=jnp.float32
        )
        return (prob_full, dprobs)

    def delta_step(state_in, pieces, key_start):
        prob_full, dprobs = attention_grads(pieces[0], pieces[1], key_start)
        return state_in + jnp.sum(prob_full * dprobs, axis=-1)

    row_delta = key_sweep(delta_step, start_sum, (whole_keys, whole_values), row_count, block_turns)

    def query_step(state_in, pieces, key_start):
        prob_full, dprobs = attention_grads(pieces[0], pieces[1], key_start)
        dscore = (prob_full * (dprobs - row_delta[..., None])).astype(jnp.bfloat16)
        key_heads = pieces[0].reshape(pieces[0].shape[0], cell_count, HEADS, HD)
        return state_in + jnp.einsum(
            "chqk,kchd->qchd", dscore, key_heads, preferred_element_type=jnp.float32
        )

    query_acc = key_sweep(query_step, start_out, (whole_keys, whole_values), row_count, block_turns)
    grad_queries = (query_acc * score_scale).reshape(row_count, cell_count, D).astype(jnp.bfloat16)
    key_piece = whole_keys
    value_piece = whole_values
    prob_full, dprobs = attention_grads(key_piece, value_piece, jnp.int32(0))
    dscore = (prob_full * (dprobs - row_delta[..., None])).astype(jnp.bfloat16)
    grad_keys = (
        jnp.einsum("chqk,qchd->kchd", dscore, query_heads, preferred_element_type=jnp.float32)
        * score_scale
    )
    grad_values = jnp.einsum(
        "chqk,qchd->kchd",
        prob_full.astype(jnp.bfloat16),
        grad_heads,
        preferred_element_type=jnp.float32,
    )
    kv_summed = lax.psum_scatter(
        jnp.concatenate(
            [
                grad_keys.reshape(row_count * lax.axis_size("blk"), cell_count, D),
                grad_values.reshape(row_count * lax.axis_size("blk"), cell_count, D),
            ],
            axis=-1,
        ),
        "blk",
        scatter_dimension=0,
        tiled=True,
    )
    grad_qkv = jnp.concatenate([grad_queries, kv_summed.astype(jnp.bfloat16)], axis=-1)
    w_qkv_grad = jnp.einsum("rcd,rce->de", normed_low, grad_qkv, preferred_element_type=jnp.float32)
    grad_normed_one = jnp.einsum("rce,de->rcd", grad_qkv, w_qkv, preferred_element_type=jnp.float32)
    grad_inputs_ln, attn_gain_grad, attn_bias_grad = norm_backward(
        grad_normed_one, normed_one, inverse_one, attn_gain
    )
    tokens_grad = (grad_hidden + grad_inputs_ln).astype(jnp.bfloat16)
    norm_sums = lax.psum(
        (attn_gain_grad, attn_bias_grad, mlp_gain_grad, mlp_bias_grad), ("blk", "cells")
    )
    shares = (
        lax.psum_scatter(
            w_qkv_grad.astype(jnp.bfloat16), "cells", scatter_dimension=0, tiled=True
        ).astype(jnp.float32),
        lax.psum_scatter(
            w_out_grad.astype(jnp.bfloat16), "cells", scatter_dimension=0, tiled=True
        ).astype(jnp.float32),
        lax.psum_scatter(
            w_up_grad.astype(jnp.bfloat16), "cells", scatter_dimension=0, tiled=True
        ).astype(jnp.float32),
        lax.psum_scatter(
            w_down_grad.astype(jnp.bfloat16), "cells", scatter_dimension=0, tiled=True
        ).astype(jnp.float32),
    )
    summed = (
        lax.psum_scatter(
            shares[0].astype(jnp.bfloat16), "blk", scatter_dimension=1, tiled=True
        ).astype(jnp.float32),
        lax.psum_scatter(
            shares[1].astype(jnp.bfloat16), "blk", scatter_dimension=1, tiled=True
        ).astype(jnp.float32),
        lax.psum_scatter(
            shares[2].astype(jnp.bfloat16), "blk", scatter_dimension=1, tiled=True
        ).astype(jnp.float32),
        lax.psum_scatter(
            shares[3].astype(jnp.bfloat16), "blk", scatter_dimension=1, tiled=True
        ).astype(jnp.float32),
    )
    return (
        mixed,
        tokens_grad,
        norm_sums[0],
        norm_sums[1],
        summed[0],
        summed[1],
        norm_sums[2],
        norm_sums[3],
        summed[2],
        summed[3],
    )


def cost(product):
    return pl.CostEstimate(flops=int(product * SHARE), bytes_accessed=1, transcendentals=0)


def dot(left, right, dims=NN):
    return lax.dot_general(left, right, dims, preferred_element_type=F32)


def head_lanes(head, width):
    start = jnp.minimum(head * HD // LANES, (width - WINDOW) // LANES) * LANES
    start = pl.multiple_of(start, LANES)
    lane = lax.broadcasted_iota(jnp.int32, (1, WINDOW), 1)
    offset = lane + (start - head * HD)
    own = (offset >= 0) & (offset < HD)
    spare = lane == jnp.where(start == head * HD, WINDOW - 1, 0)
    return start, own, spare


def key_bias(len_ref, seq):
    rows = lax.broadcasted_iota(jnp.int32, (seq, 1), 0)
    return jnp.where(rows < len_ref[0], 0.0, MASKED).astype(BF16)


def masked_query(q_ref, win, own, spare):
    return jnp.where(own, q_ref[:, win], jnp.where(spare, 1.0, 0.0).astype(BF16))


def causal_tile():
    key_row = lax.broadcasted_iota(jnp.int32, (TILE, TILE), 0)
    query_lane = lax.broadcasted_iota(jnp.int32, (TILE, TILE), 1)
    return key_row <= query_lane


def staggered(jobs, begin, middle, end):
    started = begin(jobs[0])
    waiting = None
    for index, job in enumerate(jobs):
        current = started
        if index + 1 < len(jobs):
            started = begin(jobs[index + 1])
        result = middle(job, *current)
        if waiting is not None:
            end(*waiting)
        waiting = (job, *result)
    end(*waiting)


def attention_forward_kernel(per, len_ref, q_ref, k_ref, v_ref, o_ref, lse_ref):
    step = pl.program_id(0)
    seq, width = q_ref.shape

    @pl.when(step == 0)
    def _():
        o_ref[...] = jnp.zeros_like(o_ref)

    bias = key_bias(len_ref, seq)
    keep = causal_tile()
    scale = LOG2E * HD ** (-0.5)
    jobs = []
    for slot in range(per):
        start, own, spare = head_lanes(step * per + slot, width)
        win = pl.ds(start, WINDOW)
        k_win = jnp.where(spare, bias, k_ref[:, win])
        q_win = masked_query(q_ref, win, own, spare)
        v_turned = jnp.transpose(v_ref[:, win])
        for turn in range(seq // TILE):
            jobs.append((slot, turn * TILE, win, own, k_win, q_win, v_turned))

    def begin(job):
        _, low, _, _, k_win, q_win, _ = job
        return (dot(k_win[: low + TILE], q_win[low : low + TILE], NT),)

    def middle(job, scores):
        slot, low = job[:2]
        edge = jnp.where(keep, scores[low:], MASKED)
        scores = edge if low == 0 else jnp.concatenate([scores[:low], edge], axis=0)
        peak = jnp.max(scores, axis=0, keepdims=True) * scale
        weights = jnp.exp2(scores * scale - peak)
        total = jnp.sum(weights, axis=0, keepdims=True)
        lse_ref[slot, :, low : low + TILE] = jnp.broadcast_to(peak + jnp.log2(total), (8, TILE))
        return weights.astype(BF16), total

    def end(job, weights, total):
        _, low, win, own, _, _, v_turned = job
        out = dot(v_turned[:, : low + TILE], weights) * (1.0 / total)
        rows = slice(low, low + TILE)
        o_ref[rows, win] = jnp.where(own, jnp.transpose(out).astype(BF16), o_ref[rows, win])

    staggered(jobs, begin, middle, end)


def attention_backward_kernel(
    per, len_ref, q_ref, k_ref, v_ref, o_ref, do_ref, lse_ref, grad_ref, delta_ref, acc_ref
):
    step = pl.program_id(0)
    seq, width = q_ref.shape

    @pl.when(step == 0)
    def _():
        grad_ref[...] = jnp.zeros_like(grad_ref)
        lane = lax.broadcasted_iota(jnp.int32, (delta_ref.shape[0], width), 1)
        first = lax.broadcasted_iota(jnp.int32, (delta_ref.shape[0], width), 0) * HD
        pick = jnp.where((lane >= first) & (lane < first + HD), 1.0, 0.0).astype(BF16)
        for turn in range(seq // TILE):
            rows = slice(turn * TILE, (turn + 1) * TILE)
            product = o_ref[rows].astype(F32) * do_ref[rows].astype(F32)
            upper = product.astype(BF16)
            lower = (product - upper.astype(F32)).astype(BF16)
            delta_ref[:, rows] = dot(pick, upper, NT) + dot(pick, lower, NT)

    bias = key_bias(len_ref, seq)
    keep = causal_tile()
    scale = LOG2E * HD ** (-0.5)
    turns = seq // TILE
    jobs = []
    for slot in range(per):
        head = step * per + slot
        start, own, spare = head_lanes(head, width)
        win = pl.ds(start, WINDOW)
        k_win = jnp.where(spare, bias, k_ref[:, win])
        q_win = masked_query(q_ref, win, own, spare)
        do_win = jnp.where(own, do_ref[:, win], jnp.zeros((), BF16))
        v_win = v_ref[:, win]
        lse = lse_ref[slot, 0:1, :]
        delta = delta_ref[pl.ds(head, 1), :]
        for turn in range(turns):
            jobs.append((slot, turn, start, own, k_win, q_win, do_win, v_win, lse, delta))

    def begin(job):
        _, turn, _, _, k_win, q_win, do_win, v_win, _, _ = job
        low = turn * TILE
        rows = slice(low, low + TILE)
        return dot(k_win[rows], q_win[low:], NT), dot(v_win[rows], do_win[low:], NT)

    def middle(job, scores, dprobs):
        turn, lse, delta = job[1], job[8], job[9]
        low = turn * TILE
        probs = jnp.exp2(scores * scale - lse[:, low:])
        edge = jnp.where(keep, probs[:, :TILE], 0.0)
        if turn + 1 < turns:
            edge = jnp.concatenate([edge, probs[:, TILE:]], axis=1)
        dscores = (edge * (dprobs - delta[:, low:])).astype(BF16)
        return edge.astype(BF16), dscores

    def end(job, probs, dscores):
        slot, turn, start, own, k_win, q_win, do_win = job[:7]
        low = turn * TILE
        rows = slice(low, low + TILE)

        def put(place, where, value):
            lanes = pl.ds(start + place * width, WINDOW)
            grad_ref[where, lanes] = jnp.where(own, value.astype(BF16), grad_ref[where, lanes])

        put(2, rows, dot(probs, do_win[low:]))
        put(1, rows, dot(dscores, q_win[low:]) * HD ** (-0.5))
        part = dot(dscores, k_win[rows], TN)
        if turn == 0:
            acc_ref[slot] = part
        else:
            acc_ref[slot, low:, :] += part
        if turn + 1 == turns:
            put(0, slice(0, seq), acc_ref[slot] * HD ** (-0.5))

    staggered(jobs, begin, middle, end)


def resident(shape, place=0):
    return pl.BlockSpec(shape, lambda step, *_: (0, place), pipeline_mode=pl.Buffered(1))


def attention_forward(qkv, length, heads, per=2):
    seq, width = qkv.shape[0], qkv.shape[1] // 3
    return pl.pallas_call(
        functools.partial(attention_forward_kernel, per),
        grid_spec=pltpu.PrefetchScalarGridSpec(
            num_scalar_prefetch=1,
            grid=(heads // per,),
            in_specs=[resident((seq, width), place) for place in range(3)],
            out_specs=[
                resident((seq, width)),
                pl.BlockSpec((per, 8, seq), lambda step, *_: (step, 0, 0)),
            ],
        ),
        out_shape=[
            jax.ShapeDtypeStruct((seq, width), BF16),
            jax.ShapeDtypeStruct((heads, 8, seq), F32),
        ],
        compiler_params=pltpu.CompilerParams(vmem_limit_bytes=32 << 20),
        cost_estimate=cost(4 * heads * seq * seq * WINDOW),
        name="attention_forward",
    )(length, qkv, qkv, qkv)


def attention_backward(qkv, attended, grad_attended, lse, length, per=2):
    seq, width = qkv.shape[0], qkv.shape[1] // 3
    heads = lse.shape[0]
    return pl.pallas_call(
        functools.partial(attention_backward_kernel, per),
        grid_spec=pltpu.PrefetchScalarGridSpec(
            num_scalar_prefetch=1,
            grid=(heads // per,),
            in_specs=[resident((seq, width), place) for place in (0, 1, 2, 0, 0)]
            + [pl.BlockSpec((per, 8, seq), lambda step, *_: (step, 0, 0))],
            out_specs=resident((seq, 3 * width)),
            scratch_shapes=[
                pltpu.VMEM((-(-heads // 16) * 16, seq), F32),
                pltpu.VMEM((per, seq, WINDOW), F32),
            ],
        ),
        out_shape=jax.ShapeDtypeStruct((seq, 3 * width), BF16),
        compiler_params=pltpu.CompilerParams(vmem_limit_bytes=40 << 20),
        cost_estimate=cost(7 * heads * seq * seq * WINDOW),
        name="attention_backward",
    )(length, qkv, qkv, qkv, attended, grad_attended, lse)


def once(shape):
    return pl.BlockSpec(shape, lambda step, *_: (0, 0), pipeline_mode=pl.Buffered(1))


def in_vmem():
    return pl.BlockSpec(memory_space=pltpu.VMEM)


def lane_tiles(rows, tile):
    return pl.BlockSpec((rows, tile), lambda step, *_: (0, step))


def row_tiles(tile, columns):
    return pl.BlockSpec((tile, columns), lambda step, *_: (step, 0))


def spread_store(rows_ref, scratch_ref, value, chips, lanes):
    depth = value.shape[0]
    rows = depth // chips
    padded = rows_ref.shape[0] // chips
    scratch_ref[:depth] = value
    for pair in range(chips // 2):
        first = 2 * pair * rows
        both = jnp.concatenate(
            [
                scratch_ref[first : first + padded],
                scratch_ref[first + rows : first + rows + padded],
            ],
            axis=0,
        )
        rows_ref[2 * pair * padded : 2 * (pair + 1) * padded, lanes] = both.astype(BF16)


def norm_down(value, gain, bias):
    centred = value - jnp.mean(value, axis=0, keepdims=True)
    inverse = lax.rsqrt(jnp.mean(centred * centred, axis=0, keepdims=True) + EPSILON)
    return centred * inverse * gain + bias


def half_of(core_ref, mine_ref, other_ref, lanes):
    return jnp.where(pl.program_id(0) == core_ref[0], mine_ref[0, :, lanes], other_ref[:, lanes])


def valid_lanes(len_ref, half, lanes):
    lane = lax.broadcasted_iota(jnp.int32, (1, TILE), 1) + pl.program_id(0) * half + lanes.start
    return lane < len_ref[0]


def sub_tiles(half):
    return [slice(first, first + TILE) for first in range(0, half, TILE)]


def half_specs(depth, half):
    return [
        pl.BlockSpec((1, depth, half), lambda step, core, *_: (core[0], 0, 0), pipeline_mode=pl.Buffered(1)),
        once((depth, half)),
    ]


def widen_kernel(spans, w_ref, *wide_refs):
    rows, depth = w_ref.shape[0], w_ref.shape[1] // 3
    for wide_ref, (first, size) in zip(wide_refs, spans):
        width = wide_ref.shape[1] // 3
        for part in range(3):
            begin = part * depth + first
            piece = w_ref[:, begin : begin + size]
            if size < width:
                piece = jnp.concatenate([piece, jnp.zeros((rows, width - size), BF16)], axis=1)
            wide_ref[:, part * width : (part + 1) * width] = piece


def widen(w, spans, widths, steps=5):
    depth, columns = w.shape
    tile = depth // steps
    return pl.pallas_call(
        functools.partial(widen_kernel, spans),
        grid=(steps,),
        in_specs=[row_tiles(tile, columns)],
        out_specs=[row_tiles(tile, width) for width in widths],
        out_shape=[jax.ShapeDtypeStruct((depth, width), BF16) for width in widths],
        compiler_params=pltpu.CompilerParams(vmem_limit_bytes=16 << 20),
        cost_estimate=cost(3000000000),
        name="widen",
    )(w)


def project_kernel(
    chips, core_ref, mine_ref, other_ref, norm_ref, first_w_ref, second_w_ref, first_ref, second_ref, rows_ref, scratch_ref
):
    half = other_ref.shape[1]

    @pl.when(pl.program_id(0) == 0)
    def _():
        scratch_ref[...] = jnp.zeros_like(scratch_ref)

    columns = jnp.transpose(norm_ref[...])

    def begin(lanes):
        value = half_of(core_ref, mine_ref, other_ref, lanes).astype(F32)
        normed = norm_down(value, columns[:, 0:1], columns[:, 1:2])
        spread_store(rows_ref, scratch_ref.at[lanes.start // TILE], normed, chips, lanes)
        return (jnp.transpose(normed.astype(BF16)),)

    def middle(lanes, left):
        first_ref[lanes] = dot(left, first_w_ref[...]).astype(BF16)
        second_ref[lanes] = dot(left, second_w_ref[...]).astype(BF16)
        return ()

    staggered(sub_tiles(half), begin, middle, lambda lanes: None)


def project(core, turned, other, norms, wides, chips, rows_pad):
    _, depth, half = turned.shape
    widths = [wide.shape[1] for wide in wides]
    return pl.pallas_call(
        functools.partial(project_kernel, chips),
        grid_spec=pltpu.PrefetchScalarGridSpec(
            num_scalar_prefetch=1,
            grid=(2,),
            in_specs=half_specs(depth, half) + [once(norms.shape)] + [once(wide.shape) for wide in wides],
            out_specs=[row_tiles(half, width) for width in widths] + [lane_tiles(chips * rows_pad, half)],
            scratch_shapes=[pltpu.VMEM((half // TILE, depth + 8, TILE), F32)],
        ),
        out_shape=[jax.ShapeDtypeStruct((2 * half, width), BF16) for width in widths]
        + [jax.ShapeDtypeStruct((chips * rows_pad, 2 * half), BF16)],
        compiler_params=pltpu.CompilerParams(vmem_limit_bytes=40 << 20),
        cost_estimate=cost(2 * 2 * half * depth * sum(widths)),
        name="project",
    )(core, turned, other, norms, *wides)


def hand_over_kernel(core_ref, first_ref, second_ref, first_out, second_out):
    first_out[...] = first_ref[0]
    second_out[...] = second_ref[0]


def hand_over(core, first, second):
    _, depth, half = first.shape
    tile = half // 2
    taken = pl.BlockSpec((1, depth, tile), lambda step, core: (1 - core[0], 0, step))
    return pl.pallas_call(
        hand_over_kernel,
        grid_spec=pltpu.PrefetchScalarGridSpec(
            num_scalar_prefetch=1,
            grid=(2,),
            in_specs=[taken, taken],
            out_specs=[lane_tiles(depth, tile)] * 2,
        ),
        out_shape=[jax.ShapeDtypeStruct((depth, half), BF16)] * 2,
        name="hand_over",
    )(core, first, second)


def take_over_kernel(core_ref, got_ref, whole_ref, out_ref):
    out_ref[0] = got_ref[...]


def take_over(core, whole, got):
    depth, half = got.shape
    tile = half // 2
    return pl.pallas_call(
        take_over_kernel,
        grid_spec=pltpu.PrefetchScalarGridSpec(
            num_scalar_prefetch=1,
            grid=(2,),
            in_specs=[lane_tiles(depth, tile), pl.BlockSpec(memory_space=pl.ANY)],
            out_specs=pl.BlockSpec((1, depth, tile), lambda step, core: (1 - core[0], 0, step)),
        ),
        out_shape=jax.ShapeDtypeStruct(whole.shape, BF16),
        input_output_aliases={2: 0},
        name="take_over",
    )(core, got, whole)


def hidden_kernel(
    chips,
    core_ref,
    len_ref,
    mine_ref,
    other_ref,
    mine_grad_ref,
    other_grad_ref,
    first_ref,
    second_ref,
    w_ref,
    norm_ref,
    hidden_ref,
    normed_ref,
    grad_ref,
    rows_ref,
    o_rows_ref,
    w_turned_ref,
    scratch_ref,
):
    depth = w_ref.shape[0]
    half = other_ref.shape[1]

    @pl.when(pl.program_id(0) == 0)
    def _():
        scratch_ref[...] = jnp.zeros_like(scratch_ref)
        w_turned_ref[...] = jnp.transpose(w_ref[...])

    columns = jnp.transpose(norm_ref[...])

    def begin(lanes):
        attended = jnp.concatenate([first_ref[lanes], second_ref[lanes]], axis=1)
        value = half_of(core_ref, mine_ref, other_ref, lanes).astype(F32)
        hidden = value + dot(w_turned_ref[...], attended[:, :depth], NT)
        turned = jnp.transpose(attended).astype(F32)[:depth]
        spread_store(o_rows_ref, scratch_ref.at[2 * (lanes.start // TILE)], turned, chips, lanes)
        return (hidden,)

    def middle(lanes, hidden):
        hidden_ref[:, lanes] = hidden
        grad = half_of(core_ref, mine_grad_ref, other_grad_ref, lanes)
        grad = jnp.where(valid_lanes(len_ref, half, lanes), grad, jnp.zeros((), BF16))
        grad_ref[lanes, :depth] = jnp.transpose(grad)
        grad_ref[lanes, depth:] = jnp.zeros((TILE, grad_ref.shape[1] - depth), BF16)
        normed = norm_down(hidden, columns[:, 2:3], columns[:, 3:4])
        spread_store(rows_ref, scratch_ref.at[2 * (lanes.start // TILE) + 1], normed, chips, lanes)
        normed_ref[lanes] = jnp.transpose(normed.astype(BF16))
        return ()

    staggered(sub_tiles(half), begin, middle, lambda lanes: None)


def hidden_state(core, length, cell, grad_cell, attended, w_out, norms, chips, rows_pad):
    _, depth, half = cell[0].shape
    seq = 2 * half
    spread = jax.ShapeDtypeStruct((chips * rows_pad, seq), BF16)
    return pl.pallas_call(
        functools.partial(hidden_kernel, chips),
        grid_spec=pltpu.PrefetchScalarGridSpec(
            num_scalar_prefetch=2,
            grid=(2,),
            in_specs=half_specs(depth, half) * 2
            + [row_tiles(half, part.shape[1]) for part in attended]
            + [once(w_out.shape), once(norms.shape)],
            out_specs=[lane_tiles(depth, half), row_tiles(half, depth), row_tiles(half, WIDTH)]
            + [lane_tiles(chips * rows_pad, half)] * 2,
            scratch_shapes=[
                pltpu.VMEM((depth, depth), BF16),
                pltpu.VMEM((2 * half // TILE, depth + 8, TILE), F32),
            ],
        ),
        out_shape=[
            jax.ShapeDtypeStruct((depth, seq), F32),
            jax.ShapeDtypeStruct((seq, depth), BF16),
            jax.ShapeDtypeStruct((seq, WIDTH), BF16),
            spread,
            spread,
        ],
        compiler_params=pltpu.CompilerParams(vmem_limit_bytes=40 << 20),
        cost_estimate=cost(5 * seq * depth * depth),
        name="hidden_state",
    )(core, length, *cell, *grad_cell, *attended, w_out, norms)


GELU = (2.0 / math.pi) ** 0.5


def hidden_units_kernel(
    tile, normed_ref, grad_ref, up_ref, down_ref, activated_ref, grad_upward_ref
):
    seq, depth = normed_ref.shape

    def begin(first):
        rows = slice(first, first + tile)
        return dot(normed_ref[rows], up_ref[...]), dot(grad_ref[rows, :depth], down_ref[...])

    def middle(first, upward, grad_activated):
        rows = slice(first, first + tile)
        square = upward * upward
        gate = 0.5 * jnp.tanh(upward * (GELU + (GELU * 0.044715) * square)) + 0.5
        activated = upward * gate
        slope = gate + 2.0 * activated * (1.0 - gate) * (GELU + (3 * GELU * 0.044715) * square)
        activated_ref[:, rows] = jnp.transpose(activated.astype(BF16))
        grad_upward_ref[rows] = (grad_activated * slope).astype(BF16)
        return ()

    staggered(list(range(0, seq, tile)), begin, middle, lambda first: None)


def hidden_units(normed, grad, w_up, w_down_turned, tile=512, rows=256):
    seq, depth = normed.shape
    units = w_up.shape[1]
    return pl.pallas_call(
        functools.partial(hidden_units_kernel, rows),
        grid=(pl.cdiv(units, tile),),
        in_specs=[once(normed.shape), once(grad.shape)] + [lane_tiles(depth, tile)] * 2,
        out_specs=[row_tiles(tile, seq), lane_tiles(seq, tile)],
        out_shape=[
            jax.ShapeDtypeStruct((units, seq), BF16),
            jax.ShapeDtypeStruct((seq, units), BF16),
        ],
        compiler_params=pltpu.CompilerParams(vmem_limit_bytes=56 << 20),
        cost_estimate=cost(4 * seq * depth * units),
        name="hidden_units",
    )(normed, grad, w_up, w_down_turned)


def norm_down_back(grad_in, value, gain, gain_ref, bias_ref):
    centred = value - jnp.mean(value, axis=0, keepdims=True)
    inverse = lax.rsqrt(jnp.mean(centred * centred, axis=0, keepdims=True) + EPSILON)
    normed = centred * inverse
    product = grad_in * normed
    tiles = [slice(first, first + LANES) for first in range(0, value.shape[1], LANES)]
    gain_ref[...] += sum(product[:, lanes] for lanes in tiles)
    bias_ref[...] += sum(grad_in[:, lanes] for lanes in tiles)
    scaled = grad_in * gain
    return inverse * (
        scaled
        - jnp.mean(scaled, axis=0, keepdims=True)
        - normed * jnp.mean(product * gain, axis=0, keepdims=True)
    )


def lane_sums(rows_ref, first, *refs):
    @pl.when(pl.program_id(0) == pl.num_programs(0) - 1)
    def _():
        for place, ref in enumerate(refs):
            row = jnp.sum(jnp.transpose(ref[...]), axis=0, keepdims=True)
            rows_ref[first + place : first + place + 1, :] = row


def clear_first(*refs):
    @pl.when(pl.program_id(0) == 0)
    def _():
        for ref in refs:
            ref[...] = jnp.zeros_like(ref)


def hidden_grad_kernel(
    core_ref,
    len_ref,
    grad_up_ref,
    w_up_ref,
    hidden_ref,
    mine_grad_ref,
    other_grad_ref,
    w_ref,
    norm_ref,
    grad_hidden_ref,
    branch_ref,
    first_ref,
    second_ref,
    sums_ref,
    gain_ref,
    bias_ref,
):
    clear_first(gain_ref, bias_ref, sums_ref)
    depth, half = hidden_ref.shape
    width = first_ref.shape[1]
    columns = jnp.transpose(norm_ref[...])

    def begin(lanes):
        return (dot(w_up_ref[...], grad_up_ref[lanes], NT),)

    def middle(lanes, grad_normed):
        grad = half_of(core_ref, mine_grad_ref, other_grad_ref, lanes)
        grad = jnp.where(valid_lanes(len_ref, half, lanes), grad, jnp.zeros((), BF16)).astype(F32)
        grad = grad + norm_down_back(grad_normed, hidden_ref[:, lanes], columns[:, 2:3], gain_ref, bias_ref)
        grad_hidden_ref[:, lanes] = grad
        branch = jnp.transpose(grad.astype(BF16))
        branch_ref[lanes, :depth] = branch
        branch_ref[lanes, depth:] = jnp.zeros((TILE, branch_ref.shape[1] - depth), BF16)
        return (branch,)

    def end(lanes, branch):
        first_ref[lanes] = dot(branch, w_ref[:width], NT).astype(BF16)
        second_ref[lanes, : depth - width] = dot(branch, w_ref[width:], NT).astype(BF16)
        second_ref[lanes, depth - width :] = jnp.zeros((TILE, second_ref.shape[1] - depth + width), BF16)

    staggered(sub_tiles(half), begin, middle, end)
    lane_sums(sums_ref, 2, gain_ref, bias_ref)


def hidden_grad(core, length, grad_upward, w_up, hidden, grad_cell, w_out, norms, widths):
    depth, seq = hidden.shape
    half = seq // 2
    units = w_up.shape[1]
    return pl.pallas_call(
        hidden_grad_kernel,
        grid_spec=pltpu.PrefetchScalarGridSpec(
            num_scalar_prefetch=2,
            grid=(2,),
            in_specs=[row_tiles(half, units), in_vmem(), lane_tiles(depth, half)]
            + half_specs(depth, half)
            + [once(w_out.shape), once(norms.shape)],
            out_specs=[lane_tiles(depth, half), row_tiles(half, WIDTH)]
            + [row_tiles(half, width) for width in widths]
            + [once((8, depth))],
            scratch_shapes=[pltpu.VMEM((depth, LANES), F32)] * 2,
        ),
        out_shape=[
            jax.ShapeDtypeStruct((depth, seq), F32),
            jax.ShapeDtypeStruct((seq, WIDTH), BF16),
        ]
        + [jax.ShapeDtypeStruct((seq, width), BF16) for width in widths]
        + [jax.ShapeDtypeStruct((8, depth), F32)],
        compiler_params=pltpu.CompilerParams(vmem_limit_bytes=40 << 20),
        cost_estimate=cost(2 * seq * depth * (units + 2 * depth)),
        name="hidden_grad",
    )(core, length, grad_upward, w_up, hidden, *grad_cell, w_out, norms)


def half_place(step, core):
    return jnp.where(step == 0, 1 - core, core)


def tokens_grad_kernel(
    core_ref,
    first_ref,
    second_ref,
    wide_first_ref,
    wide_second_ref,
    mine_ref,
    other_ref,
    grad_hidden_ref,
    norm_ref,
    earlier_ref,
    sent_ref,
    kept_ref,
    sums_ref,
    gain_ref,
    bias_ref,
):
    clear_first(gain_ref, bias_ref)
    sums_ref[...] = earlier_ref[...]
    step = pl.program_id(0)
    columns = jnp.transpose(norm_ref[...])

    def begin(lanes):
        grad = dot(wide_first_ref[...], first_ref[lanes], NT)
        return (grad + dot(wide_second_ref[...], second_ref[lanes], NT),)

    def middle(lanes, grad_normed):
        value = jnp.where(step == 0, other_ref[:, lanes], mine_ref[0, :, lanes]).astype(F32)
        grad = norm_down_back(grad_normed, value, columns[:, 0:1], gain_ref, bias_ref)
        grad = (grad_hidden_ref[:, lanes] + grad).astype(BF16)

        @pl.when(step == 0)
        def _():
            sent_ref[:, lanes] = grad

        @pl.when(step == 1)
        def _():
            kept_ref[0, :, lanes] = grad

        return ()

    staggered(sub_tiles(other_ref.shape[1]), begin, middle, lambda lanes: None)
    lane_sums(sums_ref, 0, gain_ref, bias_ref)


def tokens_gradient(core, grads, wides, cell, grad_hidden, norms, sums):
    depth, seq = grad_hidden.shape
    half = seq // 2
    return pl.pallas_call(
        tokens_grad_kernel,
        grid_spec=pltpu.PrefetchScalarGridSpec(
            num_scalar_prefetch=1,
            grid=(2,),
            in_specs=[
                pl.BlockSpec((half, part.shape[1]), lambda step, core: (half_place(step, core[0]), 0))
                for part in grads
            ]
            + [in_vmem() for part in wides]
            + half_specs(depth, half)
            + [
                pl.BlockSpec((depth, half), lambda step, core: (0, half_place(step, core[0]))),
                once(norms.shape),
                once(sums.shape),
            ],
            out_specs=[
                once((depth, half)),
                pl.BlockSpec((1, depth, half), lambda step, core: (core[0], 0, 0), pipeline_mode=pl.Buffered(1)),
                once(sums.shape),
            ],
            scratch_shapes=[pltpu.VMEM((depth, LANES), F32)] * 2,
        ),
        out_shape=[
            jax.ShapeDtypeStruct((depth, half), BF16),
            jax.ShapeDtypeStruct((2, depth, half), BF16),
            jax.ShapeDtypeStruct(sums.shape, F32),
        ],
        compiler_params=pltpu.CompilerParams(vmem_limit_bytes=34 << 20),
        cost_estimate=cost(7 * seq * depth * WIDTH),
        name="tokens_gradient",
    )(core, *grads, *wides, *cell, grad_hidden, norms, sums)


def mixed_sent_kernel(core_ref, activated_ref, w_ref, hidden_ref, out_ref):
    out_ref[...] = (hidden_ref[...] + dot(w_ref[...], activated_ref[...])).astype(BF16)


def mixed_kept_kernel(core_ref, activated_ref, w_ref, hidden_ref, out_ref):
    out_ref[0] = (hidden_ref[...] + dot(w_ref[...], activated_ref[...])).astype(BF16)


def mixed_half(core, activated, w_down_turned, hidden, sent):
    depth, seq = hidden.shape
    units = activated.shape[0]
    tile = seq // 4

    def place(step, core):
        return 0, (2 - 2 * core[0] if sent else 2 * core[0]) + step

    if sent:
        out_spec = lane_tiles(depth, tile)
        out_shape = jax.ShapeDtypeStruct((depth, seq // 2), BF16)
    else:
        out_spec = pl.BlockSpec((1, depth, tile), lambda step, core: (core[0], 0, step))
        out_shape = jax.ShapeDtypeStruct((2, depth, seq // 2), BF16)
    return pl.pallas_call(
        mixed_sent_kernel if sent else mixed_kept_kernel,
        grid_spec=pltpu.PrefetchScalarGridSpec(
            num_scalar_prefetch=1,
            grid=(2,),
            in_specs=[
                pl.BlockSpec((units, tile), place),
                in_vmem(),
                pl.BlockSpec((depth, tile), place),
            ],
            out_specs=out_spec,
        ),
        out_shape=out_shape,
        compiler_params=pltpu.CompilerParams(vmem_limit_bytes=20 << 20),
        cost_estimate=cost(seq * depth * units),
        name="mixed_half",
    )(core, activated, w_down_turned, hidden)


def swap_cores(value):
    return lax.ppermute(value, "blk", [(0, 1), (1, 0)])


def swap_chips(value, bit):
    count = lax.axis_size("cells")
    return lax.ppermute(value, "cells", [(place, place ^ bit) for place in range(count)])


def begin_with(chain, *scatters):
    sends = [item.send() for item in scatters]
    flat = [value for group in sends for value in group]
    chain, *flat = lax.optimization_barrier((chain, *flat))
    for item, group in zip(scatters, sends):
        item.move(flat[: len(group)])
        flat = flat[len(group) :]
    return chain


def finish_with(chain, *scatters):
    groups = [item.got for item in scatters]
    flat = [value for group in groups for value in group]
    chain, *flat = lax.optimization_barrier((chain, *flat))
    for item, group in zip(scatters, groups):
        item.arrived(flat[: len(group)])
        flat = flat[len(group) :]
    return chain


class AllSum:
    def __init__(self, value):
        self.value = value
        self.stage = 0
        self.got = None

    def send(self):
        if self.got is not None:
            self.value = self.value + self.got[0]
        return [self.value]

    def move(self, sent):
        self.got = [swap_chips(sent[0], 1 << self.stage)]
        self.stage += 1
        return self.got

    def arrived(self, got):
        self.got = list(got)

    def result(self):
        return self.value + self.got[0]


def stage_order(bits, second):
    return ([2, 0, 1] if second else [0, 1, 2]) + list(range(3, bits))


def block_mask(index, order):
    bits = len(order)
    return sum(((index >> (bits - 1 - stage)) & 1) << bit for stage, bit in enumerate(order))


def cut_rows(rows):
    return rows - rows // 16 * 8


def columns_sent_kernel(per, scalar_ref, left_ref, *refs):
    right = refs[0][...] if per == 1 else jnp.concatenate([ref[...] for ref in refs[:per]], axis=1)
    refs[-1][...] = dot(left_ref[...], right).astype(BF16)


def columns_kept_kernel(per, chips, scalar_ref, left_ref, *refs):
    right = refs[0][...] if per == 1 else jnp.concatenate([ref[...] for ref in refs[:per]], axis=1)
    got_ref, scratch_ref = refs[per], refs[-1]
    outs = refs[-5:-1]
    bits = chips.bit_length() - 1
    scratch_ref[...] = dot(left_ref[...], right) + got_ref[...].astype(F32)
    rows = left_ref.shape[0] // chips
    cut = cut_rows(rows)
    for part, (first, size) in enumerate(((0, cut), (cut, rows - cut))):
        order = stage_order(bits, part == 1)
        for index in range(chips):
            block = jnp.bitwise_xor(scalar_ref[1], block_mask(index, order))
            row = pl.multiple_of(block * rows, 8) + first
            value = scratch_ref[pl.ds(pl.multiple_of(row, 8), size), :].astype(BF16)
            outs[2 * part + index // (chips // 2)][index % (chips // 2)] = value


def column_specs(per, depth, tiles):
    return [
        pl.BlockSpec((depth, LANES), functools.partial(column_place, per, extra))
        for extra in range(per)
    ]


def column_place(per, extra, step, scalar):
    return 0, scalar[0] + per * step + extra


def columns_sent(left, right, first, place, tiles, per):
    depth, seq = left.shape
    return pl.pallas_call(
        functools.partial(columns_sent_kernel, per),
        grid_spec=pltpu.PrefetchScalarGridSpec(
            num_scalar_prefetch=1,
            grid=(tiles // per,),
            in_specs=[in_vmem()] + column_specs(per, seq, tiles),
            out_specs=lane_tiles(depth, per * LANES),
        ),
        out_shape=jax.ShapeDtypeStruct((depth, tiles * LANES), BF16),
        compiler_params=pltpu.CompilerParams(vmem_limit_bytes=24 << 20),
        cost_estimate=cost(2 * depth * seq * tiles * LANES),
        name="columns_sent",
    )(jnp.stack([first, place]), left, *[right] * per)


def columns_kept(left, right, got, first, place, chips, per, width, begin=0, into=None):
    depth, seq = left.shape
    tiles = got.shape[1] // LANES
    rows = depth // chips
    cut = cut_rows(rows)
    sizes = (cut, cut, rows - cut, rows - cut)
    shift = begin // per
    extra = [] if into is None else list(into)
    count = 3 + per
    return pl.pallas_call(
        functools.partial(columns_kept_kernel, per, chips),
        grid_spec=pltpu.PrefetchScalarGridSpec(
            num_scalar_prefetch=1,
            grid=(tiles // per,),
            in_specs=[in_vmem()]
            + column_specs(per, seq, tiles)
            + [lane_tiles(depth, per * LANES)]
            + [pl.BlockSpec(memory_space=pl.ANY)] * len(extra),
            out_specs=[
                pl.BlockSpec((chips // 2, size, per * LANES), lambda step, *_: (0, 0, step + shift))
                for size in sizes
            ],
            scratch_shapes=[pltpu.VMEM((depth, per * LANES), F32)],
        ),
        out_shape=[jax.ShapeDtypeStruct((chips // 2, size, width), BF16) for size in sizes],
        input_output_aliases={count + index: index for index in range(len(extra))},
        compiler_params=pltpu.CompilerParams(vmem_limit_bytes=32 << 20),
        cost_estimate=cost(2 * depth * seq * tiles * LANES),
        name="columns_kept",
    )(jnp.stack([first, place]), left, *[right] * per, got, *extra)


def rows_sent_kernel(window, scalar_ref, left_ref, right_ref, out_ref):
    lanes = pl.ds(pl.multiple_of(scalar_ref[0] * LANES, LANES), window)
    out_ref[...] = dot(left_ref[...], right_ref[:, lanes]).astype(BF16)


def rows_sent(left, right, first, place, window, per):
    depth, seq = left.shape
    tile = depth // per
    return pl.pallas_call(
        functools.partial(rows_sent_kernel, window),
        grid_spec=pltpu.PrefetchScalarGridSpec(
            num_scalar_prefetch=1,
            grid=(per,),
            in_specs=[row_tiles(tile, seq), once(right.shape)],
            out_specs=row_tiles(tile, window),
        ),
        out_shape=jax.ShapeDtypeStruct((depth, window), BF16),
        compiler_params=pltpu.CompilerParams(vmem_limit_bytes=48 << 20),
        cost_estimate=cost(3 * depth * seq * window),
        name="rows_sent",
    )(jnp.stack([first, place]), left, right)


def rows_kept_kernel(window, chips, scalar_ref, left_ref, right_ref, got_ref, *outs):
    lanes = pl.ds(pl.multiple_of(scalar_ref[0] * LANES, LANES), window)
    value = dot(left_ref[...], right_ref[:, lanes]) + got_ref[...].astype(F32)
    bits = chips.bit_length() - 1
    blocks = chips // pl.num_programs(0) if False else value.shape[0] // (outs[0].shape[1] + outs[2].shape[1])
    rows = value.shape[0] // blocks
    cut = cut_rows(rows)
    for slot in range(blocks):
        away = jnp.bitwise_xor(scalar_ref[1], pl.program_id(0) * blocks + slot)
        for part, (first, size) in enumerate(((0, cut), (cut, rows - cut))):
            order = stage_order(bits, part == 1)
            index = sum(((away >> bit) & 1) << (bits - 1 - stage) for stage, bit in enumerate(order))
            begin = slot * rows + first
            piece = value[begin : begin + size].astype(BF16)

            @pl.when(index < chips // 2)
            def _(piece=piece, index=index, part=part):
                outs[2 * part][index] = piece

            @pl.when(index >= chips // 2)
            def _(piece=piece, index=index, part=part):
                outs[2 * part + 1][index - chips // 2] = piece


def rows_kept(left, right, got, first, place, chips, per):
    depth, seq = left.shape
    window = got.shape[1]
    tile = depth // per
    rows = depth // chips
    cut = cut_rows(rows)
    sizes = (cut, cut, rows - cut, rows - cut)
    return pl.pallas_call(
        functools.partial(rows_kept_kernel, window, chips),
        grid_spec=pltpu.PrefetchScalarGridSpec(
            num_scalar_prefetch=1,
            grid=(per,),
            in_specs=[row_tiles(tile, seq), once(right.shape), row_tiles(tile, window)],
            out_specs=[
                pl.BlockSpec(
                    (chips // 2, size, window),
                    lambda step, *_: (0, 0, 0),
                    pipeline_mode=pl.Buffered(1),
                )
                for size in sizes
            ],
        ),
        out_shape=[jax.ShapeDtypeStruct((chips // 2, size, window), BF16) for size in sizes],
        compiler_params=pltpu.CompilerParams(vmem_limit_bytes=48 << 20),
        cost_estimate=cost(3 * depth * seq * window),
        name="rows_kept",
    )(jnp.stack([first, place]), left, right, got)


def halve_kernel(count, *refs):
    ins, outs = refs[: 4 * count], refs[4 * count :]
    kept, sent = [], []
    for part in range(count):
        near, far, near_got, far_got = ins[4 * part : 4 * part + 4]
        kept.append(near[...].astype(F32) + near_got[...].astype(F32))
        sent.append(far[...].astype(F32) + far_got[...].astype(F32))
    if len(outs) < 2 * count:
        kept, sent = [jnp.concatenate(kept, axis=1)], [jnp.concatenate(sent, axis=1)]
    for part, (one, other) in enumerate(zip(kept, sent)):
        outs[2 * part][...] = one.astype(BF16)
        outs[2 * part + 1][...] = other.astype(BF16)


def halve(kept, got, join):
    half = kept[0].shape[0] // 2
    in_specs, operands = [], []
    for own, other in zip(kept, got):
        block = (1,) + own.shape[1:]
        near = pl.BlockSpec(block, lambda step: (step, 0, 0))
        far = pl.BlockSpec(block, lambda step: (step + half, 0, 0))
        in_specs += [near, far, near, far]
        operands += [own, own, other, other]
    rows = [own.shape[1] for own in kept]
    rows = [sum(rows)] if join else rows
    width = kept[0].shape[2]
    return pl.pallas_call(
        functools.partial(halve_kernel, len(kept)),
        grid=(half,),
        in_specs=in_specs,
        out_specs=[pl.BlockSpec((1, size, width), lambda step: (step, 0, 0)) for size in rows for _ in range(2)],
        out_shape=[jax.ShapeDtypeStruct((half, size, width), BF16) for size in rows for _ in range(2)],
        compiler_params=pltpu.CompilerParams(vmem_limit_bytes=16 << 20),
        cost_estimate=cost(1000 * 1000000),
        name="halve",
    )(*operands)


class Scatter:
    def __init__(self, first_kept, first_sent, second_kept, second_sent):
        self.bits = lax.axis_size("cells").bit_length() - 1
        self.kept = [first_kept, second_kept]
        self.next = [first_sent, second_sent]
        self.stage = 0
        self.got = None

    def send(self):
        if self.got is not None:
            out = halve(self.kept, self.got, self.stage == 3)
            self.kept, self.next = list(out[0::2]), list(out[1::2])
        return self.next

    def move(self, sent):
        orders = [stage_order(self.bits, part == 1) for part in range(len(sent))]
        self.got = [swap_chips(value, 1 << order[self.stage]) for value, order in zip(sent, orders)]
        self.stage += 1
        return self.got

    def arrived(self, got):
        self.got = list(got)

    def result(self):
        return self.kept[0][0].astype(F32) + self.got[0][0].astype(F32)


def cell_split(
    tokens, lengths, attn_gain, attn_bias, w_qkv, w_out, mlp_gain, mlp_bias, w_up, w_down, cotangent
):
    row_count = tokens.shape[0]
    seq = 2 * row_count
    core = lax.axis_index("blk")
    chips = lax.axis_size("cells")
    rows = D // chips
    rows_pad = -(-rows // 8) * 8

    def tie(*values):
        return lax.optimization_barrier(values)

    def pick(first, second):
        return jnp.where(core == 0, first, second)

    core_index = core.reshape(1).astype(jnp.int32)
    length = pick(lengths[0], lengths[1])
    length = length.reshape(1)
    turned, turned_cotangent = tokens.transpose(1, 2, 0), cotangent.transpose(1, 2, 0)
    sent, sent_cotangent = hand_over(core_index, turned, turned_cotangent)
    cell = (turned, swap_cores(sent))
    grad_cell = (turned_cotangent, swap_cores(sent_cotangent))
    norms = jnp.stack([attn_gain, attn_bias, mlp_gain, mlp_bias] * 2)
    w_down_turned = w_down.T

    big, small = 16, HEADS - 16
    spans = ((0, big * HD), (big * HD, small * HD))
    widths = [3 * (-(-size // LANES) * LANES) for _, size in spans]
    wide_big, wide_small = widen(w_qkv, spans, widths)
    qkv_big, qkv_small, one_rows = project(
        core_index, *cell, norms, (wide_big, wide_small), chips, rows_pad
    )
    attended_big, lse_big = attention_forward(qkv_big, length, big)
    attended_small, lse_small = attention_forward(qkv_small, length, small)
    hidden, normed_mlp, grad_low, mlp_rows, attended_rows = hidden_state(
        core_index, length, cell, grad_cell, (attended_big, attended_small), w_out, norms, chips, rows_pad
    )
    activated, grad_upward = hidden_units(normed_mlp, grad_low, w_up, w_down_turned)

    half = D // 2
    window = -(-half // LANES) * LANES
    starts = (0, WIDTH - window)
    ours, theirs = pick(*starts), pick(*starts[::-1])
    up_all = w_up.shape[1]
    up_window = -(-up_all // 2 // LANES) * LANES
    up_starts = (0, up_all - up_window)
    up_ours, up_theirs = pick(*up_starts), pick(*up_starts[::-1])
    big_width, small_width = qkv_big.shape[1] // 3, qkv_small.shape[1] // 3
    big_window = big_width + -(-half // LANES) * LANES
    big_starts = (0, 3 * big_width - big_window)
    big_ours, big_theirs = pick(*big_starts), pick(*big_starts[::-1])
    small_window = 2 * small_width
    small_starts = (0, small_width)
    small_ours, small_theirs = pick(*small_starts), pick(*small_starts[::-1])

    place = lax.axis_index("cells").astype(jnp.int32)

    def tiles(first):
        return (first // LANES).astype(jnp.int32)

    ours, theirs, up_ours, up_theirs = tiles(ours), tiles(theirs), tiles(up_ours), tiles(up_theirs)
    big_ours, big_theirs, small_ours, small_theirs = map(
        tiles, (big_ours, big_theirs, small_ours, small_theirs)
    )
    up_count, out_count = up_window // LANES, 6
    out_starts = (0, WIDTH - out_count * LANES)
    out_ours, out_theirs = tiles(pick(*out_starts)), tiles(pick(*out_starts[::-1]))
    down_steps = chips // 4

    down_sent = rows_sent(activated, grad_low, theirs, place, window, down_steps)
    down_got = swap_cores(down_sent)
    mlp_rows, down_sent = tie(mlp_rows, down_sent)
    up_sent = columns_sent(mlp_rows, grad_upward, up_theirs, place, up_count, 6)
    up_got = swap_cores(up_sent)
    activated, up_sent = tie(activated, up_sent)
    down = Scatter(*rows_kept(activated, grad_low, down_got, ours, place, chips, down_steps))
    mlp_rows = begin_with(mlp_rows, down)
    up_parts = columns_kept(
        mlp_rows, grad_upward, up_got, up_ours, place, chips, 6, up_window + out_count * LANES
    )
    grad_upward, *up_parts = tie(grad_upward, *up_parts)
    grad_hidden, grad_branch, grad_attended_big, grad_attended_small, sums = hidden_grad(
        core_index, length, grad_upward, w_up, hidden, grad_cell, w_out, norms, (big_width, small_width)
    )
    out_sent = columns_sent(attended_rows, grad_branch, out_theirs, place, out_count, out_count)
    out_got = swap_cores(out_sent)
    grad_attended_small, out_sent = tie(grad_attended_small, out_sent)
    grad_attended_small = finish_with(grad_attended_small, down)
    grad_attended_small = begin_with(grad_attended_small, down)
    grad_small = attention_backward(
        qkv_small, attended_small, grad_attended_small, lse_small, length
    )
    small_sent = columns_sent(one_rows, grad_small, small_theirs, place, small_window // LANES, 4)
    small_got = swap_cores(small_sent)
    out_got, small_sent = tie(out_got, small_sent)
    up = Scatter(
        *columns_kept(
            attended_rows,
            grad_branch,
            out_got,
            out_ours,
            place,
            chips,
            out_count,
            up_window + out_count * LANES,
            up_count,
            up_parts,
        )
    )
    grad_attended_big = finish_with(grad_attended_big, down)
    grad_attended_big = begin_with(grad_attended_big, up, down)
    grad_attended_big, small_got = tie(grad_attended_big, small_got)
    grad_big = attention_backward(qkv_big, attended_big, grad_attended_big, lse_big, length)
    grad_big = finish_with(grad_big, up, down)
    grad_big = begin_with(grad_big, up, down)
    big_sent = columns_sent(one_rows, grad_big, big_theirs, place, big_window // LANES, 6)
    big_got = swap_cores(big_sent)
    grad_small, big_sent = tie(grad_small, big_sent)
    qkv_parts = columns_kept(
        one_rows,
        grad_small,
        small_got,
        small_ours,
        place,
        chips,
        4,
        big_window + small_window,
        big_window // LANES,
    )
    big_got, *qkv_parts = tie(big_got, *qkv_parts)
    whole = Scatter(
        *columns_kept(
            one_rows,
            grad_big,
            big_got,
            big_ours,
            place,
            chips,
            6,
            big_window + small_window,
            0,
            qkv_parts,
        )
    )
    grad_big, grad_small = begin_with((grad_big, grad_small), whole)
    tokens_sent, tokens_kept, sums = tokens_gradient(
        core_index, (grad_big, grad_small), (wide_big, wide_small), cell, grad_hidden, norms, sums
    )
    tokens_got = swap_cores(tokens_sent)
    norm_sums = AllSum(sums + swap_cores(sums))
    activated, tokens_sent = tie(activated, tokens_sent)
    activated = finish_with(activated, up, down)
    activated = begin_with(activated, up, norm_sums)
    mixed_kept = mixed_half(core_index, activated, w_down_turned, hidden, False)
    w_down_share = down.result()
    activated, mixed_kept, w_down_share = tie(activated, mixed_kept, w_down_share)
    activated = finish_with(activated, whole)
    activated = begin_with(activated, whole)
    activated = finish_with(activated, up)
    activated = begin_with(activated, up)
    mixed_sent = mixed_half(core_index, activated, w_down_turned, hidden, True)
    mixed_got = swap_cores(mixed_sent)
    tokens_grad = take_over(core_index, tokens_kept, tokens_got)
    mixed_kept, mixed_sent = tie(mixed_kept, mixed_sent)
    mixed_kept = finish_with(mixed_kept, whole, norm_sums)
    mixed_kept = begin_with(mixed_kept, whole, norm_sums)
    mixed_kept, tokens_grad = tie(mixed_kept, tokens_grad)
    mixed_kept = finish_with(mixed_kept, whole, norm_sums)
    mixed_kept = begin_with(mixed_kept, whole, norm_sums)
    mixed = take_over(core_index, mixed_kept, mixed_got)
    mixed = finish_with(mixed, norm_sums, up)
    mixed = begin_with(mixed, norm_sums)
    up_share = up.result()
    up_share, w_out_share = up_share[:, :up_window], up_share[:, up_window:]
    mixed, up_share, w_out_share = tie(mixed, up_share, w_out_share)
    mixed = finish_with(mixed, whole)
    qkv_share = whole.result()
    big_share, small_share = qkv_share[:, :big_window], qkv_share[:, big_window:]
    sums = norm_sums.result()

    shift = big_width + half - big_starts[1]
    w_qkv_share = pick(
        jnp.concatenate(
            [
                big_share[:rows, :big_width],
                small_share[:rows, : small * HD],
                big_share[:rows, big_width : big_width + half],
            ],
            axis=1,
        ),
        jnp.concatenate(
            [
                big_share[:rows, shift : 2 * big_width - big_starts[1]],
                small_share[:rows, : small * HD],
                big_share[:rows, 2 * big_width - big_starts[1] :],
                small_share[:rows, small_width : small_width + small * HD],
            ],
            axis=1,
        ),
    )

    def own_columns(share, starts, all_columns):
        second = all_columns // 2 - starts[1]
        return pick(share[:, : all_columns // 2], share[:, second : second + all_columns // 2])

    return (
        mixed.transpose(2, 0, 1),
        tokens_grad.transpose(2, 0, 1),
        sums[0],
        sums[1],
        w_qkv_share,
        own_columns(w_out_share[:rows], out_starts, D),
        sums[2],
        sums[3],
        own_columns(up_share[:rows], up_starts, up_all),
        own_columns(w_down_share, starts, D),
    )


def per_device(mesh, tokens, *rest):
    chips = mesh.shape["cells"]
    if mesh.shape["blk"] == 2 and tokens.shape[1] == 2 and chips & (chips - 1) == 0 and chips >= 16:
        return cell_split(tokens, *rest)
    return position_split(tokens, *rest)


def solution(mesh):
    placed = (
        P("blk", "cells", None),
        P("cells"),
        P(),
        P(),
        P(),
        P(),
        P(),
        P(),
        P(),
        P(),
        P("blk", "cells", None),
    )
    return jax.shard_map(
        functools.partial(per_device, mesh),
        mesh=mesh,
        in_specs=placed,
        out_specs=(
            P("blk", "cells", None),
            P("blk", "cells", None),
            P(),
            P(),
            P("cells", "blk"),
            P("cells", "blk"),
            P(),
            P(),
            P("cells", "blk"),
            P("cells", "blk"),
        ),
        check_vma=False,
    )
```

```python
import functools
import math

import jax
import jax.numpy as jnp
from jax import lax
from jax.experimental import pallas as pl
from jax.experimental.pallas import tpu as pltpu
from jax.sharding import PartitionSpec as P

D = 1120
HEADS = 20
HD = 56


EPSILON = 1e-05
MASKED = -1e30
LOG2E = 1.4426950408889634
LANES = 128
WIDTH = 1152
WINDOW = 256
SHARE = 1
SMALL = 0.1
TILE = 256
BF16 = jnp.bfloat16
F32 = jnp.float32
NN = (((1,), (0,)), ((), ()))
NT = (((1,), (1,)), ((), ()))
TN = (((0,), (0,)), ((), ()))


def norm_forward(values_in, gain_vec, bias_vec):
    centred = values_in - jnp.mean(values_in, axis=-1, keepdims=True)
    inverse = lax.rsqrt(jnp.mean(centred * centred, axis=-1, keepdims=True) + EPSILON)
    normed = centred * inverse
    return (normed, inverse, normed * gain_vec + bias_vec)


def norm_backward(grad_in, normed, inverse, gain_vec):
    scaled = grad_in * gain_vec
    grad_out = inverse * (
        scaled
        - jnp.mean(scaled, axis=-1, keepdims=True)
        - normed * jnp.mean(scaled * normed, axis=-1, keepdims=True)
    )
    return (grad_out, jnp.sum(grad_in * normed, axis=(0, 1)), jnp.sum(grad_in, axis=(0, 1)))


def key_scores(query_heads, key_piece, query_pos, key_start, lengths):
    key_count = key_piece.shape[0]
    key_heads = key_piece.reshape(key_count, key_piece.shape[1], HEADS, HD)
    scores = jnp.einsum(
        "qchd,kchd->chqk", query_heads, key_heads, preferred_element_type=jnp.float32
    ) * HD ** (-0.5)
    key_pos = key_start + jnp.arange(key_count, dtype=jnp.int32)
    allowed = (key_pos[None, None, :] <= query_pos[None, :, None]) & (
        key_pos[None, None, :] < lengths[:, None, None]
    )
    allowed = allowed[:, None, :, :]
    return (jnp.where(allowed, scores, MASKED), allowed)


def key_sweep(step_fn, initial, pieces, row_count, block_turns):

    def one_turn(turn_index, state_in):
        row_start = turn_index * row_count
        taken = tuple(
            (lax.dynamic_slice_in_dim(full_array, row_start, row_count, 0) for full_array in pieces)
        )
        return step_fn(state_in, taken, row_start)

    return lax.fori_loop(0, block_turns, one_turn, initial)


def position_split(
    tokens, lengths, attn_gain, attn_bias, w_qkv, w_out, mlp_gain, mlp_bias, w_up, w_down, cotangent
):
    row_count = tokens.shape[0]
    cell_count = tokens.shape[1]
    block_turns = lax.axis_size("blk")
    score_scale = HD ** (-0.5)
    query_pos = lax.axis_index("blk") * row_count + jnp.arange(row_count, dtype=jnp.int32)
    inputs = tokens.astype(jnp.float32)
    normed_one, inverse_one, pre_one = norm_forward(inputs, attn_gain, attn_bias)
    normed_low = pre_one.astype(jnp.bfloat16)
    qkv_vals = jnp.einsum(
        "rcd,de->rce", normed_low, w_qkv, preferred_element_type=jnp.float32
    ).astype(jnp.bfloat16)
    key_vals = qkv_vals[..., D : 2 * D]
    value_vals = qkv_vals[..., 2 * D :]
    query_heads = qkv_vals[..., :D].reshape(row_count, cell_count, HEADS, HD)
    start_max = jnp.full((cell_count, HEADS, row_count), MASKED, jnp.float32)
    start_sum = jnp.zeros((cell_count, HEADS, row_count), jnp.float32)
    start_out = jnp.zeros((row_count, cell_count, HEADS, HD), jnp.float32)
    scores, allowed = key_scores(
        query_heads,
        (lax.all_gather(key_vals, "blk", axis=0, tiled=True),)[0],
        query_pos,
        jnp.int32(0),
        lengths,
    )
    new_max = jnp.maximum(start_max, jnp.max(scores, axis=-1))
    weights = jnp.where(allowed, jnp.exp(scores - new_max[..., None]), 0.0)
    run_sum = jnp.sum(weights, axis=-1)
    log_total = new_max + jnp.log(run_sum)

    def probabilities(key_piece, key_start):
        scores, allowed = key_scores(query_heads, key_piece, query_pos, key_start, lengths)
        return jnp.where(allowed, jnp.exp(scores - log_total[..., None]), 0.0)

    pieces = (
        lax.all_gather(key_vals, "blk", axis=0, tiled=True),
        lax.all_gather(value_vals, "blk", axis=0, tiled=True),
    )
    prob_vals = probabilities(pieces[0], jnp.int32(0)).astype(jnp.bfloat16)
    value_heads = pieces[1].reshape(pieces[1].shape[0], cell_count, HEADS, HD)
    out_acc = jnp.einsum(
        "chqk,kchd->qchd", prob_vals, value_heads, preferred_element_type=jnp.float32
    )
    attended = out_acc.reshape(row_count, cell_count, D).astype(jnp.bfloat16)
    hidden = inputs + jnp.einsum("rcd,de->rce", attended, w_out, preferred_element_type=jnp.float32)
    normed_two, inverse_two, pre_two = norm_forward(hidden, mlp_gain, mlp_bias)
    normed_mlp = pre_two.astype(jnp.bfloat16)
    upward = jnp.einsum("rcd,df->rcf", normed_mlp, w_up, preferred_element_type=jnp.float32)
    activated_full, gelu_back = jax.vjp(
        lambda value_in: jax.nn.gelu(value_in, approximate=True), upward
    )
    activated = activated_full.astype(jnp.bfloat16)
    mixed = (
        hidden + jnp.einsum("rcf,fd->rcd", activated, w_down, preferred_element_type=jnp.float32)
    ).astype(jnp.bfloat16)
    valid_rows = (query_pos[:, None] < lengths[None, :]).astype(jnp.float32)
    grad_out = cotangent.astype(jnp.float32) * valid_rows[..., None]
    grad_low = grad_out.astype(jnp.bfloat16)
    w_down_grad = jnp.einsum("rcf,rcd->fd", activated, grad_low, preferred_element_type=jnp.float32)
    grad_act = jnp.einsum("rcd,fd->rcf", grad_low, w_down, preferred_element_type=jnp.float32)
    grad_upward = gelu_back(grad_act)[0].astype(jnp.bfloat16)
    w_up_grad = jnp.einsum(
        "rcd,rcf->df", normed_mlp, grad_upward, preferred_element_type=jnp.float32
    )
    grad_normed_two = jnp.einsum(
        "rcf,df->rcd", grad_upward, w_up, preferred_element_type=jnp.float32
    )
    grad_hidden_ln, mlp_gain_grad, mlp_bias_grad = norm_backward(
        grad_normed_two, normed_two, inverse_two, mlp_gain
    )
    grad_hidden = grad_out + grad_hidden_ln
    grad_branch = grad_hidden.astype(jnp.bfloat16)
    w_out_grad = jnp.einsum(
        "rce,rcd->ed", attended, grad_branch, preferred_element_type=jnp.float32
    )
    grad_attended = jnp.einsum(
        "rcd,ed->rce", grad_branch, w_out, preferred_element_type=jnp.float32
    ).astype(jnp.bfloat16)
    grad_heads = grad_attended.reshape(row_count, cell_count, HEADS, HD)
    whole_keys, whole_values = (
        lax.all_gather(key_vals, "blk", axis=0, tiled=True),
        lax.all_gather(value_vals, "blk", axis=0, tiled=True),
    )

    def attention_grads(key_piece, value_piece, key_start):
        prob_full = probabilities(key_piece, key_start)
        value_heads = value_piece.reshape(value_piece.shape[0], cell_count, HEADS, HD)
        dprobs = jnp.einsum(
            "qchd,kchd->chqk", grad_heads, value_heads, preferred_element_type=jnp.float32
        )
        return (prob_full, dprobs)

    def delta_step(state_in, pieces, key_start):
        prob_full, dprobs = attention_grads(pieces[0], pieces[1], key_start)
        return state_in + jnp.sum(prob_full * dprobs, axis=-1)

    row_delta = key_sweep(delta_step, start_sum, (whole_keys, whole_values), row_count, block_turns)

    def query_step(state_in, pieces, key_start):
        prob_full, dprobs = attention_grads(pieces[0], pieces[1], key_start)
        dscore = (prob_full * (dprobs - row_delta[..., None])).astype(jnp.bfloat16)
        key_heads = pieces[0].reshape(pieces[0].shape[0], cell_count, HEADS, HD)
        return state_in + jnp.einsum(
            "chqk,kchd->qchd", dscore, key_heads, preferred_element_type=jnp.float32
        )

    query_acc = key_sweep(query_step, start_out, (whole_keys, whole_values), row_count, block_turns)
    grad_queries = (query_acc * score_scale).reshape(row_count, cell_count, D).astype(jnp.bfloat16)
    key_piece = whole_keys
    value_piece = whole_values
    prob_full, dprobs = attention_grads(key_piece, value_piece, jnp.int32(0))
    dscore = (prob_full * (dprobs - row_delta[..., None])).astype(jnp.bfloat16)
    grad_keys = (
        jnp.einsum("chqk,qchd->kchd", dscore, query_heads, preferred_element_type=jnp.float32)
        * score_scale
    )
    grad_values = jnp.einsum(
        "chqk,qchd->kchd",
        prob_full.astype(jnp.bfloat16),
        grad_heads,
        preferred_element_type=jnp.float32,
    )
    kv_summed = lax.psum_scatter(
        jnp.concatenate(
            [
                grad_keys.reshape(row_count * lax.axis_size("blk"), cell_count, D),
                grad_values.reshape(row_count * lax.axis_size("blk"), cell_count, D),
            ],
            axis=-1,
        ),
        "blk",
        scatter_dimension=0,
        tiled=True,
    )
    grad_qkv = jnp.concatenate([grad_queries, kv_summed.astype(jnp.bfloat16)], axis=-1)
    w_qkv_grad = jnp.einsum("rcd,rce->de", normed_low, grad_qkv, preferred_element_type=jnp.float32)
    grad_normed_one = jnp.einsum("rce,de->rcd", grad_qkv, w_qkv, preferred_element_type=jnp.float32)
    grad_inputs_ln, attn_gain_grad, attn_bias_grad = norm_backward(
        grad_normed_one, normed_one, inverse_one, attn_gain
    )
    tokens_grad = (grad_hidden + grad_inputs_ln).astype(jnp.bfloat16)
    norm_sums = lax.psum(
        (attn_gain_grad, attn_bias_grad, mlp_gain_grad, mlp_bias_grad), ("blk", "cells")
    )
    shares = (
        lax.psum_scatter(
            w_qkv_grad.astype(jnp.bfloat16), "cells", scatter_dimension=0, tiled=True
        ).astype(jnp.float32),
        lax.psum_scatter(
            w_out_grad.astype(jnp.bfloat16), "cells", scatter_dimension=0, tiled=True
        ).astype(jnp.float32),
        lax.psum_scatter(
            w_up_grad.astype(jnp.bfloat16), "cells", scatter_dimension=0, tiled=True
        ).astype(jnp.float32),
        lax.psum_scatter(
            w_down_grad.astype(jnp.bfloat16), "cells", scatter_dimension=0, tiled=True
        ).astype(jnp.float32),
    )
    summed = (
        lax.psum_scatter(
            shares[0].astype(jnp.bfloat16), "blk", scatter_dimension=1, tiled=True
        ).astype(jnp.float32),
        lax.psum_scatter(
            shares[1].astype(jnp.bfloat16), "blk", scatter_dimension=1, tiled=True
        ).astype(jnp.float32),
        lax.psum_scatter(
            shares[2].astype(jnp.bfloat16), "blk", scatter_dimension=1, tiled=True
        ).astype(jnp.float32),
        lax.psum_scatter(
            shares[3].astype(jnp.bfloat16), "blk", scatter_dimension=1, tiled=True
        ).astype(jnp.float32),
    )
    return (
        mixed,
        tokens_grad,
        norm_sums[0],
        norm_sums[1],
        summed[0],
        summed[1],
        norm_sums[2],
        norm_sums[3],
        summed[2],
        summed[3],
    )


def cost(product):
    return pl.CostEstimate(flops=int(product * SHARE), bytes_accessed=1, transcendentals=0)


def dot(left, right, dims=NN):
    return lax.dot_general(left, right, dims, preferred_element_type=F32)


def head_lanes(head, width):
    start = jnp.minimum(head * HD // LANES, (width - WINDOW) // LANES) * LANES
    start = pl.multiple_of(start, LANES)
    lane = lax.broadcasted_iota(jnp.int32, (1, WINDOW), 1)
    offset = lane + (start - head * HD)
    own = (offset >= 0) & (offset < HD)
    spare = lane == jnp.where(start == head * HD, WINDOW - 1, 0)
    return start, own, spare


def key_bias(len_ref, seq):
    rows = lax.broadcasted_iota(jnp.int32, (seq, 1), 0)
    return jnp.where(rows < len_ref[0], 0.0, MASKED).astype(BF16)


def masked_query(q_ref, win, own, spare):
    return jnp.where(own, q_ref[:, win], jnp.where(spare, 1.0, 0.0).astype(BF16))


def causal_tile():
    key_row = lax.broadcasted_iota(jnp.int32, (TILE, TILE), 0)
    query_lane = lax.broadcasted_iota(jnp.int32, (TILE, TILE), 1)
    return key_row <= query_lane


def staggered(jobs, begin, middle, end):
    started = begin(jobs[0])
    waiting = None
    for index, job in enumerate(jobs):
        current = started
        if index + 1 < len(jobs):
            started = begin(jobs[index + 1])
        result = middle(job, *current)
        if waiting is not None:
            end(*waiting)
        waiting = (job, *result)
    end(*waiting)


def attention_forward_kernel(per, len_ref, q_ref, k_ref, v_ref, o_ref, lse_ref):
    step = pl.program_id(0)
    seq, width = q_ref.shape

    @pl.when(step == 0)
    def _():
        o_ref[...] = jnp.zeros_like(o_ref)

    bias = key_bias(len_ref, seq)
    keep = causal_tile()
    scale = LOG2E * HD ** (-0.5)
    jobs = []
    for slot in range(per):
        start, own, spare = head_lanes(step * per + slot, width)
        win = pl.ds(start, WINDOW)
        k_win = jnp.where(spare, bias, k_ref[:, win])
        q_win = masked_query(q_ref, win, own, spare)
        v_turned = jnp.transpose(v_ref[:, win])
        for turn in range(seq // TILE):
            jobs.append((slot, turn * TILE, win, own, k_win, q_win, v_turned))

    def begin(job):
        _, low, _, _, k_win, q_win, _ = job
        return (dot(k_win[: low + TILE], q_win[low : low + TILE], NT),)

    def middle(job, scores):
        slot, low = job[:2]
        edge = jnp.where(keep, scores[low:], MASKED)
        scores = edge if low == 0 else jnp.concatenate([scores[:low], edge], axis=0)
        peak = jnp.max(scores, axis=0, keepdims=True) * scale
        weights = jnp.exp2(scores * scale - peak)
        total = jnp.sum(weights, axis=0, keepdims=True)
        lse_ref[slot, :, low : low + TILE] = jnp.broadcast_to(peak + jnp.log2(total), (8, TILE))
        return weights.astype(BF16), total

    def end(job, weights, total):
        _, low, win, own, _, _, v_turned = job
        out = dot(v_turned[:, : low + TILE], weights) * (1.0 / total)
        rows = slice(low, low + TILE)
        o_ref[rows, win] = jnp.where(own, jnp.transpose(out).astype(BF16), o_ref[rows, win])

    staggered(jobs, begin, middle, end)


def attention_backward_kernel(
    per, len_ref, q_ref, k_ref, v_ref, o_ref, do_ref, lse_ref, grad_ref, delta_ref, acc_ref
):
    step = pl.program_id(0)
    seq, width = q_ref.shape

    @pl.when(step == 0)
    def _():
        grad_ref[...] = jnp.zeros_like(grad_ref)
        lane = lax.broadcasted_iota(jnp.int32, (delta_ref.shape[0], width), 1)
        first = lax.broadcasted_iota(jnp.int32, (delta_ref.shape[0], width), 0) * HD
        pick = jnp.where((lane >= first) & (lane < first + HD), 1.0, 0.0).astype(BF16)
        for turn in range(seq // TILE):
            rows = slice(turn * TILE, (turn + 1) * TILE)
            product = o_ref[rows].astype(F32) * do_ref[rows].astype(F32)
            upper = product.astype(BF16)
            lower = (product - upper.astype(F32)).astype(BF16)
            delta_ref[:, rows] = dot(pick, upper, NT) + dot(pick, lower, NT)

    bias = key_bias(len_ref, seq)
    keep = causal_tile()
    scale = LOG2E * HD ** (-0.5)
    turns = seq // TILE
    jobs = []
    for slot in range(per):
        head = step * per + slot
        start, own, spare = head_lanes(head, width)
        win = pl.ds(start, WINDOW)
        k_win = jnp.where(spare, bias, k_ref[:, win])
        q_win = masked_query(q_ref, win, own, spare)
        do_win = jnp.where(own, do_ref[:, win], jnp.zeros((), BF16))
        v_win = v_ref[:, win]
        lse = lse_ref[slot, 0:1, :]
        delta = delta_ref[pl.ds(head, 1), :]
        for turn in range(turns):
            jobs.append((slot, turn, start, own, k_win, q_win, do_win, v_win, lse, delta))

    def begin(job):
        _, turn, _, _, k_win, q_win, do_win, v_win, _, _ = job
        low = turn * TILE
        rows = slice(low, low + TILE)
        return dot(k_win[rows], q_win[low:], NT), dot(v_win[rows], do_win[low:], NT)

    def middle(job, scores, dprobs):
        turn, lse, delta = job[1], job[8], job[9]
        low = turn * TILE
        probs = jnp.exp2(scores * scale - lse[:, low:])
        edge = jnp.where(keep, probs[:, :TILE], 0.0)
        if turn + 1 < turns:
            edge = jnp.concatenate([edge, probs[:, TILE:]], axis=1)
        dscores = (edge * (dprobs - delta[:, low:])).astype(BF16)
        return edge.astype(BF16), dscores

    def end(job, probs, dscores):
        slot, turn, start, own, k_win, q_win, do_win = job[:7]
        low = turn * TILE
        rows = slice(low, low + TILE)

        def put(place, where, value):
            lanes = pl.ds(start + place * width, WINDOW)
            grad_ref[where, lanes] = jnp.where(own, value.astype(BF16), grad_ref[where, lanes])

        put(2, rows, dot(probs, do_win[low:]))
        put(1, rows, dot(dscores, q_win[low:]) * HD ** (-0.5))
        part = dot(dscores, k_win[rows], TN)
        if turn == 0:
            acc_ref[slot] = part
        else:
            acc_ref[slot, low:, :] += part
        if turn + 1 == turns:
            put(0, slice(0, seq), acc_ref[slot] * HD ** (-0.5))

    staggered(jobs, begin, middle, end)


def resident(shape, place=0):
    return pl.BlockSpec(shape, lambda step, *_: (0, place), pipeline_mode=pl.Buffered(1))


def attention_forward(qkv, length, heads, per=2):
    seq, width = qkv.shape[0], qkv.shape[1] // 3
    return pl.pallas_call(
        functools.partial(attention_forward_kernel, per),
        grid_spec=pltpu.PrefetchScalarGridSpec(
            num_scalar_prefetch=1,
            grid=(heads // per,),
            in_specs=[resident((seq, width), place) for place in range(3)],
            out_specs=[
                resident((seq, width)),
                pl.BlockSpec((per, 8, seq), lambda step, *_: (step, 0, 0)),
            ],
        ),
        out_shape=[
            jax.ShapeDtypeStruct((seq, width), BF16),
            jax.ShapeDtypeStruct((heads, 8, seq), F32),
        ],
        compiler_params=pltpu.CompilerParams(vmem_limit_bytes=20 << 20),
        cost_estimate=cost(4 * heads * seq * seq * WINDOW),
        name="attention_forward",
    )(length, qkv, qkv, qkv)


def attention_backward(qkv, attended, grad_attended, lse, length, per=2):
    seq, width = qkv.shape[0], qkv.shape[1] // 3
    heads = lse.shape[0]
    return pl.pallas_call(
        functools.partial(attention_backward_kernel, per),
        grid_spec=pltpu.PrefetchScalarGridSpec(
            num_scalar_prefetch=1,
            grid=(heads // per,),
            in_specs=[resident((seq, width), place) for place in (0, 1, 2, 0, 0)]
            + [pl.BlockSpec((per, 8, seq), lambda step, *_: (step, 0, 0))],
            out_specs=resident((seq, 3 * width)),
            scratch_shapes=[
                pltpu.VMEM((-(-heads // 16) * 16, seq), F32),
                pltpu.VMEM((per, seq, WINDOW), F32),
            ],
        ),
        out_shape=jax.ShapeDtypeStruct((seq, 3 * width), BF16),
        compiler_params=pltpu.CompilerParams(vmem_limit_bytes=30 << 20),
        cost_estimate=cost(7 * heads * seq * seq * WINDOW * (heads > 8) + 1),
        name="attention_backward",
    )(length, qkv, qkv, qkv, attended, grad_attended, lse)


def once(shape):
    return pl.BlockSpec(shape, lambda step, *_: (0, 0), pipeline_mode=pl.Buffered(1))


def in_vmem():
    return pl.BlockSpec(memory_space=pltpu.VMEM)


def lane_tiles(rows, tile):
    return pl.BlockSpec((rows, tile), lambda step, *_: (0, step))


def row_tiles(tile, columns):
    return pl.BlockSpec((tile, columns), lambda step, *_: (step, 0))


def spread_store(rows_ref, scratch_ref, value, chips, lanes):
    depth = value.shape[0]
    rows = depth // chips
    padded = rows_ref.shape[0] // chips
    scratch_ref[:depth] = value
    for pair in range(chips // 2):
        first = 2 * pair * rows
        both = jnp.concatenate(
            [
                scratch_ref[first : first + padded],
                scratch_ref[first + rows : first + rows + padded],
            ],
            axis=0,
        )
        rows_ref[2 * pair * padded : 2 * (pair + 1) * padded, lanes] = both.astype(BF16)


def norm_down(value, gain, bias):
    centred = value - jnp.mean(value, axis=0, keepdims=True)
    inverse = lax.rsqrt(jnp.mean(centred * centred, axis=0, keepdims=True) + EPSILON)
    return centred * inverse * gain + bias


def half_of(core_ref, mine_ref, other_ref, lanes):
    return jnp.where(pl.program_id(0) == core_ref[0], mine_ref[0, :, lanes], other_ref[:, lanes])


def valid_lanes(len_ref, half, lanes):
    lane = lax.broadcasted_iota(jnp.int32, (1, TILE), 1) + pl.program_id(0) * half + lanes.start
    return lane < len_ref[0]


def sub_tiles(half):
    return [slice(first, first + TILE) for first in range(0, half, TILE)]


def half_specs(depth, half):
    return [
        pl.BlockSpec((1, depth, half), lambda step, core, *_: (core[0], 0, 0), pipeline_mode=pl.Buffered(1)),
        once((depth, half)),
    ]


def widen_kernel(spans, w_ref, *wide_refs):
    rows, depth = w_ref.shape[0], w_ref.shape[1] // 3
    for wide_ref, (first, size) in zip(wide_refs, spans):
        width = wide_ref.shape[1] // 3
        for part in range(3):
            begin = part * depth + first
            piece = w_ref[:, begin : begin + size]
            if size < width:
                piece = jnp.concatenate([piece, jnp.zeros((rows, width - size), BF16)], axis=1)
            wide_ref[:, part * width : (part + 1) * width] = piece


def widen(w, spans, widths, steps=5):
    depth, columns = w.shape
    tile = depth // steps
    return pl.pallas_call(
        functools.partial(widen_kernel, spans),
        grid=(steps,),
        in_specs=[row_tiles(tile, columns)],
        out_specs=[row_tiles(tile, width) for width in widths],
        out_shape=[jax.ShapeDtypeStruct((depth, width), BF16) for width in widths],
        compiler_params=pltpu.CompilerParams(vmem_limit_bytes=16 << 20),
        cost_estimate=cost(3000000000),
        name="widen",
    )(w)


def project_kernel(
    chips, core_ref, mine_ref, other_ref, norm_ref, first_w_ref, second_w_ref, first_ref, second_ref, rows_ref, scratch_ref
):
    half = other_ref.shape[1]

    @pl.when(pl.program_id(0) == 0)
    def _():
        scratch_ref[...] = jnp.zeros_like(scratch_ref)

    columns = jnp.transpose(norm_ref[...])

    def begin(lanes):
        value = half_of(core_ref, mine_ref, other_ref, lanes).astype(F32)
        normed = norm_down(value, columns[:, 0:1], columns[:, 1:2])
        spread_store(rows_ref, scratch_ref.at[lanes.start // TILE], normed, chips, lanes)
        return (jnp.transpose(normed.astype(BF16)),)

    def middle(lanes, left):
        first_ref[lanes] = dot(left, first_w_ref[...]).astype(BF16)
        second_ref[lanes] = dot(left, second_w_ref[...]).astype(BF16)
        return ()

    staggered(sub_tiles(half), begin, middle, lambda lanes: None)


def project(core, turned, other, norms, wides, chips, rows_pad):
    _, depth, half = turned.shape
    widths = [wide.shape[1] for wide in wides]
    return pl.pallas_call(
        functools.partial(project_kernel, chips),
        grid_spec=pltpu.PrefetchScalarGridSpec(
            num_scalar_prefetch=1,
            grid=(2,),
            in_specs=half_specs(depth, half) + [once(norms.shape)] + [once(wide.shape) for wide in wides],
            out_specs=[row_tiles(half, width) for width in widths] + [lane_tiles(chips * rows_pad, half)],
            scratch_shapes=[pltpu.VMEM((half // TILE, depth + 8, TILE), F32)],
        ),
        out_shape=[jax.ShapeDtypeStruct((2 * half, width), BF16) for width in widths]
        + [jax.ShapeDtypeStruct((chips * rows_pad, 2 * half), BF16)],
        compiler_params=pltpu.CompilerParams(vmem_limit_bytes=22 << 20),
        cost_estimate=cost(2 * 2 * half * depth * sum(widths)),
        name="project",
    )(core, turned, other, norms, *wides)


def hand_over_kernel(core_ref, first_ref, second_ref, first_out, second_out):
    first_out[...] = first_ref[0]
    second_out[...] = second_ref[0]


def hand_over(core, first, second):
    _, depth, half = first.shape
    tile = half // 2
    taken = pl.BlockSpec((1, depth, tile), lambda step, core: (1 - core[0], 0, step))
    return pl.pallas_call(
        hand_over_kernel,
        grid_spec=pltpu.PrefetchScalarGridSpec(
            num_scalar_prefetch=1,
            grid=(2,),
            in_specs=[taken, taken],
            out_specs=[lane_tiles(depth, tile)] * 2,
        ),
        out_shape=[jax.ShapeDtypeStruct((depth, half), BF16)] * 2,
        name="hand_over",
    )(core, first, second)


def take_over_kernel(core_ref, got_ref, whole_ref, out_ref):
    out_ref[0] = got_ref[...]


def take_over(core, whole, got):
    depth, half = got.shape
    tile = half // 2
    return pl.pallas_call(
        take_over_kernel,
        grid_spec=pltpu.PrefetchScalarGridSpec(
            num_scalar_prefetch=1,
            grid=(2,),
            in_specs=[lane_tiles(depth, tile), pl.BlockSpec(memory_space=pl.ANY)],
            out_specs=pl.BlockSpec((1, depth, tile), lambda step, core: (1 - core[0], 0, step)),
        ),
        out_shape=jax.ShapeDtypeStruct(whole.shape, BF16),
        input_output_aliases={2: 0},
        compiler_params=pltpu.CompilerParams(vmem_limit_bytes=10 << 20),
        name="take_over",
    )(core, got, whole)


def hidden_kernel(
    chips,
    core_ref,
    len_ref,
    mine_ref,
    other_ref,
    mine_grad_ref,
    other_grad_ref,
    first_ref,
    second_ref,
    w_ref,
    norm_ref,
    hidden_ref,
    normed_ref,
    grad_ref,
    rows_ref,
    o_rows_ref,
    w_turned_ref,
    scratch_ref,
):
    depth = w_ref.shape[0]
    half = other_ref.shape[1]

    @pl.when(pl.program_id(0) == 0)
    def _():
        scratch_ref[...] = jnp.zeros_like(scratch_ref)
        w_turned_ref[...] = jnp.transpose(w_ref[...])

    columns = jnp.transpose(norm_ref[...])

    def begin(lanes):
        attended = jnp.concatenate([first_ref[lanes], second_ref[lanes]], axis=1)
        value = half_of(core_ref, mine_ref, other_ref, lanes).astype(F32)
        hidden = value + dot(w_turned_ref[...], attended[:, :depth], NT)
        turned = jnp.transpose(attended).astype(F32)[:depth]
        spread_store(o_rows_ref, scratch_ref.at[2 * (lanes.start // TILE)], turned, chips, lanes)
        return (hidden,)

    def middle(lanes, hidden):
        hidden_ref[:, lanes] = hidden
        grad = half_of(core_ref, mine_grad_ref, other_grad_ref, lanes)
        grad = jnp.where(valid_lanes(len_ref, half, lanes), grad, jnp.zeros((), BF16))
        grad_ref[lanes, :depth] = jnp.transpose(grad)
        grad_ref[lanes, depth:] = jnp.zeros((TILE, grad_ref.shape[1] - depth), BF16)
        normed = norm_down(hidden, columns[:, 2:3], columns[:, 3:4])
        spread_store(rows_ref, scratch_ref.at[2 * (lanes.start // TILE) + 1], normed, chips, lanes)
        normed_ref[lanes] = jnp.transpose(normed.astype(BF16))
        return ()

    staggered(sub_tiles(half), begin, middle, lambda lanes: None)


def hidden_state(core, length, cell, grad_cell, attended, w_out, norms, chips, rows_pad):
    _, depth, half = cell[0].shape
    seq = 2 * half
    spread = jax.ShapeDtypeStruct((chips * rows_pad, seq), BF16)
    return pl.pallas_call(
        functools.partial(hidden_kernel, chips),
        grid_spec=pltpu.PrefetchScalarGridSpec(
            num_scalar_prefetch=2,
            grid=(2,),
            in_specs=half_specs(depth, half) * 2
            + [row_tiles(half, part.shape[1]) for part in attended]
            + [once(w_out.shape), once(norms.shape)],
            out_specs=[lane_tiles(depth, half), row_tiles(half, depth), row_tiles(half, WIDTH)]
            + [lane_tiles(chips * rows_pad, half)] * 2,
            scratch_shapes=[
                pltpu.VMEM((depth, depth), BF16),
                pltpu.VMEM((2 * half // TILE, depth + 8, TILE), F32),
            ],
        ),
        out_shape=[
            jax.ShapeDtypeStruct((depth, seq), F32),
            jax.ShapeDtypeStruct((seq, depth), BF16),
            jax.ShapeDtypeStruct((seq, WIDTH), BF16),
            spread,
            spread,
        ],
        compiler_params=pltpu.CompilerParams(vmem_limit_bytes=60 << 20),
        cost_estimate=cost(5 * seq * depth * depth),
        name="hidden_state",
    )(core, length, *cell, *grad_cell, *attended, w_out, norms)


GELU = (2.0 / math.pi) ** 0.5


def hidden_units_kernel(
    tile, normed_ref, grad_ref, up_ref, down_ref, activated_ref, grad_upward_ref
):
    seq, depth = normed_ref.shape

    def begin(first):
        rows = slice(first, first + tile)
        return dot(normed_ref[rows], up_ref[...]), dot(grad_ref[rows, :depth], down_ref[...])

    def middle(first, upward, grad_activated):
        rows = slice(first, first + tile)
        square = upward * upward
        gate = 0.5 * jnp.tanh(upward * (GELU + (GELU * 0.044715) * square)) + 0.5
        activated = upward * gate
        slope = gate + 2.0 * activated * (1.0 - gate) * (GELU + (3 * GELU * 0.044715) * square)
        activated_ref[:, rows] = jnp.transpose(activated.astype(BF16))
        grad_upward_ref[rows] = (grad_activated * slope).astype(BF16)
        return ()

    staggered(list(range(0, seq, tile)), begin, middle, lambda first: None)


def hidden_units(normed, grad, w_up, w_down_turned, tile=768, rows=256):
    seq, depth = normed.shape
    units = w_up.shape[1]
    return pl.pallas_call(
        functools.partial(hidden_units_kernel, rows),
        grid=(pl.cdiv(units, tile),),
        in_specs=[once(normed.shape), once(grad.shape)] + [lane_tiles(depth, tile)] * 2,
        out_specs=[row_tiles(tile, seq), lane_tiles(seq, tile)],
        out_shape=[
            jax.ShapeDtypeStruct((units, seq), BF16),
            jax.ShapeDtypeStruct((seq, units), BF16),
        ],
        compiler_params=pltpu.CompilerParams(vmem_limit_bytes=60 << 20),
        cost_estimate=cost(4 * seq * depth * units),
        name="hidden_units",
    )(normed, grad, w_up, w_down_turned)


def norm_down_back(grad_in, value, gain, gain_ref, bias_ref):
    centred = value - jnp.mean(value, axis=0, keepdims=True)
    inverse = lax.rsqrt(jnp.mean(centred * centred, axis=0, keepdims=True) + EPSILON)
    normed = centred * inverse
    product = grad_in * normed
    tiles = [slice(first, first + LANES) for first in range(0, value.shape[1], LANES)]
    gain_ref[...] += sum(product[:, lanes] for lanes in tiles)
    bias_ref[...] += sum(grad_in[:, lanes] for lanes in tiles)
    scaled = grad_in * gain
    return inverse * (
        scaled
        - jnp.mean(scaled, axis=0, keepdims=True)
        - normed * jnp.mean(product * gain, axis=0, keepdims=True)
    )


def lane_sums(rows_ref, first, *refs):
    @pl.when(pl.program_id(0) == pl.num_programs(0) - 1)
    def _():
        for place, ref in enumerate(refs):
            row = jnp.sum(jnp.transpose(ref[...]), axis=0, keepdims=True)
            rows_ref[first + place : first + place + 1, :] = row


def clear_first(*refs):
    @pl.when(pl.program_id(0) == 0)
    def _():
        for ref in refs:
            ref[...] = jnp.zeros_like(ref)


def hidden_grad_kernel(
    core_ref,
    len_ref,
    grad_up_ref,
    w_up_ref,
    hidden_ref,
    mine_grad_ref,
    other_grad_ref,
    w_ref,
    norm_ref,
    grad_hidden_ref,
    branch_ref,
    first_ref,
    second_ref,
    sums_ref,
    gain_ref,
    bias_ref,
):
    clear_first(gain_ref, bias_ref, sums_ref)
    depth, half = hidden_ref.shape
    width = first_ref.shape[1]
    columns = jnp.transpose(norm_ref[...])

    def begin(lanes):
        return (dot(w_up_ref[...], grad_up_ref[lanes], NT),)

    def middle(lanes, grad_normed):
        grad = half_of(core_ref, mine_grad_ref, other_grad_ref, lanes)
        grad = jnp.where(valid_lanes(len_ref, half, lanes), grad, jnp.zeros((), BF16)).astype(F32)
        grad = grad + norm_down_back(grad_normed, hidden_ref[:, lanes], columns[:, 2:3], gain_ref, bias_ref)
        grad_hidden_ref[:, lanes] = grad
        branch = jnp.transpose(grad.astype(BF16))
        branch_ref[lanes, :depth] = branch
        branch_ref[lanes, depth:] = jnp.zeros((TILE, branch_ref.shape[1] - depth), BF16)
        return (branch,)

    def end(lanes, branch):
        first_ref[lanes] = dot(branch, w_ref[:width], NT).astype(BF16)
        second_ref[lanes, : depth - width] = dot(branch, w_ref[width:], NT).astype(BF16)
        second_ref[lanes, depth - width :] = jnp.zeros((TILE, second_ref.shape[1] - depth + width), BF16)

    staggered(sub_tiles(half), begin, middle, end)
    lane_sums(sums_ref, 2, gain_ref, bias_ref)


def hidden_grad(core, length, grad_upward, w_up, hidden, grad_cell, w_out, norms, widths):
    depth, seq = hidden.shape
    half = seq // 2
    units = w_up.shape[1]
    return pl.pallas_call(
        hidden_grad_kernel,
        grid_spec=pltpu.PrefetchScalarGridSpec(
            num_scalar_prefetch=2,
            grid=(2,),
            in_specs=[row_tiles(half, units), once(w_up.shape), lane_tiles(depth, half)]
            + half_specs(depth, half)
            + [once(w_out.shape), once(norms.shape)],
            out_specs=[lane_tiles(depth, half), row_tiles(half, WIDTH)]
            + [row_tiles(half, width) for width in widths]
            + [once((8, depth))],
            scratch_shapes=[pltpu.VMEM((depth, LANES), F32)] * 2,
        ),
        out_shape=[
            jax.ShapeDtypeStruct((depth, seq), F32),
            jax.ShapeDtypeStruct((seq, WIDTH), BF16),
        ]
        + [jax.ShapeDtypeStruct((seq, width), BF16) for width in widths]
        + [jax.ShapeDtypeStruct((8, depth), F32)],
        compiler_params=pltpu.CompilerParams(vmem_limit_bytes=60 << 20),
        cost_estimate=cost(2 * seq * depth * (units + 2 * depth)),
        name="hidden_grad",
    )(core, length, grad_upward, w_up, hidden, *grad_cell, w_out, norms)


def half_place(step, core):
    return jnp.where(step == 0, 1 - core, core)


def tokens_grad_kernel(
    core_ref,
    first_ref,
    second_ref,
    wide_first_ref,
    wide_second_ref,
    mine_ref,
    other_ref,
    grad_hidden_ref,
    norm_ref,
    earlier_ref,
    sent_ref,
    kept_ref,
    sums_ref,
    gain_ref,
    bias_ref,
):
    clear_first(gain_ref, bias_ref)
    sums_ref[...] = earlier_ref[...]
    step = pl.program_id(0)
    columns = jnp.transpose(norm_ref[...])

    def begin(lanes):
        grad = dot(wide_first_ref[...], first_ref[lanes], NT)
        return (grad + dot(wide_second_ref[...], second_ref[lanes], NT),)

    def middle(lanes, grad_normed):
        value = jnp.where(step == 0, other_ref[:, lanes], mine_ref[0, :, lanes]).astype(F32)
        grad = norm_down_back(grad_normed, value, columns[:, 0:1], gain_ref, bias_ref)
        grad = (grad_hidden_ref[:, lanes] + grad).astype(BF16)

        @pl.when(step == 0)
        def _():
            sent_ref[:, lanes] = grad

        @pl.when(step == 1)
        def _():
            kept_ref[0, :, lanes] = grad

        return ()

    staggered(sub_tiles(other_ref.shape[1]), begin, middle, lambda lanes: None)
    lane_sums(sums_ref, 0, gain_ref, bias_ref)


def tokens_gradient(core, grads, wides, cell, grad_hidden, norms, sums):
    depth, seq = grad_hidden.shape
    half = seq // 2
    return pl.pallas_call(
        tokens_grad_kernel,
        grid_spec=pltpu.PrefetchScalarGridSpec(
            num_scalar_prefetch=1,
            grid=(2,),
            in_specs=[
                pl.BlockSpec((half, part.shape[1]), lambda step, core: (half_place(step, core[0]), 0))
                for part in grads
            ]
            + [in_vmem() for part in wides]
            + half_specs(depth, half)
            + [
                pl.BlockSpec((depth, half), lambda step, core: (0, half_place(step, core[0]))),
                once(norms.shape),
                once(sums.shape),
            ],
            out_specs=[
                once((depth, half)),
                pl.BlockSpec((1, depth, half), lambda step, core: (core[0], 0, 0), pipeline_mode=pl.Buffered(1)),
                once(sums.shape),
            ],
            scratch_shapes=[pltpu.VMEM((depth, LANES), F32)] * 2,
        ),
        out_shape=[
            jax.ShapeDtypeStruct((depth, half), BF16),
            jax.ShapeDtypeStruct((2, depth, half), BF16),
            jax.ShapeDtypeStruct(sums.shape, F32),
        ],
        compiler_params=pltpu.CompilerParams(vmem_limit_bytes=26 << 20),
        cost_estimate=cost(7 * seq * depth * WIDTH),
        name="tokens_gradient",
    )(core, *grads, *wides, *cell, grad_hidden, norms, sums)


def mixed_sent_kernel(core_ref, activated_ref, w_ref, hidden_ref, out_ref):
    out_ref[...] = (hidden_ref[...] + dot(w_ref[...], activated_ref[...])).astype(BF16)


def mixed_kept_kernel(core_ref, activated_ref, w_ref, hidden_ref, out_ref):
    out_ref[0] = (hidden_ref[...] + dot(w_ref[...], activated_ref[...])).astype(BF16)


def mixed_half(core, activated, w_down_turned, hidden, sent):
    depth, seq = hidden.shape
    units = activated.shape[0]
    tile = seq // 4

    def place(step, core):
        return 0, (2 - 2 * core[0] if sent else 2 * core[0]) + step

    if sent:
        out_spec = lane_tiles(depth, tile)
        out_shape = jax.ShapeDtypeStruct((depth, seq // 2), BF16)
    else:
        out_spec = pl.BlockSpec((1, depth, tile), lambda step, core: (core[0], 0, step))
        out_shape = jax.ShapeDtypeStruct((2, depth, seq // 2), BF16)
    return pl.pallas_call(
        mixed_sent_kernel if sent else mixed_kept_kernel,
        grid_spec=pltpu.PrefetchScalarGridSpec(
            num_scalar_prefetch=1,
            grid=(2,),
            in_specs=[
                pl.BlockSpec((units, tile), place),
                once(w_down_turned.shape),
                pl.BlockSpec((depth, tile), place),
            ],
            out_specs=out_spec,
        ),
        out_shape=out_shape,
        compiler_params=pltpu.CompilerParams(vmem_limit_bytes=60 << 20),
        cost_estimate=cost(seq * depth * units),
        name="mixed_half",
    )(core, activated, w_down_turned, hidden)


def swap_cores(value):
    return lax.ppermute(value, "blk", [(0, 1), (1, 0)])


def swap_chips(value, bit):
    count = lax.axis_size("cells")
    return lax.ppermute(value, "cells", [(place, place ^ bit) for place in range(count)])


def begin_with(chain, *scatters):
    sends = [item.send() for item in scatters]
    flat = [value for group in sends for value in group]
    chain, *flat = lax.optimization_barrier((chain, *flat))
    for item, group in zip(scatters, sends):
        item.move(flat[: len(group)])
        flat = flat[len(group) :]
    return chain


def finish_with(chain, *scatters):
    groups = [item.got for item in scatters]
    flat = [value for group in groups for value in group]
    chain, *flat = lax.optimization_barrier((chain, *flat))
    for item, group in zip(scatters, groups):
        item.arrived(flat[: len(group)])
        flat = flat[len(group) :]
    return chain


class AllSum:
    def __init__(self, value):
        self.value = value
        self.stage = 0
        self.got = None

    def send(self):
        if self.got is not None:
            self.value = self.value + self.got[0]
        return [self.value]

    def move(self, sent):
        self.got = [swap_chips(sent[0], 1 << self.stage)]
        self.stage += 1
        return self.got

    def arrived(self, got):
        self.got = list(got)

    def result(self):
        return self.value + self.got[0]


def stage_order(bits, second):
    return ([1, 0] if second else [0, 1]) + list(range(2, bits))


def block_mask(index, order):
    bits = len(order)
    return sum(((index >> (bits - 1 - stage)) & 1) << bit for stage, bit in enumerate(order))


def cut_rows(rows):
    return rows - rows // 16 * 8


def columns_sent_kernel(per, scalar_ref, left_ref, *refs):
    right = refs[0][...] if per == 1 else jnp.concatenate([ref[...] for ref in refs[:per]], axis=1)
    refs[-1][...] = dot(left_ref[...], right).astype(BF16)


def columns_kept_kernel(per, chips, scalar_ref, left_ref, *refs):
    right = refs[0][...] if per == 1 else jnp.concatenate([ref[...] for ref in refs[:per]], axis=1)
    got_ref, scratch_ref = refs[per], refs[-1]
    outs = refs[-5:-1]
    bits = chips.bit_length() - 1
    scratch_ref[...] = dot(left_ref[...], right) + got_ref[...].astype(F32)
    rows = left_ref.shape[0] // chips
    cut = cut_rows(rows)
    for part, (first, size) in enumerate(((0, cut), (cut, rows - cut))):
        order = stage_order(bits, part == 1)
        for index in range(chips):
            block = jnp.bitwise_xor(scalar_ref[1], block_mask(index, order))
            row = pl.multiple_of(block * rows, 8) + first
            value = scratch_ref[pl.ds(pl.multiple_of(row, 8), size), :].astype(BF16)
            outs[2 * part + index // (chips // 2)][index % (chips // 2)] = value


def column_specs(per, depth, tiles):
    return [
        pl.BlockSpec((depth, LANES), functools.partial(column_place, per, extra))
        for extra in range(per)
    ]


def column_place(per, extra, step, scalar):
    return 0, scalar[0] + per * step + extra


def columns_sent(left, right, first, place, tiles, per, room=14):
    depth, seq = left.shape
    return pl.pallas_call(
        functools.partial(columns_sent_kernel, per),
        grid_spec=pltpu.PrefetchScalarGridSpec(
            num_scalar_prefetch=1,
            grid=(tiles // per,),
            in_specs=[in_vmem()] + column_specs(per, seq, tiles),
            out_specs=lane_tiles(depth, per * LANES),
        ),
        out_shape=jax.ShapeDtypeStruct((depth, tiles * LANES), BF16),
        compiler_params=pltpu.CompilerParams(vmem_limit_bytes=room << 20),
        cost_estimate=cost(SMALL * 2 * depth * seq * tiles * LANES),
        name="columns_sent",
    )(jnp.stack([first, place]), left, *[right] * per)


def columns_kept(left, right, got, first, place, chips, per, width, begin=0, into=None, room=22):
    depth, seq = left.shape
    tiles = got.shape[1] // LANES
    rows = depth // chips
    cut = cut_rows(rows)
    sizes = (cut, cut, rows - cut, rows - cut)
    shift = begin // per
    extra = [] if into is None else list(into)
    count = 3 + per
    return pl.pallas_call(
        functools.partial(columns_kept_kernel, per, chips),
        grid_spec=pltpu.PrefetchScalarGridSpec(
            num_scalar_prefetch=1,
            grid=(tiles // per,),
            in_specs=[in_vmem()]
            + column_specs(per, seq, tiles)
            + [lane_tiles(depth, per * LANES)]
            + [pl.BlockSpec(memory_space=pl.ANY)] * len(extra),
            out_specs=[
                pl.BlockSpec((chips // 2, size, per * LANES), lambda step, *_: (0, 0, step + shift))
                for size in sizes
            ],
            scratch_shapes=[pltpu.VMEM((depth, per * LANES), F32)],
        ),
        out_shape=[jax.ShapeDtypeStruct((chips // 2, size, width), BF16) for size in sizes],
        input_output_aliases={count + index: index for index in range(len(extra))},
        compiler_params=pltpu.CompilerParams(vmem_limit_bytes=room << 20),
        cost_estimate=cost(SMALL * 2 * depth * seq * tiles * LANES),
        name="columns_kept",
    )(jnp.stack([first, place]), left, *[right] * per, got, *extra)


def rows_sent_kernel(window, scalar_ref, left_ref, right_ref, out_ref):
    lanes = pl.ds(pl.multiple_of(scalar_ref[0] * LANES, LANES), window)
    out_ref[...] = dot(left_ref[...], right_ref[:, lanes]).astype(BF16)


def rows_sent(left, right, first, place, window, per):
    depth, seq = left.shape
    tile = depth // per
    return pl.pallas_call(
        functools.partial(rows_sent_kernel, window),
        grid_spec=pltpu.PrefetchScalarGridSpec(
            num_scalar_prefetch=1,
            grid=(per,),
            in_specs=[row_tiles(tile, seq), once(right.shape)],
            out_specs=row_tiles(tile, window),
        ),
        out_shape=jax.ShapeDtypeStruct((depth, window), BF16),
        compiler_params=pltpu.CompilerParams(vmem_limit_bytes=60 << 20),
        cost_estimate=cost(3 * depth * seq * window),
        name="rows_sent",
    )(jnp.stack([first, place]), left, right)


def rows_kept_kernel(window, chips, scalar_ref, left_ref, right_ref, got_ref, *outs):
    lanes = pl.ds(pl.multiple_of(scalar_ref[0] * LANES, LANES), window)
    value = dot(left_ref[...], right_ref[:, lanes]) + got_ref[...].astype(F32)
    bits = chips.bit_length() - 1
    blocks = chips // pl.num_programs(0) if False else value.shape[0] // (outs[0].shape[1] + outs[2].shape[1])
    rows = value.shape[0] // blocks
    cut = cut_rows(rows)
    for slot in range(blocks):
        away = jnp.bitwise_xor(scalar_ref[1], pl.program_id(0) * blocks + slot)
        for part, (first, size) in enumerate(((0, cut), (cut, rows - cut))):
            order = stage_order(bits, part == 1)
            index = sum(((away >> bit) & 1) << (bits - 1 - stage) for stage, bit in enumerate(order))
            begin = slot * rows + first
            piece = value[begin : begin + size].astype(BF16)

            @pl.when(index < chips // 2)
            def _(piece=piece, index=index, part=part):
                outs[2 * part][index] = piece

            @pl.when(index >= chips // 2)
            def _(piece=piece, index=index, part=part):
                outs[2 * part + 1][index - chips // 2] = piece


def rows_kept(left, right, got, first, place, chips, per):
    depth, seq = left.shape
    window = got.shape[1]
    tile = depth // per
    rows = depth // chips
    cut = cut_rows(rows)
    sizes = (cut, cut, rows - cut, rows - cut)
    return pl.pallas_call(
        functools.partial(rows_kept_kernel, window, chips),
        grid_spec=pltpu.PrefetchScalarGridSpec(
            num_scalar_prefetch=1,
            grid=(per,),
            in_specs=[row_tiles(tile, seq), once(right.shape), row_tiles(tile, window)],
            out_specs=[
                pl.BlockSpec(
                    (chips // 2, size, window),
                    lambda step, *_: (0, 0, 0),
                    pipeline_mode=pl.Buffered(1),
                )
                for size in sizes
            ],
        ),
        out_shape=[jax.ShapeDtypeStruct((chips // 2, size, window), BF16) for size in sizes],
        compiler_params=pltpu.CompilerParams(vmem_limit_bytes=60 << 20),
        cost_estimate=cost(3 * depth * seq * window),
        name="rows_kept",
    )(jnp.stack([first, place]), left, right, got)


def halve_kernel(count, *refs):
    ins, outs = refs[: 4 * count], refs[4 * count :]
    kept, sent = [], []
    for part in range(count):
        near, far, near_got, far_got = ins[4 * part : 4 * part + 4]
        kept.append(near[...].astype(F32) + near_got[...].astype(F32))
        sent.append(far[...].astype(F32) + far_got[...].astype(F32))
    if len(outs) < 2 * count:
        kept, sent = [jnp.concatenate(kept, axis=1)], [jnp.concatenate(sent, axis=1)]
    for part, (one, other) in enumerate(zip(kept, sent)):
        outs[2 * part][...] = one.astype(BF16)
        outs[2 * part + 1][...] = other.astype(BF16)


def halve(kept, got, join):
    half = kept[0].shape[0] // 2
    in_specs, operands = [], []
    for own, other in zip(kept, got):
        block = (1,) + own.shape[1:]
        near = pl.BlockSpec(block, lambda step: (step, 0, 0))
        far = pl.BlockSpec(block, lambda step: (step + half, 0, 0))
        in_specs += [near, far, near, far]
        operands += [own, own, other, other]
    rows = [own.shape[1] for own in kept]
    rows = [sum(rows)] if join else rows
    width = kept[0].shape[2]
    return pl.pallas_call(
        functools.partial(halve_kernel, len(kept)),
        grid=(half,),
        in_specs=in_specs,
        out_specs=[pl.BlockSpec((1, size, width), lambda step: (step, 0, 0)) for size in rows for _ in range(2)],
        out_shape=[jax.ShapeDtypeStruct((half, size, width), BF16) for size in rows for _ in range(2)],
        compiler_params=pltpu.CompilerParams(vmem_limit_bytes=12 << 20),
        cost_estimate=cost(1000 * 1000000),
        name="halve",
    )(*operands)


class Scatter:
    def __init__(self, first_kept, first_sent, second_kept, second_sent):
        self.bits = lax.axis_size("cells").bit_length() - 1
        self.kept = [first_kept, second_kept]
        self.next = [first_sent, second_sent]
        self.stage = 0
        self.got = None

    def send(self):
        if self.got is not None:
            out = halve(self.kept, self.got, self.stage == 2)
            self.kept, self.next = list(out[0::2]), list(out[1::2])
        return self.next

    def move(self, sent):
        orders = [stage_order(self.bits, part == 1) for part in range(len(sent))]
        self.got = [swap_chips(value, 1 << order[self.stage]) for value, order in zip(sent, orders)]
        self.stage += 1
        return self.got

    def arrived(self, got):
        self.got = list(got)

    def result(self):
        return self.kept[0][0].astype(F32) + self.got[0][0].astype(F32)


def cell_split(
    tokens, lengths, attn_gain, attn_bias, w_qkv, w_out, mlp_gain, mlp_bias, w_up, w_down, cotangent
):
    row_count = tokens.shape[0]
    seq = 2 * row_count
    core = lax.axis_index("blk")
    chips = lax.axis_size("cells")
    rows = D // chips
    rows_pad = -(-rows // 8) * 8

    def tie(*values):
        return lax.optimization_barrier(values)

    def pick(first, second):
        return jnp.where(core == 0, first, second)

    core_index = core.reshape(1).astype(jnp.int32)
    length = pick(lengths[0], lengths[1])
    length = length.reshape(1)
    turned, turned_cotangent = tokens.transpose(1, 2, 0), cotangent.transpose(1, 2, 0)
    sent, sent_cotangent = hand_over(core_index, turned, turned_cotangent)
    cell = (turned, swap_cores(sent))
    grad_cell = (turned_cotangent, swap_cores(sent_cotangent))
    norms = jnp.stack([attn_gain, attn_bias, mlp_gain, mlp_bias] * 2)
    w_down_turned = w_down.T

    big, small = 16, HEADS - 16
    spans = ((0, big * HD), (big * HD, small * HD))
    widths = [3 * (-(-size // LANES) * LANES) for _, size in spans]
    wide_big, wide_small = widen(w_qkv, spans, widths)
    qkv_big, qkv_small, one_rows = project(
        core_index, *cell, norms, (wide_big, wide_small), chips, rows_pad
    )
    attended_big, lse_big = attention_forward(qkv_big, length, big)
    attended_small, lse_small = attention_forward(qkv_small, length, small)
    hidden, normed_mlp, grad_low, mlp_rows, attended_rows = hidden_state(
        core_index, length, cell, grad_cell, (attended_big, attended_small), w_out, norms, chips, rows_pad
    )
    activated, grad_upward = hidden_units(normed_mlp, grad_low, w_up, w_down_turned)

    half = D // 2
    window = -(-half // LANES) * LANES
    starts = (0, WIDTH - window)
    ours, theirs = pick(*starts), pick(*starts[::-1])
    up_all = w_up.shape[1]
    up_window = -(-up_all // 2 // LANES) * LANES
    up_starts = (0, up_all - up_window)
    up_ours, up_theirs = pick(*up_starts), pick(*up_starts[::-1])
    big_width, small_width = qkv_big.shape[1] // 3, qkv_small.shape[1] // 3
    big_window = big_width + -(-half // LANES) * LANES
    big_starts = (0, 3 * big_width - big_window)
    big_ours, big_theirs = pick(*big_starts), pick(*big_starts[::-1])
    small_window = 2 * small_width
    small_starts = (0, small_width)
    small_ours, small_theirs = pick(*small_starts), pick(*small_starts[::-1])

    place = lax.axis_index("cells").astype(jnp.int32)

    def tiles(first):
        return (first // LANES).astype(jnp.int32)

    ours, theirs, up_ours, up_theirs = tiles(ours), tiles(theirs), tiles(up_ours), tiles(up_theirs)
    big_ours, big_theirs, small_ours, small_theirs = map(
        tiles, (big_ours, big_theirs, small_ours, small_theirs)
    )
    up_count, out_count = up_window // LANES, 6
    out_starts = (0, WIDTH - out_count * LANES)
    out_ours, out_theirs = tiles(pick(*out_starts)), tiles(pick(*out_starts[::-1]))
    down_steps = chips // 4

    down_sent = rows_sent(activated, grad_low, theirs, place, window, down_steps)
    down_got = swap_cores(down_sent)
    mlp_rows, down_sent = tie(mlp_rows, down_sent)
    up_sent = columns_sent(mlp_rows, grad_upward, up_theirs, place, up_count, 6, 60)
    up_got = swap_cores(up_sent)
    activated, up_sent = tie(activated, up_sent)
    down = Scatter(*rows_kept(activated, grad_low, down_got, ours, place, chips, down_steps))
    mlp_rows = begin_with(mlp_rows, down)
    up_parts = columns_kept(
        mlp_rows, grad_upward, up_got, up_ours, place, chips, 6, up_window + out_count * LANES, room=60
    )
    grad_upward, *up_parts = tie(grad_upward, *up_parts)
    grad_hidden, grad_branch, grad_attended_big, grad_attended_small, sums = hidden_grad(
        core_index, length, grad_upward, w_up, hidden, grad_cell, w_out, norms, (big_width, small_width)
    )
    out_sent = columns_sent(
        attended_rows, grad_branch, out_theirs, place, out_count, out_count, 60
    )
    out_got = swap_cores(out_sent)
    grad_attended_small, out_sent = tie(grad_attended_small, out_sent)
    grad_attended_small = finish_with(grad_attended_small, down)
    grad_attended_small = begin_with(grad_attended_small, down)
    grad_small = attention_backward(
        qkv_small, attended_small, grad_attended_small, lse_small, length
    )
    out_got, grad_small = tie(out_got, grad_small)
    up = Scatter(
        *columns_kept(
            attended_rows,
            grad_branch,
            out_got,
            out_ours,
            place,
            chips,
            out_count,
            up_window + out_count * LANES,
            up_count,
            up_parts,
            60,
        )
    )
    grad_attended_big = finish_with(grad_attended_big, down)
    grad_attended_big = begin_with(grad_attended_big, up, down)
    small_sent = columns_sent(one_rows, grad_small, small_theirs, place, small_window // LANES, 4)
    small_got = swap_cores(small_sent)
    grad_attended_big, small_sent = tie(grad_attended_big, small_sent)
    grad_big = attention_backward(qkv_big, attended_big, grad_attended_big, lse_big, length)
    grad_big = finish_with(grad_big, up, down)
    grad_big = begin_with(grad_big, up, down)
    big_sent = columns_sent(one_rows, grad_big, big_theirs, place, big_window // LANES, 6)
    big_got = swap_cores(big_sent)
    grad_small, big_sent, small_got = tie(grad_small, big_sent, small_got)
    qkv_parts = columns_kept(
        one_rows,
        grad_small,
        small_got,
        small_ours,
        place,
        chips,
        4,
        big_window + small_window,
        big_window // LANES,
    )
    big_got, *qkv_parts = tie(big_got, *qkv_parts)
    whole = Scatter(
        *columns_kept(
            one_rows,
            grad_big,
            big_got,
            big_ours,
            place,
            chips,
            6,
            big_window + small_window,
            0,
            qkv_parts,
        )
    )
    grad_big, grad_small = begin_with((grad_big, grad_small), whole)
    grad_big, grad_small = finish_with((grad_big, grad_small), up, down)
    grad_big, grad_small = begin_with((grad_big, grad_small), up)
    tokens_sent, tokens_kept, sums = tokens_gradient(
        core_index, (grad_big, grad_small), (wide_big, wide_small), cell, grad_hidden, norms, sums
    )
    tokens_got = swap_cores(tokens_sent)
    norm_sums = AllSum(sums + swap_cores(sums))
    w_down_share = down.result()
    activated, tokens_sent, w_down_share = tie(activated, tokens_sent, w_down_share)
    activated = finish_with(activated, up, whole)
    activated = begin_with(activated, up, whole)
    activated = begin_with(activated, norm_sums)
    mixed_kept = mixed_half(core_index, activated, w_down_turned, hidden, False)
    activated, mixed_kept = tie(activated, mixed_kept)
    activated = finish_with(activated, whole, norm_sums)
    activated = begin_with(activated, whole, norm_sums)
    mixed_sent = mixed_half(core_index, activated, w_down_turned, hidden, True)
    mixed_got = swap_cores(mixed_sent)
    mixed_kept, mixed_sent = tie(mixed_kept, mixed_sent)
    mixed_kept = finish_with(mixed_kept, whole, norm_sums, up)
    mixed_kept = begin_with(mixed_kept, whole)
    mixed_kept = begin_with(mixed_kept, norm_sums)
    up_share = up.result()
    up_share, w_out_share = up_share[:, :up_window], up_share[:, up_window:]
    tokens_grad = take_over(core_index, tokens_kept, tokens_got)
    mixed_kept, tokens_grad, up_share, w_out_share = tie(mixed_kept, tokens_grad, up_share, w_out_share)
    mixed_kept = finish_with(mixed_kept, norm_sums)
    mixed_kept = begin_with(mixed_kept, norm_sums)
    mixed = take_over(core_index, mixed_kept, mixed_got)
    mixed = finish_with(mixed, whole, norm_sums)
    qkv_share = whole.result()
    big_share, small_share = qkv_share[:, :big_window], qkv_share[:, big_window:]
    sums = norm_sums.result()

    shift = big_width + half - big_starts[1]
    w_qkv_share = pick(
        jnp.concatenate(
            [
                big_share[:rows, :big_width],
                small_share[:rows, : small * HD],
                big_share[:rows, big_width : big_width + half],
            ],
            axis=1,
        ),
        jnp.concatenate(
            [
                big_share[:rows, shift : 2 * big_width - big_starts[1]],
                small_share[:rows, : small * HD],
                big_share[:rows, 2 * big_width - big_starts[1] :],
                small_share[:rows, small_width : small_width + small * HD],
            ],
            axis=1,
        ),
    )

    def own_columns(share, starts, all_columns):
        second = all_columns // 2 - starts[1]
        return pick(share[:, : all_columns // 2], share[:, second : second + all_columns // 2])

    return (
        mixed.transpose(2, 0, 1),
        tokens_grad.transpose(2, 0, 1),
        sums[0],
        sums[1],
        w_qkv_share,
        own_columns(w_out_share[:rows], out_starts, D),
        sums[2],
        sums[3],
        own_columns(up_share[:rows], up_starts, up_all),
        own_columns(w_down_share, starts, D),
    )


def per_device(mesh, tokens, *rest):
    chips = mesh.shape["cells"]
    if mesh.shape["blk"] == 2 and tokens.shape[1] == 2 and chips & (chips - 1) == 0 and chips >= 16:
        return cell_split(tokens, *rest)
    return position_split(tokens, *rest)


def solution(mesh):
    placed = (
        P("blk", "cells", None),
        P("cells"),
        P(),
        P(),
        P(),
        P(),
        P(),
        P(),
        P(),
        P(),
        P("blk", "cells", None),
    )
    return jax.shard_map(
        functools.partial(per_device, mesh),
        mesh=mesh,
        in_specs=placed,
        out_specs=(
            P("blk", "cells", None),
            P("blk", "cells", None),
            P(),
            P(),
            P("cells", "blk"),
            P("cells", "blk"),
            P(),
            P(),
            P("cells", "blk"),
            P("cells", "blk"),
        ),
        check_vma=False,
    )
```

```python
import functools
import math

import jax
import jax.numpy as jnp
from jax import lax
from jax.experimental import pallas as pl
from jax.experimental.pallas import tpu as pltpu
from jax.sharding import PartitionSpec as P

D = 1120
HEADS = 20
HD = 56


EPSILON = 1e-05
MASKED = -1e30
LOG2E = 1.4426950408889634
LANES = 128
WIDTH = 1152
WINDOW = 256
SHARE = 1
SMALL = 0.1
TILE = 256
BF16 = jnp.bfloat16
F32 = jnp.float32
NN = (((1,), (0,)), ((), ()))
NT = (((1,), (1,)), ((), ()))
TN = (((0,), (0,)), ((), ()))


def norm_forward(values_in, gain_vec, bias_vec):
    centred = values_in - jnp.mean(values_in, axis=-1, keepdims=True)
    inverse = lax.rsqrt(jnp.mean(centred * centred, axis=-1, keepdims=True) + EPSILON)
    normed = centred * inverse
    return (normed, inverse, normed * gain_vec + bias_vec)


def norm_backward(grad_in, normed, inverse, gain_vec):
    scaled = grad_in * gain_vec
    grad_out = inverse * (
        scaled
        - jnp.mean(scaled, axis=-1, keepdims=True)
        - normed * jnp.mean(scaled * normed, axis=-1, keepdims=True)
    )
    return (grad_out, jnp.sum(grad_in * normed, axis=(0, 1)), jnp.sum(grad_in, axis=(0, 1)))


def key_scores(query_heads, key_piece, query_pos, key_start, lengths):
    key_count = key_piece.shape[0]
    key_heads = key_piece.reshape(key_count, key_piece.shape[1], HEADS, HD)
    scores = jnp.einsum(
        "qchd,kchd->chqk", query_heads, key_heads, preferred_element_type=jnp.float32
    ) * HD ** (-0.5)
    key_pos = key_start + jnp.arange(key_count, dtype=jnp.int32)
    allowed = (key_pos[None, None, :] <= query_pos[None, :, None]) & (
        key_pos[None, None, :] < lengths[:, None, None]
    )
    allowed = allowed[:, None, :, :]
    return (jnp.where(allowed, scores, MASKED), allowed)


def key_sweep(step_fn, initial, pieces, row_count, block_turns):

    def one_turn(turn_index, state_in):
        row_start = turn_index * row_count
        taken = tuple(
            (lax.dynamic_slice_in_dim(full_array, row_start, row_count, 0) for full_array in pieces)
        )
        return step_fn(state_in, taken, row_start)

    return lax.fori_loop(0, block_turns, one_turn, initial)


def position_split(
    tokens, lengths, attn_gain, attn_bias, w_qkv, w_out, mlp_gain, mlp_bias, w_up, w_down, cotangent
):
    row_count = tokens.shape[0]
    cell_count = tokens.shape[1]
    block_turns = lax.axis_size("blk")
    score_scale = HD ** (-0.5)
    query_pos = lax.axis_index("blk") * row_count + jnp.arange(row_count, dtype=jnp.int32)
    inputs = tokens.astype(jnp.float32)
    normed_one, inverse_one, pre_one = norm_forward(inputs, attn_gain, attn_bias)
    normed_low = pre_one.astype(jnp.bfloat16)
    qkv_vals = jnp.einsum(
        "rcd,de->rce", normed_low, w_qkv, preferred_element_type=jnp.float32
    ).astype(jnp.bfloat16)
    key_vals = qkv_vals[..., D : 2 * D]
    value_vals = qkv_vals[..., 2 * D :]
    query_heads = qkv_vals[..., :D].reshape(row_count, cell_count, HEADS, HD)
    start_max = jnp.full((cell_count, HEADS, row_count), MASKED, jnp.float32)
    start_sum = jnp.zeros((cell_count, HEADS, row_count), jnp.float32)
    start_out = jnp.zeros((row_count, cell_count, HEADS, HD), jnp.float32)
    scores, allowed = key_scores(
        query_heads,
        (lax.all_gather(key_vals, "blk", axis=0, tiled=True),)[0],
        query_pos,
        jnp.int32(0),
        lengths,
    )
    new_max = jnp.maximum(start_max, jnp.max(scores, axis=-1))
    weights = jnp.where(allowed, jnp.exp(scores - new_max[..., None]), 0.0)
    run_sum = jnp.sum(weights, axis=-1)
    log_total = new_max + jnp.log(run_sum)

    def probabilities(key_piece, key_start):
        scores, allowed = key_scores(query_heads, key_piece, query_pos, key_start, lengths)
        return jnp.where(allowed, jnp.exp(scores - log_total[..., None]), 0.0)

    pieces = (
        lax.all_gather(key_vals, "blk", axis=0, tiled=True),
        lax.all_gather(value_vals, "blk", axis=0, tiled=True),
    )
    prob_vals = probabilities(pieces[0], jnp.int32(0)).astype(jnp.bfloat16)
    value_heads = pieces[1].reshape(pieces[1].shape[0], cell_count, HEADS, HD)
    out_acc = jnp.einsum(
        "chqk,kchd->qchd", prob_vals, value_heads, preferred_element_type=jnp.float32
    )
    attended = out_acc.reshape(row_count, cell_count, D).astype(jnp.bfloat16)
    hidden = inputs + jnp.einsum("rcd,de->rce", attended, w_out, preferred_element_type=jnp.float32)
    normed_two, inverse_two, pre_two = norm_forward(hidden, mlp_gain, mlp_bias)
    normed_mlp = pre_two.astype(jnp.bfloat16)
    upward = jnp.einsum("rcd,df->rcf", normed_mlp, w_up, preferred_element_type=jnp.float32)
    activated_full, gelu_back = jax.vjp(
        lambda value_in: jax.nn.gelu(value_in, approximate=True), upward
    )
    activated = activated_full.astype(jnp.bfloat16)
    mixed = (
        hidden + jnp.einsum("rcf,fd->rcd", activated, w_down, preferred_element_type=jnp.float32)
    ).astype(jnp.bfloat16)
    valid_rows = (query_pos[:, None] < lengths[None, :]).astype(jnp.float32)
    grad_out = cotangent.astype(jnp.float32) * valid_rows[..., None]
    grad_low = grad_out.astype(jnp.bfloat16)
    w_down_grad = jnp.einsum("rcf,rcd->fd", activated, grad_low, preferred_element_type=jnp.float32)
    grad_act = jnp.einsum("rcd,fd->rcf", grad_low, w_down, preferred_element_type=jnp.float32)
    grad_upward = gelu_back(grad_act)[0].astype(jnp.bfloat16)
    w_up_grad = jnp.einsum(
        "rcd,rcf->df", normed_mlp, grad_upward, preferred_element_type=jnp.float32
    )
    grad_normed_two = jnp.einsum(
        "rcf,df->rcd", grad_upward, w_up, preferred_element_type=jnp.float32
    )
    grad_hidden_ln, mlp_gain_grad, mlp_bias_grad = norm_backward(
        grad_normed_two, normed_two, inverse_two, mlp_gain
    )
    grad_hidden = grad_out + grad_hidden_ln
    grad_branch = grad_hidden.astype(jnp.bfloat16)
    w_out_grad = jnp.einsum(
        "rce,rcd->ed", attended, grad_branch, preferred_element_type=jnp.float32
    )
    grad_attended = jnp.einsum(
        "rcd,ed->rce", grad_branch, w_out, preferred_element_type=jnp.float32
    ).astype(jnp.bfloat16)
    grad_heads = grad_attended.reshape(row_count, cell_count, HEADS, HD)
    whole_keys, whole_values = (
        lax.all_gather(key_vals, "blk", axis=0, tiled=True),
        lax.all_gather(value_vals, "blk", axis=0, tiled=True),
    )

    def attention_grads(key_piece, value_piece, key_start):
        prob_full = probabilities(key_piece, key_start)
        value_heads = value_piece.reshape(value_piece.shape[0], cell_count, HEADS, HD)
        dprobs = jnp.einsum(
            "qchd,kchd->chqk", grad_heads, value_heads, preferred_element_type=jnp.float32
        )
        return (prob_full, dprobs)

    def delta_step(state_in, pieces, key_start):
        prob_full, dprobs = attention_grads(pieces[0], pieces[1], key_start)
        return state_in + jnp.sum(prob_full * dprobs, axis=-1)

    row_delta = key_sweep(delta_step, start_sum, (whole_keys, whole_values), row_count, block_turns)

    def query_step(state_in, pieces, key_start):
        prob_full, dprobs = attention_grads(pieces[0], pieces[1], key_start)
        dscore = (prob_full * (dprobs - row_delta[..., None])).astype(jnp.bfloat16)
        key_heads = pieces[0].reshape(pieces[0].shape[0], cell_count, HEADS, HD)
        return state_in + jnp.einsum(
            "chqk,kchd->qchd", dscore, key_heads, preferred_element_type=jnp.float32
        )

    query_acc = key_sweep(query_step, start_out, (whole_keys, whole_values), row_count, block_turns)
    grad_queries = (query_acc * score_scale).reshape(row_count, cell_count, D).astype(jnp.bfloat16)
    key_piece = whole_keys
    value_piece = whole_values
    prob_full, dprobs = attention_grads(key_piece, value_piece, jnp.int32(0))
    dscore = (prob_full * (dprobs - row_delta[..., None])).astype(jnp.bfloat16)
    grad_keys = (
        jnp.einsum("chqk,qchd->kchd", dscore, query_heads, preferred_element_type=jnp.float32)
        * score_scale
    )
    grad_values = jnp.einsum(
        "chqk,qchd->kchd",
        prob_full.astype(jnp.bfloat16),
        grad_heads,
        preferred_element_type=jnp.float32,
    )
    kv_summed = lax.psum_scatter(
        jnp.concatenate(
            [
                grad_keys.reshape(row_count * lax.axis_size("blk"), cell_count, D),
                grad_values.reshape(row_count * lax.axis_size("blk"), cell_count, D),
            ],
            axis=-1,
        ),
        "blk",
        scatter_dimension=0,
        tiled=True,
    )
    grad_qkv = jnp.concatenate([grad_queries, kv_summed.astype(jnp.bfloat16)], axis=-1)
    w_qkv_grad = jnp.einsum("rcd,rce->de", normed_low, grad_qkv, preferred_element_type=jnp.float32)
    grad_normed_one = jnp.einsum("rce,de->rcd", grad_qkv, w_qkv, preferred_element_type=jnp.float32)
    grad_inputs_ln, attn_gain_grad, attn_bias_grad = norm_backward(
        grad_normed_one, normed_one, inverse_one, attn_gain
    )
    tokens_grad = (grad_hidden + grad_inputs_ln).astype(jnp.bfloat16)
    norm_sums = lax.psum(
        (attn_gain_grad, attn_bias_grad, mlp_gain_grad, mlp_bias_grad), ("blk", "cells")
    )
    shares = (
        lax.psum_scatter(
            w_qkv_grad.astype(jnp.bfloat16), "cells", scatter_dimension=0, tiled=True
        ).astype(jnp.float32),
        lax.psum_scatter(
            w_out_grad.astype(jnp.bfloat16), "cells", scatter_dimension=0, tiled=True
        ).astype(jnp.float32),
        lax.psum_scatter(
            w_up_grad.astype(jnp.bfloat16), "cells", scatter_dimension=0, tiled=True
        ).astype(jnp.float32),
        lax.psum_scatter(
            w_down_grad.astype(jnp.bfloat16), "cells", scatter_dimension=0, tiled=True
        ).astype(jnp.float32),
    )
    summed = (
        lax.psum_scatter(
            shares[0].astype(jnp.bfloat16), "blk", scatter_dimension=1, tiled=True
        ).astype(jnp.float32),
        lax.psum_scatter(
            shares[1].astype(jnp.bfloat16), "blk", scatter_dimension=1, tiled=True
        ).astype(jnp.float32),
        lax.psum_scatter(
            shares[2].astype(jnp.bfloat16), "blk", scatter_dimension=1, tiled=True
        ).astype(jnp.float32),
        lax.psum_scatter(
            shares[3].astype(jnp.bfloat16), "blk", scatter_dimension=1, tiled=True
        ).astype(jnp.float32),
    )
    return (
        mixed,
        tokens_grad,
        norm_sums[0],
        norm_sums[1],
        summed[0],
        summed[1],
        norm_sums[2],
        norm_sums[3],
        summed[2],
        summed[3],
    )


def cost(product):
    return pl.CostEstimate(flops=int(product * SHARE), bytes_accessed=1, transcendentals=0)


def dot(left, right, dims=NN):
    return lax.dot_general(left, right, dims, preferred_element_type=F32)


def head_lanes(head, width):
    start = jnp.minimum(head * HD // LANES, (width - WINDOW) // LANES) * LANES
    start = pl.multiple_of(start, LANES)
    lane = lax.broadcasted_iota(jnp.int32, (1, WINDOW), 1)
    offset = lane + (start - head * HD)
    own = (offset >= 0) & (offset < HD)
    spare = lane == jnp.where(start == head * HD, WINDOW - 1, 0)
    return start, own, spare


def key_bias(len_ref, seq):
    rows = lax.broadcasted_iota(jnp.int32, (seq, 1), 0)
    return jnp.where(rows < len_ref[0], 0.0, MASKED).astype(BF16)


def masked_query(q_ref, win, own, spare):
    return jnp.where(own, q_ref[:, win], jnp.where(spare, 1.0, 0.0).astype(BF16))


def causal_tile():
    key_row = lax.broadcasted_iota(jnp.int32, (TILE, TILE), 0)
    query_lane = lax.broadcasted_iota(jnp.int32, (TILE, TILE), 1)
    return key_row <= query_lane


def staggered(jobs, begin, middle, end):
    started = begin(jobs[0])
    waiting = None
    for index, job in enumerate(jobs):
        current = started
        if index + 1 < len(jobs):
            started = begin(jobs[index + 1])
        result = middle(job, *current)
        if waiting is not None:
            end(*waiting)
        waiting = (job, *result)
    end(*waiting)


def attention_forward_kernel(per, len_ref, q_ref, k_ref, v_ref, o_ref, lse_ref):
    step = pl.program_id(0)
    seq, width = q_ref.shape

    @pl.when(step == 0)
    def _():
        o_ref[...] = jnp.zeros_like(o_ref)

    bias = key_bias(len_ref, seq)
    keep = causal_tile()
    jobs = []
    for slot in range(per):
        start, own, spare = head_lanes(step * per + slot, width)
        win = pl.ds(start, WINDOW)
        k_win = jnp.where(spare, bias, k_ref[:, win])
        q_win = masked_query(q_ref, win, own, spare)
        v_turned = jnp.transpose(v_ref[:, win])
        for turn in range(seq // TILE):
            jobs.append((slot, turn * TILE, win, own, k_win, q_win, v_turned))

    def begin(job):
        _, low, _, _, k_win, q_win, _ = job
        return (dot(k_win[: low + TILE], q_win[low : low + TILE], NT),)

    def middle(job, scores):
        slot, low = job[:2]
        edge = jnp.where(keep, scores[low:], MASKED)
        scores = edge if low == 0 else jnp.concatenate([scores[:low], edge], axis=0)
        peak = jnp.max(scores, axis=0, keepdims=True)
        weights = jnp.exp2(scores - peak)
        total = jnp.sum(weights, axis=0, keepdims=True)
        lse_ref[slot, :, low : low + TILE] = jnp.broadcast_to(peak + jnp.log2(total), (8, TILE))
        return weights.astype(BF16), total

    def end(job, weights, total):
        _, low, win, own, _, _, v_turned = job
        out = dot(v_turned[:, : low + TILE], weights) * (1.0 / total)
        rows = slice(low, low + TILE)
        o_ref[rows, win] = jnp.where(own, jnp.transpose(out).astype(BF16), o_ref[rows, win])

    staggered(jobs, begin, middle, end)


def attention_backward_kernel(
    per, len_ref, q_ref, k_ref, v_ref, o_ref, do_ref, lse_ref, grad_ref, delta_ref, acc_ref
):
    step = pl.program_id(0)
    seq, width = q_ref.shape

    @pl.when(step == 0)
    def _():
        grad_ref[...] = jnp.zeros_like(grad_ref)
        lane = lax.broadcasted_iota(jnp.int32, (delta_ref.shape[0], width), 1)
        first = lax.broadcasted_iota(jnp.int32, (delta_ref.shape[0], width), 0) * HD
        pick = jnp.where((lane >= first) & (lane < first + HD), 1.0, 0.0).astype(BF16)
        for turn in range(seq // TILE):
            rows = slice(turn * TILE, (turn + 1) * TILE)
            product = o_ref[rows].astype(F32) * do_ref[rows].astype(F32)
            upper = product.astype(BF16)
            lower = (product - upper.astype(F32)).astype(BF16)
            delta_ref[:, rows] = dot(pick, upper, NT) + dot(pick, lower, NT)

    bias = key_bias(len_ref, seq)
    keep = causal_tile()
    turns = seq // TILE
    jobs = []
    for slot in range(per):
        head = step * per + slot
        start, own, spare = head_lanes(head, width)
        win = pl.ds(start, WINDOW)
        k_win = jnp.where(spare, bias, k_ref[:, win])
        q_win = masked_query(q_ref, win, own, spare)
        do_win = jnp.where(own, do_ref[:, win], jnp.zeros((), BF16))
        v_win = v_ref[:, win]
        lse = lse_ref[slot, 0:1, :]
        delta = delta_ref[pl.ds(head, 1), :]
        for turn in range(turns):
            jobs.append((slot, turn, start, own, k_win, q_win, do_win, v_win, lse, delta))

    def begin(job):
        _, turn, _, _, k_win, q_win, do_win, v_win, _, _ = job
        low = turn * TILE
        rows = slice(low, low + TILE)
        return dot(k_win[rows], q_win[low:], NT), dot(v_win[rows], do_win[low:], NT)

    def middle(job, scores, dprobs):
        turn, lse, delta = job[1], job[8], job[9]
        low = turn * TILE
        probs = jnp.exp2(scores - lse[:, low:])
        edge = jnp.where(keep, probs[:, :TILE], 0.0)
        if turn + 1 < turns:
            edge = jnp.concatenate([edge, probs[:, TILE:]], axis=1)
        dscores = (edge * (dprobs - delta[:, low:])).astype(BF16)
        return edge.astype(BF16), dscores

    def end(job, probs, dscores):
        slot, turn, start, own, k_win, q_win, do_win = job[:7]
        low = turn * TILE
        rows = slice(low, low + TILE)

        def put(place, where, value):
            lanes = pl.ds(start + place * width, WINDOW)
            grad_ref[where, lanes] = jnp.where(own, value.astype(BF16), grad_ref[where, lanes])

        put(2, rows, dot(probs, do_win[low:]))
        put(1, rows, dot(dscores, q_win[low:]) * (1.0 / LOG2E))
        part = dot(dscores, k_win[rows], TN)
        if turn == 0:
            acc_ref[slot] = part
        else:
            acc_ref[slot, low:, :] += part
        if turn + 1 == turns:
            put(0, slice(0, seq), acc_ref[slot] * HD ** (-0.5))

    staggered(jobs, begin, middle, end)


def resident(shape, place=0):
    return pl.BlockSpec(shape, lambda step, *_: (0, place), pipeline_mode=pl.Buffered(1))


def attention_forward(qkv, length, heads, per=2):
    seq, width = qkv.shape[0], qkv.shape[1] // 3
    return pl.pallas_call(
        functools.partial(attention_forward_kernel, per),
        grid_spec=pltpu.PrefetchScalarGridSpec(
            num_scalar_prefetch=1,
            grid=(heads // per,),
            in_specs=[resident((seq, width), place) for place in range(3)],
            out_specs=[
                resident((seq, width)),
                pl.BlockSpec((per, 8, seq), lambda step, *_: (step, 0, 0)),
            ],
        ),
        out_shape=[
            jax.ShapeDtypeStruct((seq, width), BF16),
            jax.ShapeDtypeStruct((heads, 8, seq), F32),
        ],
        compiler_params=pltpu.CompilerParams(vmem_limit_bytes=20 << 20),
        cost_estimate=cost(4 * heads * seq * seq * WINDOW),
        name="attention_forward",
    )(length, qkv, qkv, qkv)


def attention_backward(qkv, attended, grad_attended, lse, length, per=2):
    seq, width = qkv.shape[0], qkv.shape[1] // 3
    heads = lse.shape[0]
    return pl.pallas_call(
        functools.partial(attention_backward_kernel, per),
        grid_spec=pltpu.PrefetchScalarGridSpec(
            num_scalar_prefetch=1,
            grid=(heads // per,),
            in_specs=[resident((seq, width), place) for place in (0, 1, 2, 0, 0)]
            + [pl.BlockSpec((per, 8, seq), lambda step, *_: (step, 0, 0))],
            out_specs=resident((seq, 3 * width)),
            scratch_shapes=[
                pltpu.VMEM((-(-heads // 16) * 16, seq), F32),
                pltpu.VMEM((per, seq, WINDOW), F32),
            ],
        ),
        out_shape=jax.ShapeDtypeStruct((seq, 3 * width), BF16),
        compiler_params=pltpu.CompilerParams(vmem_limit_bytes=30 << 20),
        cost_estimate=cost(7 * heads * seq * seq * WINDOW * (heads > 8) + 1),
        name="attention_backward",
    )(length, qkv, qkv, qkv, attended, grad_attended, lse)


def once(shape):
    return pl.BlockSpec(shape, lambda step, *_: (0, 0), pipeline_mode=pl.Buffered(1))


def in_vmem():
    return pl.BlockSpec(memory_space=pltpu.VMEM)


def lane_tiles(rows, tile):
    return pl.BlockSpec((rows, tile), lambda step, *_: (0, step))


def row_tiles(tile, columns):
    return pl.BlockSpec((tile, columns), lambda step, *_: (step, 0))


def spread_store(rows_ref, scratch_ref, value, chips, lanes):
    depth = value.shape[0]
    rows = depth // chips
    padded = rows_ref.shape[0] // chips
    scratch_ref[:depth] = value
    for pair in range(chips // 2):
        first = 2 * pair * rows
        both = jnp.concatenate(
            [
                scratch_ref[first : first + padded],
                scratch_ref[first + rows : first + rows + padded],
            ],
            axis=0,
        )
        rows_ref[2 * pair * padded : 2 * (pair + 1) * padded, lanes] = both.astype(BF16)


def norm_down(value, gain, bias):
    centred = value - jnp.mean(value, axis=0, keepdims=True)
    inverse = lax.rsqrt(jnp.mean(centred * centred, axis=0, keepdims=True) + EPSILON)
    return centred * inverse * gain + bias


def half_of(core_ref, mine_ref, other_ref, lanes):
    return jnp.where(pl.program_id(0) == core_ref[0], mine_ref[0, :, lanes], other_ref[:, lanes])


def valid_lanes(len_ref, half, lanes):
    lane = lax.broadcasted_iota(jnp.int32, (1, TILE), 1) + pl.program_id(0) * half + lanes.start
    return lane < len_ref[0]


def sub_tiles(half):
    return [slice(first, first + TILE) for first in range(0, half, TILE)]


def half_specs(depth, half):
    return [
        pl.BlockSpec((1, depth, half), lambda step, core, *_: (core[0], 0, 0), pipeline_mode=pl.Buffered(1)),
        once((depth, half)),
    ]


def widen_kernel(spans, w_ref, *wide_refs):
    rows, depth = w_ref.shape[0], w_ref.shape[1] // 3
    for wide_ref, (first, size) in zip(wide_refs, spans):
        width = wide_ref.shape[1] // 3
        for part in range(3):
            begin = part * depth + first
            piece = w_ref[:, begin : begin + size]
            if size < width:
                piece = jnp.concatenate([piece, jnp.zeros((rows, width - size), BF16)], axis=1)
            wide_ref[:, part * width : (part + 1) * width] = piece


def widen(w, spans, widths, steps=5):
    depth, columns = w.shape
    tile = depth // steps
    return pl.pallas_call(
        functools.partial(widen_kernel, spans),
        grid=(steps,),
        in_specs=[row_tiles(tile, columns)],
        out_specs=[row_tiles(tile, width) for width in widths],
        out_shape=[jax.ShapeDtypeStruct((depth, width), BF16) for width in widths],
        compiler_params=pltpu.CompilerParams(vmem_limit_bytes=16 << 20),
        cost_estimate=cost(3000000000),
        name="widen",
    )(w)


def project_kernel(
    chips, core_ref, mine_ref, other_ref, norm_ref, first_w_ref, second_w_ref, first_ref, second_ref, rows_ref, scratch_ref
):
    half = other_ref.shape[1]

    @pl.when(pl.program_id(0) == 0)
    def _():
        scratch_ref[...] = jnp.zeros_like(scratch_ref)

    columns = jnp.transpose(norm_ref[...])

    def begin(lanes):
        value = half_of(core_ref, mine_ref, other_ref, lanes).astype(F32)
        normed = norm_down(value, columns[:, 0:1], columns[:, 1:2])
        spread_store(rows_ref, scratch_ref.at[lanes.start // TILE], normed, chips, lanes)
        return (jnp.transpose(normed.astype(BF16)),)

    def middle(lanes, left):
        for out_ref, w_ref in ((first_ref, first_w_ref), (second_ref, second_w_ref)):
            width = w_ref.shape[1] // 3
            value = dot(left, w_ref[...])
            out_ref[lanes, :width] = (value[:, :width] * (LOG2E * HD ** (-0.5))).astype(BF16)
            out_ref[lanes, width:] = value[:, width:].astype(BF16)
        return ()

    staggered(sub_tiles(half), begin, middle, lambda lanes: None)


def project(core, turned, other, norms, wides, chips, rows_pad):
    _, depth, half = turned.shape
    widths = [wide.shape[1] for wide in wides]
    return pl.pallas_call(
        functools.partial(project_kernel, chips),
        grid_spec=pltpu.PrefetchScalarGridSpec(
            num_scalar_prefetch=1,
            grid=(2,),
            in_specs=half_specs(depth, half) + [once(norms.shape)] + [once(wide.shape) for wide in wides],
            out_specs=[row_tiles(half, width) for width in widths] + [lane_tiles(chips * rows_pad, half)],
            scratch_shapes=[pltpu.VMEM((half // TILE, depth + 8, TILE), F32)],
        ),
        out_shape=[jax.ShapeDtypeStruct((2 * half, width), BF16) for width in widths]
        + [jax.ShapeDtypeStruct((chips * rows_pad, 2 * half), BF16)],
        compiler_params=pltpu.CompilerParams(vmem_limit_bytes=22 << 20),
        cost_estimate=cost(2 * 2 * half * depth * sum(widths)),
        name="project",
    )(core, turned, other, norms, *wides)


def hand_over_kernel(core_ref, first_ref, second_ref, first_out, second_out):
    first_out[...] = first_ref[0]
    second_out[...] = second_ref[0]


def hand_over(core, first, second):
    _, depth, half = first.shape
    tile = half // 2
    taken = pl.BlockSpec((1, depth, tile), lambda step, core: (1 - core[0], 0, step))
    return pl.pallas_call(
        hand_over_kernel,
        grid_spec=pltpu.PrefetchScalarGridSpec(
            num_scalar_prefetch=1,
            grid=(2,),
            in_specs=[taken, taken],
            out_specs=[lane_tiles(depth, tile)] * 2,
        ),
        out_shape=[jax.ShapeDtypeStruct((depth, half), BF16)] * 2,
        name="hand_over",
    )(core, first, second)


def take_over_kernel(core_ref, got_ref, whole_ref, out_ref):
    out_ref[0] = got_ref[...]


def take_over(core, whole, got):
    depth, half = got.shape
    tile = half // 2
    return pl.pallas_call(
        take_over_kernel,
        grid_spec=pltpu.PrefetchScalarGridSpec(
            num_scalar_prefetch=1,
            grid=(2,),
            in_specs=[lane_tiles(depth, tile), pl.BlockSpec(memory_space=pl.ANY)],
            out_specs=pl.BlockSpec((1, depth, tile), lambda step, core: (1 - core[0], 0, step)),
        ),
        out_shape=jax.ShapeDtypeStruct(whole.shape, BF16),
        input_output_aliases={2: 0},
        compiler_params=pltpu.CompilerParams(vmem_limit_bytes=10 << 20),
        name="take_over",
    )(core, got, whole)


def hidden_kernel(
    chips,
    core_ref,
    len_ref,
    mine_ref,
    other_ref,
    mine_grad_ref,
    other_grad_ref,
    first_ref,
    second_ref,
    w_ref,
    norm_ref,
    hidden_ref,
    normed_ref,
    grad_ref,
    rows_ref,
    o_rows_ref,
    w_turned_ref,
    scratch_ref,
):
    depth = w_ref.shape[0]
    half = other_ref.shape[1]

    @pl.when(pl.program_id(0) == 0)
    def _():
        scratch_ref[...] = jnp.zeros_like(scratch_ref)
        w_turned_ref[...] = jnp.transpose(w_ref[...])

    columns = jnp.transpose(norm_ref[...])

    def begin(lanes):
        attended = jnp.concatenate([first_ref[lanes], second_ref[lanes]], axis=1)
        value = half_of(core_ref, mine_ref, other_ref, lanes).astype(F32)
        hidden = value + dot(w_turned_ref[...], attended[:, :depth], NT)
        turned = jnp.transpose(attended).astype(F32)[:depth]
        spread_store(o_rows_ref, scratch_ref.at[2 * (lanes.start // TILE)], turned, chips, lanes)
        return (hidden,)

    def middle(lanes, hidden):
        hidden_ref[:, lanes] = hidden
        grad = half_of(core_ref, mine_grad_ref, other_grad_ref, lanes)
        grad = jnp.where(valid_lanes(len_ref, half, lanes), grad, jnp.zeros((), BF16))
        grad_ref[lanes, :depth] = jnp.transpose(grad)
        grad_ref[lanes, depth:] = jnp.zeros((TILE, grad_ref.shape[1] - depth), BF16)
        normed = norm_down(hidden, columns[:, 2:3], columns[:, 3:4])
        spread_store(rows_ref, scratch_ref.at[2 * (lanes.start // TILE) + 1], normed, chips, lanes)
        normed_ref[lanes] = jnp.transpose(normed.astype(BF16))
        return ()

    staggered(sub_tiles(half), begin, middle, lambda lanes: None)


def hidden_state(core, length, cell, grad_cell, attended, w_out, norms, chips, rows_pad):
    _, depth, half = cell[0].shape
    seq = 2 * half
    spread = jax.ShapeDtypeStruct((chips * rows_pad, seq), BF16)
    return pl.pallas_call(
        functools.partial(hidden_kernel, chips),
        grid_spec=pltpu.PrefetchScalarGridSpec(
            num_scalar_prefetch=2,
            grid=(2,),
            in_specs=half_specs(depth, half) * 2
            + [row_tiles(half, part.shape[1]) for part in attended]
            + [once(w_out.shape), once(norms.shape)],
            out_specs=[lane_tiles(depth, half), row_tiles(half, depth), row_tiles(half, WIDTH)]
            + [lane_tiles(chips * rows_pad, half)] * 2,
            scratch_shapes=[
                pltpu.VMEM((depth, depth), BF16),
                pltpu.VMEM((2 * half // TILE, depth + 8, TILE), F32),
            ],
        ),
        out_shape=[
            jax.ShapeDtypeStruct((depth, seq), F32),
            jax.ShapeDtypeStruct((seq, depth), BF16),
            jax.ShapeDtypeStruct((seq, WIDTH), BF16),
            spread,
            spread,
        ],
        compiler_params=pltpu.CompilerParams(vmem_limit_bytes=60 << 20),
        cost_estimate=cost(5 * seq * depth * depth),
        name="hidden_state",
    )(core, length, *cell, *grad_cell, *attended, w_out, norms)


GELU = (2.0 / math.pi) ** 0.5


def hidden_units_kernel(
    tile, normed_ref, grad_ref, up_ref, down_ref, activated_ref, grad_upward_ref
):
    seq, depth = normed_ref.shape

    def begin(first):
        rows = slice(first, first + tile)
        return dot(normed_ref[rows], up_ref[...]), dot(grad_ref[rows, :depth], down_ref[...])

    def middle(first, upward, grad_activated):
        rows = slice(first, first + tile)
        square = upward * upward
        gate = 0.5 * jnp.tanh(upward * (GELU + (GELU * 0.044715) * square)) + 0.5
        activated = upward * gate
        slope = gate + 2.0 * activated * (1.0 - gate) * (GELU + (3 * GELU * 0.044715) * square)
        activated_ref[:, rows] = jnp.transpose(activated.astype(BF16))
        grad_upward_ref[rows] = (grad_activated * slope).astype(BF16)
        return ()

    staggered(list(range(0, seq, tile)), begin, middle, lambda first: None)


def hidden_units(normed, grad, w_up, w_down_turned, tile=768, rows=256):
    seq, depth = normed.shape
    units = w_up.shape[1]
    return pl.pallas_call(
        functools.partial(hidden_units_kernel, rows),
        grid=(pl.cdiv(units, tile),),
        in_specs=[once(normed.shape), once(grad.shape)] + [lane_tiles(depth, tile)] * 2,
        out_specs=[row_tiles(tile, seq), lane_tiles(seq, tile)],
        out_shape=[
            jax.ShapeDtypeStruct((units, seq), BF16),
            jax.ShapeDtypeStruct((seq, units), BF16),
        ],
        compiler_params=pltpu.CompilerParams(vmem_limit_bytes=60 << 20),
        cost_estimate=cost(4 * seq * depth * units),
        name="hidden_units",
    )(normed, grad, w_up, w_down_turned)


def norm_down_back(grad_in, value, gain, gain_ref, bias_ref):
    centred = value - jnp.mean(value, axis=0, keepdims=True)
    inverse = lax.rsqrt(jnp.mean(centred * centred, axis=0, keepdims=True) + EPSILON)
    normed = centred * inverse
    product = grad_in * normed
    tiles = [slice(first, first + LANES) for first in range(0, value.shape[1], LANES)]
    gain_ref[...] += sum(product[:, lanes] for lanes in tiles)
    bias_ref[...] += sum(grad_in[:, lanes] for lanes in tiles)
    scaled = grad_in * gain
    return inverse * (
        scaled
        - jnp.mean(scaled, axis=0, keepdims=True)
        - normed * jnp.mean(product * gain, axis=0, keepdims=True)
    )


def lane_sums(rows_ref, first, *refs):
    @pl.when(pl.program_id(0) == pl.num_programs(0) - 1)
    def _():
        for place, ref in enumerate(refs):
            row = jnp.sum(jnp.transpose(ref[...]), axis=0, keepdims=True)
            rows_ref[first + place : first + place + 1, :] = row


def clear_first(*refs):
    @pl.when(pl.program_id(0) == 0)
    def _():
        for ref in refs:
            ref[...] = jnp.zeros_like(ref)


def hidden_grad_kernel(
    core_ref,
    len_ref,
    grad_up_ref,
    w_up_ref,
    hidden_ref,
    mine_grad_ref,
    other_grad_ref,
    w_ref,
    norm_ref,
    grad_hidden_ref,
    branch_ref,
    first_ref,
    second_ref,
    sums_ref,
    gain_ref,
    bias_ref,
):
    clear_first(gain_ref, bias_ref, sums_ref)
    depth, half = hidden_ref.shape
    width = first_ref.shape[1]
    columns = jnp.transpose(norm_ref[...])

    def begin(lanes):
        return (dot(w_up_ref[...], grad_up_ref[lanes], NT),)

    def middle(lanes, grad_normed):
        grad = half_of(core_ref, mine_grad_ref, other_grad_ref, lanes)
        grad = jnp.where(valid_lanes(len_ref, half, lanes), grad, jnp.zeros((), BF16)).astype(F32)
        grad = grad + norm_down_back(grad_normed, hidden_ref[:, lanes], columns[:, 2:3], gain_ref, bias_ref)
        grad_hidden_ref[:, lanes] = grad
        branch = jnp.transpose(grad.astype(BF16))
        branch_ref[lanes, :depth] = branch
        branch_ref[lanes, depth:] = jnp.zeros((TILE, branch_ref.shape[1] - depth), BF16)
        return (branch,)

    def end(lanes, branch):
        first_ref[lanes] = dot(branch, w_ref[:width], NT).astype(BF16)
        second_ref[lanes, : depth - width] = dot(branch, w_ref[width:], NT).astype(BF16)
        second_ref[lanes, depth - width :] = jnp.zeros((TILE, second_ref.shape[1] - depth + width), BF16)

    staggered(sub_tiles(half), begin, middle, end)
    lane_sums(sums_ref, 2, gain_ref, bias_ref)


def hidden_grad(core, length, grad_upward, w_up, hidden, grad_cell, w_out, norms, widths):
    depth, seq = hidden.shape
    half = seq // 2
    units = w_up.shape[1]
    return pl.pallas_call(
        hidden_grad_kernel,
        grid_spec=pltpu.PrefetchScalarGridSpec(
            num_scalar_prefetch=2,
            grid=(2,),
            in_specs=[row_tiles(half, units), once(w_up.shape), lane_tiles(depth, half)]
            + half_specs(depth, half)
            + [once(w_out.shape), once(norms.shape)],
            out_specs=[lane_tiles(depth, half), row_tiles(half, WIDTH)]
            + [row_tiles(half, width) for width in widths]
            + [once((8, depth))],
            scratch_shapes=[pltpu.VMEM((depth, LANES), F32)] * 2,
        ),
        out_shape=[
            jax.ShapeDtypeStruct((depth, seq), F32),
            jax.ShapeDtypeStruct((seq, WIDTH), BF16),
        ]
        + [jax.ShapeDtypeStruct((seq, width), BF16) for width in widths]
        + [jax.ShapeDtypeStruct((8, depth), F32)],
        compiler_params=pltpu.CompilerParams(vmem_limit_bytes=60 << 20),
        cost_estimate=cost(2 * seq * depth * (units + 2 * depth)),
        name="hidden_grad",
    )(core, length, grad_upward, w_up, hidden, *grad_cell, w_out, norms)


def half_place(step, core):
    return jnp.where(step == 0, 1 - core, core)


def tokens_grad_kernel(
    core_ref,
    first_ref,
    second_ref,
    wide_first_ref,
    wide_second_ref,
    mine_ref,
    other_ref,
    grad_hidden_ref,
    norm_ref,
    earlier_ref,
    sent_ref,
    kept_ref,
    sums_ref,
    gain_ref,
    bias_ref,
):
    clear_first(gain_ref, bias_ref)
    sums_ref[...] = earlier_ref[...]
    step = pl.program_id(0)
    columns = jnp.transpose(norm_ref[...])

    def begin(lanes):
        grad = dot(wide_first_ref[...], first_ref[lanes], NT)
        return (grad + dot(wide_second_ref[...], second_ref[lanes], NT),)

    def middle(lanes, grad_normed):
        value = jnp.where(step == 0, other_ref[:, lanes], mine_ref[0, :, lanes]).astype(F32)
        grad = norm_down_back(grad_normed, value, columns[:, 0:1], gain_ref, bias_ref)
        grad = (grad_hidden_ref[:, lanes] + grad).astype(BF16)

        @pl.when(step == 0)
        def _():
            sent_ref[:, lanes] = grad

        @pl.when(step == 1)
        def _():
            kept_ref[0, :, lanes] = grad

        return ()

    staggered(sub_tiles(other_ref.shape[1]), begin, middle, lambda lanes: None)
    lane_sums(sums_ref, 0, gain_ref, bias_ref)


def tokens_gradient(core, grads, wides, cell, grad_hidden, norms, sums):
    depth, seq = grad_hidden.shape
    half = seq // 2
    return pl.pallas_call(
        tokens_grad_kernel,
        grid_spec=pltpu.PrefetchScalarGridSpec(
            num_scalar_prefetch=1,
            grid=(2,),
            in_specs=[
                pl.BlockSpec((half, part.shape[1]), lambda step, core: (half_place(step, core[0]), 0))
                for part in grads
            ]
            + [in_vmem() for part in wides]
            + half_specs(depth, half)
            + [
                pl.BlockSpec((depth, half), lambda step, core: (0, half_place(step, core[0]))),
                once(norms.shape),
                once(sums.shape),
            ],
            out_specs=[
                once((depth, half)),
                pl.BlockSpec((1, depth, half), lambda step, core: (core[0], 0, 0), pipeline_mode=pl.Buffered(1)),
                once(sums.shape),
            ],
            scratch_shapes=[pltpu.VMEM((depth, LANES), F32)] * 2,
        ),
        out_shape=[
            jax.ShapeDtypeStruct((depth, half), BF16),
            jax.ShapeDtypeStruct((2, depth, half), BF16),
            jax.ShapeDtypeStruct(sums.shape, F32),
        ],
        compiler_params=pltpu.CompilerParams(vmem_limit_bytes=26 << 20),
        cost_estimate=cost(7 * seq * depth * WIDTH),
        name="tokens_gradient",
    )(core, *grads, *wides, *cell, grad_hidden, norms, sums)


def mixed_sent_kernel(core_ref, activated_ref, w_ref, hidden_ref, out_ref):
    out_ref[...] = (hidden_ref[...] + dot(w_ref[...], activated_ref[...])).astype(BF16)


def mixed_kept_kernel(core_ref, activated_ref, w_ref, hidden_ref, out_ref):
    out_ref[0] = (hidden_ref[...] + dot(w_ref[...], activated_ref[...])).astype(BF16)


def mixed_half(core, activated, w_down_turned, hidden, sent):
    depth, seq = hidden.shape
    units = activated.shape[0]
    tile = seq // 4

    def place(step, core):
        return 0, (2 - 2 * core[0] if sent else 2 * core[0]) + step

    if sent:
        out_spec = lane_tiles(depth, tile)
        out_shape = jax.ShapeDtypeStruct((depth, seq // 2), BF16)
    else:
        out_spec = pl.BlockSpec((1, depth, tile), lambda step, core: (core[0], 0, step))
        out_shape = jax.ShapeDtypeStruct((2, depth, seq // 2), BF16)
    return pl.pallas_call(
        mixed_sent_kernel if sent else mixed_kept_kernel,
        grid_spec=pltpu.PrefetchScalarGridSpec(
            num_scalar_prefetch=1,
            grid=(2,),
            in_specs=[
                pl.BlockSpec((units, tile), place),
                once(w_down_turned.shape),
                pl.BlockSpec((depth, tile), place),
            ],
            out_specs=out_spec,
        ),
        out_shape=out_shape,
        compiler_params=pltpu.CompilerParams(vmem_limit_bytes=60 << 20),
        cost_estimate=cost(seq * depth * units),
        name="mixed_half",
    )(core, activated, w_down_turned, hidden)


def swap_cores(value):
    return lax.ppermute(value, "blk", [(0, 1), (1, 0)])


def swap_chips(value, bit):
    count = lax.axis_size("cells")
    return lax.ppermute(value, "cells", [(place, place ^ bit) for place in range(count)])


def begin_with(chain, *scatters):
    sends = [item.send() for item in scatters]
    flat = [value for group in sends for value in group]
    chain, *flat = lax.optimization_barrier((chain, *flat))
    for item, group in zip(scatters, sends):
        item.move(flat[: len(group)])
        flat = flat[len(group) :]
    return chain


def finish_with(chain, *scatters):
    groups = [item.got for item in scatters]
    flat = [value for group in groups for value in group]
    chain, *flat = lax.optimization_barrier((chain, *flat))
    for item, group in zip(scatters, groups):
        item.arrived(flat[: len(group)])
        flat = flat[len(group) :]
    return chain


class AllSum:
    def __init__(self, value):
        self.value = value
        self.stage = 0
        self.got = None

    def send(self):
        if self.got is not None:
            self.value = self.value + self.got[0]
        return [self.value]

    def move(self, sent):
        bits = lax.axis_size("cells").bit_length() - 1
        order = list(range(2, bits)) + [0, 1]
        self.got = [swap_chips(sent[0], 1 << order[self.stage])]
        self.stage += 1
        return self.got

    def arrived(self, got):
        self.got = list(got)

    def result(self):
        return self.value + self.got[0]


def stage_order(bits, second):
    return ([1, 0] if second else [0, 1]) + list(range(2, bits))


def block_mask(index, order):
    bits = len(order)
    return sum(((index >> (bits - 1 - stage)) & 1) << bit for stage, bit in enumerate(order))


def cut_rows(rows):
    return rows - rows // 16 * 8


def columns_sent_kernel(per, scalar_ref, left_ref, *refs):
    right = refs[0][...] if per == 1 else jnp.concatenate([ref[...] for ref in refs[:per]], axis=1)
    refs[-1][...] = dot(left_ref[...], right).astype(BF16)


def columns_kept_kernel(per, chips, scalar_ref, left_ref, *refs):
    right = refs[0][...] if per == 1 else jnp.concatenate([ref[...] for ref in refs[:per]], axis=1)
    got_ref, scratch_ref = refs[per], refs[-1]
    outs = refs[-5:-1]
    bits = chips.bit_length() - 1
    scratch_ref[...] = dot(left_ref[...], right) + got_ref[...].astype(F32)
    rows = left_ref.shape[0] // chips
    cut = cut_rows(rows)
    for part, (first, size) in enumerate(((0, cut), (cut, rows - cut))):
        order = stage_order(bits, part == 1)
        for index in range(chips):
            block = jnp.bitwise_xor(scalar_ref[1], block_mask(index, order))
            row = pl.multiple_of(block * rows, 8) + first
            value = scratch_ref[pl.ds(pl.multiple_of(row, 8), size), :].astype(BF16)
            outs[2 * part + index // (chips // 2)][index % (chips // 2)] = value


def column_specs(per, depth, tiles):
    return [
        pl.BlockSpec((depth, LANES), functools.partial(column_place, per, extra))
        for extra in range(per)
    ]


def column_place(per, extra, step, scalar):
    return 0, scalar[0] + per * step + extra


def columns_sent(left, right, first, place, tiles, per, room=14):
    depth, seq = left.shape
    return pl.pallas_call(
        functools.partial(columns_sent_kernel, per),
        grid_spec=pltpu.PrefetchScalarGridSpec(
            num_scalar_prefetch=1,
            grid=(tiles // per,),
            in_specs=[in_vmem()] + column_specs(per, seq, tiles),
            out_specs=lane_tiles(depth, per * LANES),
        ),
        out_shape=jax.ShapeDtypeStruct((depth, tiles * LANES), BF16),
        compiler_params=pltpu.CompilerParams(vmem_limit_bytes=room << 20),
        cost_estimate=cost(SMALL * 2 * depth * seq * tiles * LANES),
        name="columns_sent",
    )(jnp.stack([first, place]), left, *[right] * per)


def columns_kept(left, right, got, first, place, chips, per, width, begin=0, into=None, room=22):
    depth, seq = left.shape
    tiles = got.shape[1] // LANES
    rows = depth // chips
    cut = cut_rows(rows)
    sizes = (cut, cut, rows - cut, rows - cut)
    shift = begin // per
    extra = [] if into is None else list(into)
    count = 3 + per
    return pl.pallas_call(
        functools.partial(columns_kept_kernel, per, chips),
        grid_spec=pltpu.PrefetchScalarGridSpec(
            num_scalar_prefetch=1,
            grid=(tiles // per,),
            in_specs=[in_vmem()]
            + column_specs(per, seq, tiles)
            + [lane_tiles(depth, per * LANES)]
            + [pl.BlockSpec(memory_space=pl.ANY)] * len(extra),
            out_specs=[
                pl.BlockSpec((chips // 2, size, per * LANES), lambda step, *_: (0, 0, step + shift))
                for size in sizes
            ],
            scratch_shapes=[pltpu.VMEM((depth, per * LANES), F32)],
        ),
        out_shape=[jax.ShapeDtypeStruct((chips // 2, size, width), BF16) for size in sizes],
        input_output_aliases={count + index: index for index in range(len(extra))},
        compiler_params=pltpu.CompilerParams(vmem_limit_bytes=room << 20),
        cost_estimate=cost(SMALL * 2 * depth * seq * tiles * LANES),
        name="columns_kept",
    )(jnp.stack([first, place]), left, *[right] * per, got, *extra)


def rows_sent_kernel(window, scalar_ref, left_ref, right_ref, out_ref):
    lanes = pl.ds(pl.multiple_of(scalar_ref[0] * LANES, LANES), window)
    out_ref[...] = dot(left_ref[...], right_ref[:, lanes]).astype(BF16)


def rows_sent(left, right, first, place, window, per):
    depth, seq = left.shape
    tile = depth // per
    return pl.pallas_call(
        functools.partial(rows_sent_kernel, window),
        grid_spec=pltpu.PrefetchScalarGridSpec(
            num_scalar_prefetch=1,
            grid=(per,),
            in_specs=[row_tiles(tile, seq), once(right.shape)],
            out_specs=row_tiles(tile, window),
        ),
        out_shape=jax.ShapeDtypeStruct((depth, window), BF16),
        compiler_params=pltpu.CompilerParams(vmem_limit_bytes=60 << 20),
        cost_estimate=cost(3 * depth * seq * window),
        name="rows_sent",
    )(jnp.stack([first, place]), left, right)


def rows_kept_kernel(window, chips, scalar_ref, left_ref, right_ref, got_ref, *outs):
    lanes = pl.ds(pl.multiple_of(scalar_ref[0] * LANES, LANES), window)
    value = dot(left_ref[...], right_ref[:, lanes]) + got_ref[...].astype(F32)
    bits = chips.bit_length() - 1
    blocks = chips // pl.num_programs(0) if False else value.shape[0] // (outs[0].shape[1] + outs[2].shape[1])
    rows = value.shape[0] // blocks
    cut = cut_rows(rows)
    for slot in range(blocks):
        away = jnp.bitwise_xor(scalar_ref[1], pl.program_id(0) * blocks + slot)
        for part, (first, size) in enumerate(((0, cut), (cut, rows - cut))):
            order = stage_order(bits, part == 1)
            index = sum(((away >> bit) & 1) << (bits - 1 - stage) for stage, bit in enumerate(order))
            begin = slot * rows + first
            piece = value[begin : begin + size].astype(BF16)

            @pl.when(index < chips // 2)
            def _(piece=piece, index=index, part=part):
                outs[2 * part][index] = piece

            @pl.when(index >= chips // 2)
            def _(piece=piece, index=index, part=part):
                outs[2 * part + 1][index - chips // 2] = piece


def rows_kept(left, right, got, first, place, chips, per):
    depth, seq = left.shape
    window = got.shape[1]
    tile = depth // per
    rows = depth // chips
    cut = cut_rows(rows)
    sizes = (cut, cut, rows - cut, rows - cut)
    return pl.pallas_call(
        functools.partial(rows_kept_kernel, window, chips),
        grid_spec=pltpu.PrefetchScalarGridSpec(
            num_scalar_prefetch=1,
            grid=(per,),
            in_specs=[row_tiles(tile, seq), once(right.shape), row_tiles(tile, window)],
            out_specs=[
                pl.BlockSpec(
                    (chips // 2, size, window),
                    lambda step, *_: (0, 0, 0),
                    pipeline_mode=pl.Buffered(1),
                )
                for size in sizes
            ],
        ),
        out_shape=[jax.ShapeDtypeStruct((chips // 2, size, window), BF16) for size in sizes],
        compiler_params=pltpu.CompilerParams(vmem_limit_bytes=60 << 20),
        cost_estimate=cost(3 * depth * seq * window),
        name="rows_kept",
    )(jnp.stack([first, place]), left, right, got)


def halve_kernel(count, *refs):
    ins, outs = refs[: 4 * count], refs[4 * count :]
    kept, sent = [], []
    for part in range(count):
        near, far, near_got, far_got = ins[4 * part : 4 * part + 4]
        kept.append(near[...].astype(F32) + near_got[...].astype(F32))
        sent.append(far[...].astype(F32) + far_got[...].astype(F32))
    if len(outs) < 2 * count:
        kept, sent = [jnp.concatenate(kept, axis=1)], [jnp.concatenate(sent, axis=1)]
    for part, (one, other) in enumerate(zip(kept, sent)):
        outs[2 * part][...] = one.astype(BF16)
        outs[2 * part + 1][...] = other.astype(BF16)


def halve(kept, got, join):
    half = kept[0].shape[0] // 2
    in_specs, operands = [], []
    for own, other in zip(kept, got):
        block = (1,) + own.shape[1:]
        near = pl.BlockSpec(block, lambda step: (step, 0, 0))
        far = pl.BlockSpec(block, lambda step: (step + half, 0, 0))
        in_specs += [near, far, near, far]
        operands += [own, own, other, other]
    rows = [own.shape[1] for own in kept]
    rows = [sum(rows)] if join else rows
    width = kept[0].shape[2]
    return pl.pallas_call(
        functools.partial(halve_kernel, len(kept)),
        grid=(half,),
        in_specs=in_specs,
        out_specs=[pl.BlockSpec((1, size, width), lambda step: (step, 0, 0)) for size in rows for _ in range(2)],
        out_shape=[jax.ShapeDtypeStruct((half, size, width), BF16) for size in rows for _ in range(2)],
        compiler_params=pltpu.CompilerParams(vmem_limit_bytes=12 << 20),
        cost_estimate=cost(1000 * 1000000),
        name="halve",
    )(*operands)


class Scatter:
    def __init__(self, first_kept, first_sent, second_kept, second_sent):
        self.bits = lax.axis_size("cells").bit_length() - 1
        self.kept = [first_kept, second_kept]
        self.next = [first_sent, second_sent]
        self.stage = 0
        self.got = None

    def send(self):
        if self.got is not None:
            out = halve(self.kept, self.got, self.stage == 2)
            self.kept, self.next = list(out[0::2]), list(out[1::2])
        return self.next

    def move(self, sent):
        orders = [stage_order(self.bits, part == 1) for part in range(len(sent))]
        self.got = [swap_chips(value, 1 << order[self.stage]) for value, order in zip(sent, orders)]
        self.stage += 1
        return self.got

    def arrived(self, got):
        self.got = list(got)

    def result(self):
        return self.kept[0][0].astype(F32) + self.got[0][0].astype(F32)


def cell_split(
    tokens, lengths, attn_gain, attn_bias, w_qkv, w_out, mlp_gain, mlp_bias, w_up, w_down, cotangent
):
    row_count = tokens.shape[0]
    seq = 2 * row_count
    core = lax.axis_index("blk")
    chips = lax.axis_size("cells")
    rows = D // chips
    rows_pad = -(-rows // 8) * 8

    def tie(*values):
        return lax.optimization_barrier(values)

    def pick(first, second):
        return jnp.where(core == 0, first, second)

    core_index = core.reshape(1).astype(jnp.int32)
    length = pick(lengths[0], lengths[1])
    length = length.reshape(1)
    turned, turned_cotangent = tokens.transpose(1, 2, 0), cotangent.transpose(1, 2, 0)
    sent, sent_cotangent = hand_over(core_index, turned, turned_cotangent)
    cell = (turned, swap_cores(sent))
    grad_cell = (turned_cotangent, swap_cores(sent_cotangent))
    norms = jnp.stack([attn_gain, attn_bias, mlp_gain, mlp_bias] * 2)
    w_down_turned = w_down.T

    big, small = 16, HEADS - 16
    spans = ((0, big * HD), (big * HD, small * HD))
    widths = [3 * (-(-size // LANES) * LANES) for _, size in spans]
    wide_big, wide_small = widen(w_qkv, spans, widths)
    qkv_big, qkv_small, one_rows = project(
        core_index, *cell, norms, (wide_big, wide_small), chips, rows_pad
    )
    attended_big, lse_big = attention_forward(qkv_big, length, big)
    attended_small, lse_small = attention_forward(qkv_small, length, small)
    hidden, normed_mlp, grad_low, mlp_rows, attended_rows = hidden_state(
        core_index, length, cell, grad_cell, (attended_big, attended_small), w_out, norms, chips, rows_pad
    )
    activated, grad_upward = hidden_units(normed_mlp, grad_low, w_up, w_down_turned)

    half = D // 2
    window = -(-half // LANES) * LANES
    starts = (0, WIDTH - window)
    ours, theirs = pick(*starts), pick(*starts[::-1])
    up_all = w_up.shape[1]
    up_window = -(-up_all // 2 // LANES) * LANES
    up_starts = (0, up_all - up_window)
    up_ours, up_theirs = pick(*up_starts), pick(*up_starts[::-1])
    big_width, small_width = qkv_big.shape[1] // 3, qkv_small.shape[1] // 3
    big_window = big_width + -(-half // LANES) * LANES
    big_starts = (0, 3 * big_width - big_window)
    big_ours, big_theirs = pick(*big_starts), pick(*big_starts[::-1])
    small_window = 2 * small_width
    small_starts = (0, small_width)
    small_ours, small_theirs = pick(*small_starts), pick(*small_starts[::-1])

    place = lax.axis_index("cells").astype(jnp.int32)

    def tiles(first):
        return (first // LANES).astype(jnp.int32)

    ours, theirs, up_ours, up_theirs = tiles(ours), tiles(theirs), tiles(up_ours), tiles(up_theirs)
    big_ours, big_theirs, small_ours, small_theirs = map(
        tiles, (big_ours, big_theirs, small_ours, small_theirs)
    )
    up_count, out_count = up_window // LANES, 6
    out_starts = (0, WIDTH - out_count * LANES)
    out_ours, out_theirs = tiles(pick(*out_starts)), tiles(pick(*out_starts[::-1]))
    down_steps = chips // 4

    down_sent = rows_sent(activated, grad_low, theirs, place, window, down_steps)
    down_got = swap_cores(down_sent)
    mlp_rows, down_sent = tie(mlp_rows, down_sent)
    up_sent = columns_sent(mlp_rows, grad_upward, up_theirs, place, up_count, 6, 60)
    up_got = swap_cores(up_sent)
    activated, up_sent = tie(activated, up_sent)
    down = Scatter(*rows_kept(activated, grad_low, down_got, ours, place, chips, down_steps))
    mlp_rows = begin_with(mlp_rows, down)
    up_parts = columns_kept(
        mlp_rows, grad_upward, up_got, up_ours, place, chips, 6, up_window + out_count * LANES, room=60
    )
    grad_upward, *up_parts = tie(grad_upward, *up_parts)
    grad_hidden, grad_branch, grad_attended_big, grad_attended_small, sums = hidden_grad(
        core_index, length, grad_upward, w_up, hidden, grad_cell, w_out, norms, (big_width, small_width)
    )
    out_sent = columns_sent(
        attended_rows, grad_branch, out_theirs, place, out_count, out_count, 60
    )
    out_got = swap_cores(out_sent)
    grad_attended_small, out_sent = tie(grad_attended_small, out_sent)
    grad_attended_small = finish_with(grad_attended_small, down)
    grad_attended_small = begin_with(grad_attended_small, down)
    grad_small = attention_backward(
        qkv_small, attended_small, grad_attended_small, lse_small, length
    )
    out_got, grad_small = tie(out_got, grad_small)
    up = Scatter(
        *columns_kept(
            attended_rows,
            grad_branch,
            out_got,
            out_ours,
            place,
            chips,
            out_count,
            up_window + out_count * LANES,
            up_count,
            up_parts,
            60,
        )
    )
    grad_attended_big = finish_with(grad_attended_big, down)
    grad_attended_big = begin_with(grad_attended_big, up, down)
    small_sent = columns_sent(one_rows, grad_small, small_theirs, place, small_window // LANES, 4)
    small_got = swap_cores(small_sent)
    grad_attended_big, small_sent = tie(grad_attended_big, small_sent)
    grad_big = attention_backward(qkv_big, attended_big, grad_attended_big, lse_big, length)
    grad_big = finish_with(grad_big, up, down)
    grad_big = begin_with(grad_big, up, down)
    big_sent = columns_sent(one_rows, grad_big, big_theirs, place, big_window // LANES, 6)
    big_got = swap_cores(big_sent)
    grad_small, big_sent, small_got = tie(grad_small, big_sent, small_got)
    qkv_parts = columns_kept(
        one_rows,
        grad_small,
        small_got,
        small_ours,
        place,
        chips,
        4,
        big_window + small_window,
        big_window // LANES,
    )
    big_got, *qkv_parts = tie(big_got, *qkv_parts)
    whole = Scatter(
        *columns_kept(
            one_rows,
            grad_big,
            big_got,
            big_ours,
            place,
            chips,
            6,
            big_window + small_window,
            0,
            qkv_parts,
        )
    )
    grad_big, grad_small = begin_with((grad_big, grad_small), whole)
    grad_big, grad_small = finish_with((grad_big, grad_small), up, down)
    grad_big, grad_small = begin_with((grad_big, grad_small), up)
    tokens_sent, tokens_kept, sums = tokens_gradient(
        core_index, (grad_big, grad_small), (wide_big, wide_small), cell, grad_hidden, norms, sums
    )
    tokens_got = swap_cores(tokens_sent)
    norm_sums = AllSum(sums + swap_cores(sums))
    w_down_share = down.result()
    activated, tokens_sent, w_down_share = tie(activated, tokens_sent, w_down_share)
    activated = finish_with(activated, up, whole)
    activated = begin_with(activated, up, whole)
    activated = begin_with(activated, norm_sums)
    mixed_kept = mixed_half(core_index, activated, w_down_turned, hidden, False)
    activated, mixed_kept = tie(activated, mixed_kept)
    activated = finish_with(activated, whole, norm_sums)
    activated = begin_with(activated, whole, norm_sums)
    mixed_sent = mixed_half(core_index, activated, w_down_turned, hidden, True)
    mixed_got = swap_cores(mixed_sent)
    mixed_kept, mixed_sent = tie(mixed_kept, mixed_sent)
    mixed_kept = finish_with(mixed_kept, whole, norm_sums, up)
    mixed_kept = begin_with(mixed_kept, whole)
    mixed_kept = begin_with(mixed_kept, norm_sums)
    up_share = up.result()
    up_share, w_out_share = up_share[:, :up_window], up_share[:, up_window:]
    tokens_grad = take_over(core_index, tokens_kept, tokens_got)
    mixed_kept, tokens_grad, up_share, w_out_share = tie(mixed_kept, tokens_grad, up_share, w_out_share)
    mixed_kept = finish_with(mixed_kept, norm_sums)
    mixed_kept = begin_with(mixed_kept, norm_sums)
    mixed = take_over(core_index, mixed_kept, mixed_got)
    mixed = finish_with(mixed, whole, norm_sums)
    qkv_share = whole.result()
    big_share, small_share = qkv_share[:, :big_window], qkv_share[:, big_window:]
    sums = norm_sums.result()

    shift = big_width + half - big_starts[1]
    w_qkv_share = pick(
        jnp.concatenate(
            [
                big_share[:rows, :big_width],
                small_share[:rows, : small * HD],
                big_share[:rows, big_width : big_width + half],
            ],
            axis=1,
        ),
        jnp.concatenate(
            [
                big_share[:rows, shift : 2 * big_width - big_starts[1]],
                small_share[:rows, : small * HD],
                big_share[:rows, 2 * big_width - big_starts[1] :],
                small_share[:rows, small_width : small_width + small * HD],
            ],
            axis=1,
        ),
    )

    def own_columns(share, starts, all_columns):
        second = all_columns // 2 - starts[1]
        return pick(share[:, : all_columns // 2], share[:, second : second + all_columns // 2])

    return (
        mixed.transpose(2, 0, 1),
        tokens_grad.transpose(2, 0, 1),
        sums[0],
        sums[1],
        w_qkv_share,
        own_columns(w_out_share[:rows], out_starts, D),
        sums[2],
        sums[3],
        own_columns(up_share[:rows], up_starts, up_all),
        own_columns(w_down_share, starts, D),
    )


def per_device(mesh, tokens, *rest):
    chips = mesh.shape["cells"]
    if mesh.shape["blk"] == 2 and tokens.shape[1] == 2 and chips & (chips - 1) == 0 and chips >= 16:
        return cell_split(tokens, *rest)
    return position_split(tokens, *rest)


def solution(mesh):
    placed = (
        P("blk", "cells", None),
        P("cells"),
        P(),
        P(),
        P(),
        P(),
        P(),
        P(),
        P(),
        P(),
        P("blk", "cells", None),
    )
    return jax.shard_map(
        functools.partial(per_device, mesh),
        mesh=mesh,
        in_specs=placed,
        out_specs=(
            P("blk", "cells", None),
            P("blk", "cells", None),
            P(),
            P(),
            P("cells", "blk"),
            P("cells", "blk"),
            P(),
            P(),
            P("cells", "blk"),
            P("cells", "blk"),
        ),
        check_vma=False,
    )
```
